32 devices in a mesh: seq: 8 (over z, x), head: 4 (over y, core).
Axes of the slice: x: 2, y: 2, z: 4, core: 2. Of those that a mesh axis runs over, the one named last changes fastest.
Arguments:
- queries: bfloat16 [4096, 4096], P('seq', 'head'), may hold values from -6 to 6
- key_input: bfloat16 [4096, 4096], P('seq', 'head'), may hold values from -6 to 6
- value_input: bfloat16 [4096, 4096], P('seq', 'head'), may hold values from -40 to 40
- gate_input: bfloat16 [4096, 4096], P('seq', 'head'), may hold values from -8 to 8
- kv_state: float32 [32, 128, 128], P('head'), may hold values from -512 to 512
- norm_gain: float32 [4096], replicated, may hold values from 0.25 to 1.75
- out_weight: bfloat16 [4096, 4096], P('head', 'seq'), may hold values from -0.09375 to 0.09375
Outputs:
- output: bfloat16 [4096, 4096], P(('seq', 'head'))
The draws below stay inside these ranges and needn't reach their ends.
All inputs are finite; a program needn't handle non-finite values.
Results may differ from the reference program's by a relative error of at most 0.02.
Values may be sent and summed in bfloat16 or wider, within the bound.
No kernel may reach another device: no remote copies, remote signals or barrier semaphores. Data moves between devices by JAX's collectives and lax.ppermute only.
A program may use at most 128 MiB of HBM per device.

```python
import jax
import jax.numpy as jnp
from jax import lax

H = 32
DH = 128
HD = 4096
D = 4096
BLOCK = 512
TOK_DEV = 512
TOKENS = 4096
N_HEAD = 4


def draw_value_input(key, part):
    key_base, key_cols, key_rows = jax.random.split(jax.random.fold_in(key, 7), 3)
    base = jnp.clip(jax.random.normal(key_base, (TOKENS, HD), jnp.float32), -4.0, 4.0)
    col_scale = jnp.exp(jax.random.uniform(key_cols, (1, HD), jnp.float32) * jnp.log(10.0))
    row_scale = jnp.exp(jax.random.uniform(key_rows, (TOKENS, 1), jnp.float32) * jnp.log(10.0))
    values = base * col_scale * row_scale / 10.0
    return values.astype(jnp.bfloat16)


def block_levels(own_key, extent, cuts, least, largest):
    def one(position, shards_of):
        draws = jax.random.uniform(jax.random.fold_in(jax.random.fold_in(own_key, 6), position), (shards_of,), jnp.float32, least / len(cuts), largest / len(cuts))
        return jnp.repeat(jnp.exp(draws), extent[position] // shards_of).reshape((-1,) + (1,) * (len(extent) - position - 1))

    factor_of = one(*cuts[0])
    for cut in cuts[1:]:
        factor_of = factor_of * one(*cut)
    return factor_of


def normal_values(key, shape, width, limit, cuts=(), held_as=jnp.bfloat16):
    loudness = block_levels(key, shape, cuts, -0.22, 0.18) if cuts else 1.0
    drawn = jax.random.normal(key, shape, jnp.float32) * width * loudness
    return jnp.minimum(jnp.maximum(drawn, -limit), limit).astype(held_as)


def setup_inputs(seed: int = 0) -> dict:
    seeds = jax.random.split(jax.random.key(seed), 8)
    return {
        "queries": normal_values(seeds[0], (TOKENS, HD), 1.0, 6.0, ((0, 8), (1, 4))),
        "key_input": normal_values(seeds[1], (TOKENS, HD), 1.0, 6.0, ((0, 8), (1, 4))),
        "value_input": draw_value_input(jax.random.fold_in(seeds[7], 71), 0),
        "gate_input": normal_values(seeds[3], (TOKENS, HD), 1.5, 8.0, ((0, 8), (1, 4))),
        "kv_state": normal_values(seeds[4], (H, DH, DH), (4 * TOK_DEV ** 0.5), 512.0, ((0, 4),), jnp.float32),
        "norm_gain": jnp.clip(1.0 + 0.15 * jax.random.normal(seeds[5], (HD,), jnp.float32), 0.25, 1.75),
        "out_weight": normal_values(seeds[6], (HD, D), HD ** -0.5, 0.09375, ((0, 4), (1, 8))),
    }


epsilon = 1e-05

def reference(queries, key_input, value_input, gate_input, kv_state, norm_gain, out_weight):
    num_blocks = TOKENS // BLOCK
    q_blocks = queries.reshape(num_blocks, BLOCK, H, DH)
    k_blocks = key_input.reshape(num_blocks, BLOCK, H, DH)
    v_blocks = value_input.reshape(num_blocks, BLOCK, H, DH)
    causal = jnp.arange(BLOCK)[:, None] >= jnp.arange(BLOCK)[None, :]
    highest = lax.Precision.HIGHEST

    def advance(state, blocks):
        q_rows, k_rows, v_rows = blocks
        q_float = q_rows.astype(jnp.float32)
        k_float = k_rows.astype(jnp.float32)
        v_float = v_rows.astype(jnp.float32)
        carried_part = jnp.einsum('thd,hde->the', q_float, state, precision=highest)
        scores = jnp.einsum('thd,shd->hts', q_float, k_float, precision=highest)
        scores = jnp.where(causal[None], scores, 0.0).astype(jnp.bfloat16)
        scores = lax.optimization_barrier(scores).astype(jnp.float32)
        inner_part = jnp.einsum('hts,she->the', scores, v_float, precision=highest)
        new_state = state + jnp.einsum('thd,the->hde', k_float, v_float, precision=highest)
        return (new_state, (carried_part + inner_part).astype(jnp.bfloat16))
    final_state, attn = lax.scan(advance, kv_state.astype(jnp.float32), (q_blocks, k_blocks, v_blocks))
    attn_float = attn.reshape(TOKENS, HD).astype(jnp.float32)
    mean_square = lax.optimization_barrier(jnp.mean(attn_float * attn_float, axis=1, keepdims=True))
    hidden = attn_float * lax.rsqrt(mean_square + epsilon) * norm_gain[None, :]
    hidden = (hidden * jax.nn.sigmoid(gate_input.astype(jnp.float32))).astype(jnp.bfloat16)
    group = HD // N_HEAD
    hidden_blocks = hidden.reshape(num_blocks, BLOCK, HD)

    def project(rows):
        summed = jnp.zeros((BLOCK, D), jnp.float32)
        for index in range(N_HEAD):
            partial_rows = jnp.dot(rows[:, index * group:(index + 1) * group], out_weight[index * group:(index + 1) * group], preferred_element_type=jnp.float32).astype(jnp.bfloat16)
            summed = summed + lax.optimization_barrier(partial_rows).astype(jnp.float32)
        return summed.astype(jnp.bfloat16)
    return lax.map(project, hidden_blocks).reshape(TOKENS, D)
```

```python
import jax
import jax.numpy as jnp
from jax import lax
from jax.sharding import PartitionSpec as P

DH = 128
BLOCK = 512
LINE = 4


epsilon = 1e-05


def line_pairs(n_seq, hops):
    inner = n_seq // LINE
    return [(a * inner + i, b * inner + i) for a, b in hops for i in range(inner)]


def turn_pairs(n_seq, turn):
    inner = n_seq // LINE
    return [(a * inner + i, a * inner + (i + turn) % inner) for a in range(LINE) for i in range(inner)]


def flip_pairs(n_head, bit):
    return [(h, h ^ bit) for h in range(n_head)]


SWAP_OUTER = [(0, 1), (1, 0), (2, 3), (3, 2)]
SWAP_MIDDLE = [(1, 2), (2, 1)]
TO_ENDS = [(1, 0), (2, 3)]


def state_prefix(own_total, n_seq, place):
    inner = n_seq // LINE
    i = place % inner
    shape = own_total.shape
    parts = own_total.reshape(inner, -1, DH)
    parts_low = parts.astype(jnp.bfloat16)
    from_member = [lax.dynamic_index_in_dim(parts, i, 0, False)]
    members = [i]
    for turn in range(1, inner):
        sent = lax.dynamic_index_in_dim(parts_low, (i + turn) % inner, 0, False)
        got = lax.ppermute(sent, "seq", turn_pairs(n_seq, turn))
        from_member.append(got.astype(jnp.float32))
        members.append((i - turn) % inner)
    group_sum = sum(from_member)
    from_left = lax.ppermute(group_sum.astype(jnp.bfloat16), "seq", line_pairs(n_seq, [(0, 1), (2, 3)]))
    from_left = from_left.astype(jnp.float32)
    pair_sum = (group_sum + from_left).astype(jnp.bfloat16)
    near = lax.ppermute(pair_sum, "seq", line_pairs(n_seq, [(1, 2)]))
    far = lax.ppermute(pair_sum, "seq", line_pairs(n_seq, [(1, 3)]))
    entering = from_left + near.astype(jnp.float32) + far.astype(jnp.float32)

    def before(member):
        total = entering
        for value, owner in zip(from_member, members):
            total = total + jnp.where(owner < member, value, 0.0)
        return total

    result = jnp.zeros_like(parts)
    result = lax.dynamic_update_index_in_dim(result, before(i), i, 0)
    for turn in range(1, inner):
        sent = before((i + turn) % inner).astype(jnp.bfloat16)
        got = lax.ppermute(sent, "seq", turn_pairs(n_seq, turn))
        result = lax.dynamic_update_index_in_dim(result, got.astype(jnp.float32), (i - turn) % inner, 0)
    return result.reshape(shape)


def shards(queries, key_input, value_input, gate_input, kv_state, norm_gain, out_weight):
    n_seq, n_head = lax.axis_size("seq"), lax.axis_size("head")
    inner = n_seq // LINE
    place, h = lax.axis_index("seq"), lax.axis_index("head")
    z, i = place // inner, place % inner
    tok_rows, local_width = queries.shape
    local_heads = local_width // DH
    num_blocks = tok_rows // BLOCK
    total_width = local_width * n_head

    def along(value, hops):
        return lax.ppermute(value, "seq", line_pairs(n_seq, hops))

    w_pair = along(out_weight, SWAP_OUTER)
    w_mid1 = along(out_weight, SWAP_MIDDLE)
    w_mid2 = along(w_pair, SWAP_MIDDLE)
    w_end1 = along(w_mid1, TO_ENDS)
    w_end2 = along(w_mid2, TO_ENDS)
    is_end = (z == 0) | (z == LINE - 1)
    weights = [
        out_weight,
        w_pair,
        jnp.where(is_end, w_end1, w_mid1),
        jnp.where(is_end, w_end2, w_mid2),
    ]
    low = z < 2
    weight_from = [z, z ^ 1, jnp.where(low, 2, 1), jnp.where(low, 3, 0)]

    block_shape = (num_blocks, BLOCK, local_heads, DH)
    q_blocks = queries.reshape(block_shape)
    k_blocks = key_input.reshape(block_shape)
    v_blocks = value_input.reshape(block_shape)
    block_states = jnp.einsum(
        "nthd,nthe->nhde", k_blocks, v_blocks, preferred_element_type=jnp.float32
    )
    own_total = jnp.sum(block_states, axis=0)
    start_state = kv_state + state_prefix(own_total, n_seq, place)
    running = jnp.cumsum(block_states, axis=0) - block_states
    before = start_state[None] + running
    carried_part = jnp.einsum(
        "nthd,nhde->nthe", q_blocks.astype(jnp.float32), before, precision=lax.Precision.HIGHEST
    )
    scores = jnp.einsum("nthd,nshd->nhts", q_blocks, k_blocks, preferred_element_type=jnp.float32)
    causal = jnp.arange(BLOCK)[:, None] >= jnp.arange(BLOCK)[None, :]
    masked = jnp.where(causal[None, None], scores, 0.0).astype(jnp.bfloat16)
    inner_part = jnp.einsum(
        "nhts,nshe->nthe", masked, v_blocks, preferred_element_type=jnp.float32
    )
    attn = (carried_part + inner_part).astype(jnp.bfloat16).reshape(tok_rows, local_width)
    attn_float = attn.astype(jnp.float32)

    squares = jnp.sum(attn_float * attn_float, axis=1)
    bit = 1
    while bit < n_head:
        squares = squares + lax.ppermute(squares, "head", flip_pairs(n_head, bit))
        bit *= 2
    out_rows = tok_rows // n_head
    own_squares = lax.dynamic_slice_in_dim(squares, h * out_rows, out_rows, 0)
    scale = lax.rsqrt(own_squares / total_width + epsilon)

    gain_part = lax.dynamic_slice_in_dim(norm_gain, h * local_width, local_width, 0)
    gated = attn_float * gain_part[None, :] * jax.nn.sigmoid(gate_input.astype(jnp.float32))
    gated = gated.astype(jnp.bfloat16).reshape(n_head, out_rows, local_width)
    bits = n_head.bit_length() - 1
    order = [int(format(j, "b").zfill(bits)[::-1], 2) for j in range(n_head)] if bits else [0]
    hidden = jnp.concatenate(
        [lax.dynamic_index_in_dim(gated, j ^ h, 0, False) for j in order], axis=0
    )
    hiddens = [hidden]
    for turn in range(1, inner):
        hiddens.append(lax.ppermute(hidden, "seq", turn_pairs(n_seq, turn)))

    def project(rows, weight):
        return jnp.dot(rows, weight, preferred_element_type=jnp.float32)

    width = out_weight.shape[1]
    output = jnp.zeros((out_rows, width * n_seq), jnp.bfloat16)
    for weight, owner in zip(weights, weight_from):
        half = tok_rows // 2
        sent = jnp.stack([project(rows[half:], weight).astype(jnp.bfloat16) for rows in hiddens])
        kept = jnp.stack([project(rows[:half], weight) for rows in hiddens])
        bit = 1
        while bit < n_head:
            kept = kept + lax.ppermute(sent, "head", flip_pairs(n_head, bit)).astype(jnp.float32)
            half = half // 2
            bit *= 2
            if bit < n_head:
                sent = kept[:, half:].astype(jnp.bfloat16)
                kept = kept[:, :half]
        pieces = [(kept[0], i)]
        for turn in range(1, inner):
            got = lax.ppermute(kept[turn].astype(jnp.bfloat16), "seq", turn_pairs(n_seq, -turn))
            pieces.append((got, (i + turn) % inner))
        for piece, member in pieces:
            scaled = (piece.astype(jnp.float32) * scale[:, None]).astype(jnp.bfloat16)
            output = lax.dynamic_update_slice_in_dim(
                output, scaled, (owner * inner + member) * width, 1
            )
    return output


def solution(mesh):
    in_specs = (
        P("seq", "head"),
        P("seq", "head"),
        P("seq", "head"),
        P("seq", "head"),
        P("head", None, None),
        P(),
        P("head", "seq"),
    )
    out_specs = P(("seq", "head"), None)
    return jax.shard_map(shards, mesh=mesh, in_specs=in_specs, out_specs=out_specs, check_vma=False)
```

```python
import functools

import jax
import jax.numpy as jnp
from jax import lax
from jax.experimental import pallas as pl
from jax.experimental.pallas import tpu as pltpu
from jax.sharding import PartitionSpec as P

DH = 128
BLOCK = 512
LINE = 4


epsilon = 1e-05


def line_pairs(n_seq, hops):
    inner = n_seq // LINE
    return [(a * inner + i, b * inner + i) for a, b in hops for i in range(inner)]


def turn_pairs(n_seq, turn):
    inner = n_seq // LINE
    return [(a * inner + i, a * inner + (i + turn) % inner) for a in range(LINE) for i in range(inner)]


def flip_pairs(n_head, bit):
    return [(h, h ^ bit) for h in range(n_head)]


SWAP_OUTER = [(0, 1), (1, 0), (2, 3), (3, 2)]
SWAP_MIDDLE = [(1, 2), (2, 1)]
TO_ENDS = [(1, 0), (2, 3)]


def states_kernel(k_ref, v_ref, wide_ref, low_ref):
    for index in range(wide_ref.shape[0]):
        columns = pl.ds(index * DH, DH)
        state = lax.dot_general(
            k_ref[:, columns],
            v_ref[:, columns],
            (((0,), (0,)), ((), ())),
            preferred_element_type=jnp.float32,
        )
        wide_ref[index] = state
        low_ref[index] = state.astype(jnp.bfloat16)


def block_states(key_input, value_input, heads_at_once=2):
    rows, width = key_input.shape
    heads = width // DH
    steps = heads // heads_at_once
    shape = (heads, DH, DH)
    rows_spec = pl.BlockSpec((rows, heads_at_once * DH), lambda step: (0, step))
    state_spec = pl.BlockSpec((heads_at_once, DH, DH), lambda step: (step, 0, 0))
    return pl.pallas_call(
        states_kernel,
        grid=(steps,),
        in_specs=[rows_spec, rows_spec],
        out_specs=[state_spec, state_spec],
        out_shape=[
            jax.ShapeDtypeStruct(shape, jnp.float32),
            jax.ShapeDtypeStruct(shape, jnp.bfloat16),
        ],
        cost_estimate=pl.CostEstimate(
            flops=2 * rows * width * DH, bytes_accessed=4 * rows * width, transcendentals=0
        ),
    )(key_input, value_input)


def causal_kernel(q_ref, k_ref, v_ref, *rest):
    out_ref = rest[-1]
    rows = q_ref.shape[0]
    half = rows // 2
    for index in range(q_ref.shape[1] // DH):
        columns = pl.ds(index * DH, DH)
        for first in (0, half):
            seen = first + half
            scores = lax.dot_general(
                q_ref[pl.ds(first, half), columns],
                k_ref[pl.ds(0, seen), columns],
                (((1,), (1,)), ((), ())),
                preferred_element_type=jnp.float32,
            )
            at_row = first + lax.broadcasted_iota(jnp.int32, scores.shape, 0)
            at_column = lax.broadcasted_iota(jnp.int32, scores.shape, 1)
            scores = jnp.where(at_row >= at_column, scores, 0.0).astype(jnp.bfloat16)
            out_ref[pl.ds(first, half), columns] = jnp.dot(
                scores, v_ref[pl.ds(0, seen), columns], preferred_element_type=jnp.float32
            )


def causal_part(queries, key_input, value_input, calls=2):
    rows, width = queries.shape
    heads = width // DH // calls
    result = None
    for call in range(calls):
        spec = pl.BlockSpec((rows, DH), lambda head, base=call * heads: (0, base + head))
        operands = [queries, key_input, value_input]
        specs = [spec] * 3
        aliases = {}
        if result is not None:
            operands.append(result)
            specs.append(pl.BlockSpec(memory_space=pl.ANY))
            aliases = {3: 0}
        result = pl.pallas_call(
            causal_kernel,
            grid=(heads,),
            in_specs=specs,
            out_specs=spec,
            out_shape=jax.ShapeDtypeStruct((rows, width), jnp.float32),
            input_output_aliases=aliases,
            cost_estimate=pl.CostEstimate(
                flops=4 * rows * rows * heads * DH,
                bytes_accessed=10 * rows * heads * DH,
                transcendentals=0,
            ),
        )(*operands)
    return result


def hidden_kernel(order, h_ref, q_ref, inner_ref, state_ref, gate_ref, gain_ref, *rest):
    hidden_ref, squares_ref = rest[-2:]
    state = state_ref[0]
    high = state.astype(jnp.bfloat16)
    low = (state - high.astype(jnp.float32)).astype(jnp.bfloat16)
    size = q_ref.shape[0] // len(order)
    gain = gain_ref[0]

    @pl.when(pl.program_id(0) == 0)
    def _():
        squares_ref[...] = jnp.zeros_like(squares_ref)

    for position, block in enumerate(order):
        start = pl.multiple_of((h_ref[0] ^ block) * size, size)
        rows = pl.ds(start, size)
        q_rows = q_ref[rows, :]
        carried = jnp.dot(q_rows, high, preferred_element_type=jnp.float32) + jnp.dot(
            q_rows, low, preferred_element_type=jnp.float32
        )
        attn = (carried + inner_ref[rows, :]).astype(jnp.bfloat16).astype(jnp.float32)
        gate = jax.nn.sigmoid(gate_ref[rows, :].astype(jnp.float32))
        placed = pl.ds(position * size, size)
        hidden_ref[placed, :] = (attn * gain * gate).astype(jnp.bfloat16)
        squares_ref[placed, :] += attn * attn


def gated_hidden(queries, inner, state, gate_input, norm_gain, h, order, after):
    rows, width = queries.shape
    heads = width // DH
    columns = pl.BlockSpec((rows, DH), lambda head, h_ref: (0, head))
    return pl.pallas_call(
        functools.partial(hidden_kernel, order),
        grid_spec=pltpu.PrefetchScalarGridSpec(
            num_scalar_prefetch=1,
            grid=(heads,),
            in_specs=[
                columns,
                columns,
                pl.BlockSpec((1, DH, DH), lambda head, h_ref: (head, 0, 0)),
                columns,
                pl.BlockSpec((1, 1, DH), lambda head, h_ref: (h_ref[0] * heads + head, 0, 0)),
            ]
            + [pl.BlockSpec(memory_space=pl.ANY)] * len(after),
            out_specs=[columns, pl.BlockSpec((rows, DH), lambda head, h_ref: (0, 0))],
        ),
        out_shape=[
            jax.ShapeDtypeStruct((rows, width), jnp.bfloat16),
            jax.ShapeDtypeStruct((rows, DH), jnp.float32),
        ],
        cost_estimate=pl.CostEstimate(
            flops=4 * rows * width * DH, bytes_accessed=12 * rows * width, transcendentals=rows * width
        ),
    )(
        jnp.reshape(h, (1,)).astype(jnp.int32),
        queries,
        inner,
        state,
        gate_input,
        norm_gain.reshape(-1, 1, DH),
        *after,
    )


def state_prefix(wide, low, n_seq, place):
    inner = n_seq // LINE
    i = place % inner
    shape = wide.shape
    parts = wide.reshape(inner, -1, DH)
    parts_low = low.reshape(inner, -1, DH)
    from_member = [lax.dynamic_index_in_dim(parts, i, 0, False)]
    members = [i]
    for turn in range(1, inner):
        sent = lax.dynamic_index_in_dim(parts_low, (i + turn) % inner, 0, False)
        got = lax.ppermute(sent, "seq", turn_pairs(n_seq, turn))
        from_member.append(got.astype(jnp.float32))
        members.append((i - turn) % inner)
    group_sum = sum(from_member)
    from_left = lax.ppermute(group_sum.astype(jnp.bfloat16), "seq", line_pairs(n_seq, [(0, 1), (2, 3)]))
    from_left = from_left.astype(jnp.float32)
    pair_sum = (group_sum + from_left).astype(jnp.bfloat16)
    near = lax.ppermute(pair_sum, "seq", line_pairs(n_seq, [(1, 2)]))
    far = lax.ppermute(pair_sum, "seq", line_pairs(n_seq, [(1, 3)]))
    entering = from_left + near.astype(jnp.float32) + far.astype(jnp.float32)

    def before(member):
        total = entering
        for value, owner in zip(from_member, members):
            total = total + jnp.where(owner < member, value, 0.0)
        return total

    index = jnp.arange(inner)[:, None, None]
    result = jnp.where(index == i, before(i)[None], 0.0)
    for turn in range(1, inner):
        sent = before((i + turn) % inner).astype(jnp.bfloat16)
        got = lax.ppermute(sent, "seq", turn_pairs(n_seq, turn)).astype(jnp.float32)
        result = jnp.where(index == (i - turn) % inner, got[None], result)
    return result.reshape(shape)


def shards(queries, key_input, value_input, gate_input, kv_state, norm_gain, out_weight):
    n_seq, n_head = lax.axis_size("seq"), lax.axis_size("head")
    inner = n_seq // LINE
    place, h = lax.axis_index("seq"), lax.axis_index("head")
    z, i = place // inner, place % inner
    tok_rows, local_width = queries.shape
    assert tok_rows == BLOCK
    total_width = local_width * n_head

    def along(value, hops):
        return lax.ppermute(value, "seq", line_pairs(n_seq, hops))

    w_pair = along(out_weight, SWAP_OUTER)
    w_mid1 = along(out_weight, SWAP_MIDDLE)
    w_mid2 = along(w_pair, SWAP_MIDDLE)
    w_end1 = along(w_mid1, TO_ENDS)
    w_end2 = along(w_mid2, TO_ENDS)
    is_end = (z == 0) | (z == LINE - 1)
    weights = [
        out_weight,
        w_pair,
        jnp.where(is_end, w_end1, w_mid1),
        jnp.where(is_end, w_end2, w_mid2),
    ]
    low = z < 2
    weight_from = [z, z ^ 1, jnp.where(low, 2, 1), jnp.where(low, 3, 0)]

    wide, low_states = block_states(key_input, value_input)
    state = kv_state + state_prefix(wide, low_states, n_seq, place)
    inner_part = causal_part(queries, key_input, value_input)
    bits = n_head.bit_length() - 1
    order = [int(format(j, "b").zfill(bits)[::-1], 2) for j in range(n_head)] if bits else [0]
    hidden, squares = gated_hidden(
        queries, inner_part, state, gate_input, norm_gain, h, order, [w_pair, w_mid1]
    )

    squares = jnp.sum(squares, axis=1)
    out_rows = tok_rows // n_head
    half, bit = tok_rows // 2, 1
    while bit < n_head:
        squares = squares[:half] + lax.ppermute(squares[half:], "head", flip_pairs(n_head, bit))
        half //= 2
        bit *= 2
    scale = lax.rsqrt(squares / total_width + epsilon)

    hiddens = [hidden]
    for turn in range(1, inner):
        hiddens.append(lax.ppermute(hidden, "seq", turn_pairs(n_seq, turn)))

    def project(rows, weight):
        return jnp.dot(rows, weight, preferred_element_type=jnp.float32)

    width = out_weight.shape[1]
    output = jnp.zeros((out_rows, width * n_seq), jnp.bfloat16)
    for weight, owner in zip(weights, weight_from):
        half = tok_rows // 2
        sent = jnp.stack([project(rows[half:], weight).astype(jnp.bfloat16) for rows in hiddens])
        kept = jnp.stack([project(rows[:half], weight) for rows in hiddens])
        bit = 1
        while bit < n_head:
            kept = kept + lax.ppermute(sent, "head", flip_pairs(n_head, bit)).astype(jnp.float32)
            half = half // 2
            bit *= 2
            if bit < n_head:
                sent = kept[:, half:].astype(jnp.bfloat16)
                kept = kept[:, :half]
        pieces = [(kept[0], i)]
        for turn in range(1, inner):
            got = lax.ppermute(kept[turn].astype(jnp.bfloat16), "seq", turn_pairs(n_seq, -turn))
            pieces.append((got, (i + turn) % inner))
        for piece, member in pieces:
            scaled = (piece.astype(jnp.float32) * scale[:, None]).astype(jnp.bfloat16)
            output = lax.dynamic_update_slice_in_dim(
                output, scaled, (owner * inner + member) * width, 1
            )
    return output


def solution(mesh):
    in_specs = (
        P("seq", "head"),
        P("seq", "head"),
        P("seq", "head"),
        P("seq", "head"),
        P("head", None, None),
        P(),
        P("head", "seq"),
    )
    out_specs = P(("seq", "head"), None)
    return jax.shard_map(shards, mesh=mesh, in_specs=in_specs, out_specs=out_specs, check_vma=False)
```

```python
import functools

import jax
import jax.numpy as jnp
from jax import lax
from jax.experimental import pallas as pl
from jax.experimental.pallas import tpu as pltpu
from jax.sharding import PartitionSpec as P

DH = 128
BLOCK = 512
LINE = 4
VMEM_BYTES = 48 * 1024 * 1024


epsilon = 1e-05


def line_pairs(n_seq, hops):
    inner = n_seq // LINE
    return [(a * inner + i, b * inner + i) for a, b in hops for i in range(inner)]


def turn_pairs(n_seq, turn):
    inner = n_seq // LINE
    return [(a * inner + i, a * inner + (i + turn) % inner) for a in range(LINE) for i in range(inner)]


def flip_pairs(n_head, bit):
    return [(h, h ^ bit) for h in range(n_head)]


SWAP_OUTER = [(0, 1), (1, 0), (2, 3), (3, 2)]
SWAP_MIDDLE = [(1, 2), (2, 1)]
TO_ENDS = [(1, 0), (2, 3)]


def hold(value, *others):
    return lax.optimization_barrier((value, *others))[0]


def scalars(*values):
    return jnp.stack([jnp.asarray(value, jnp.int32) for value in values])


def states_kernel(part_ref, k_ref, v_ref, out_ref):
    for index in range(out_ref.shape[0]):
        columns = pl.ds(index * DH, DH)
        out_ref[index] = lax.dot_general(
            k_ref[:, columns],
            v_ref[:, columns],
            (((0,), (0,)), ((), ())),
            preferred_element_type=jnp.float32,
        ).astype(out_ref.dtype)


def block_states(key_input, value_input, part, heads, dtype):
    rows = key_input.shape[0]
    at_once = 2 if heads % 2 == 0 else 1
    steps = heads // at_once
    rows_spec = pl.BlockSpec((rows, at_once * DH), lambda step, part_ref: (0, part_ref[0] * steps + step))
    return pl.pallas_call(
        states_kernel,
        grid_spec=pltpu.PrefetchScalarGridSpec(
            num_scalar_prefetch=1,
            grid=(steps,),
            in_specs=[rows_spec, rows_spec],
            out_specs=pl.BlockSpec((at_once, DH, DH), lambda step, part_ref: (step, 0, 0)),
        ),
        out_shape=jax.ShapeDtypeStruct((heads, DH, DH), dtype),
        cost_estimate=pl.CostEstimate(
            flops=2 * rows * heads * DH * DH, bytes_accessed=4 * rows * heads * DH, transcendentals=0
        ),
    )(scalars(part), key_input, value_input)


def state_prefix(key_input, value_input, n_seq, place, early):
    inner = n_seq // LINE
    i = place % inner
    heads = key_input.shape[1] // DH
    split = heads % inner == 0
    share = heads // inner if split else heads
    sends = []
    if split:
        for turn in range(1, inner):
            sends.append(block_states(key_input, value_input, (i + turn) % inner, share, jnp.bfloat16))
        own = block_states(key_input, value_input, i, share, jnp.float32)
    else:
        own = block_states(key_input, value_input, 0, share, jnp.float32)
        sends = [own.astype(jnp.bfloat16)] * (inner - 1)
    members = [(i, own)]
    for turn in range(1, inner):
        got = lax.ppermute(sends[turn - 1], "seq", turn_pairs(n_seq, turn))
        members.append(((i - turn) % inner, got.astype(jnp.float32)))
    group_sum = sum(value for _, value in members)
    first = hold(group_sum.astype(jnp.bfloat16), *early)
    from_left = lax.ppermute(first, "seq", line_pairs(n_seq, [(0, 1), (2, 3)])).astype(jnp.float32)
    second = (group_sum + from_left).astype(jnp.bfloat16)
    near = lax.ppermute(second, "seq", line_pairs(n_seq, [(1, 2)]))
    far = lax.ppermute(second, "seq", line_pairs(n_seq, [(1, 3)]))
    entering = from_left + near.astype(jnp.float32) + far.astype(jnp.float32)

    def before(member):
        total = entering
        for owner, value in members:
            total = total + jnp.where(owner < member, value, 0.0)
        return total

    terms = [before(i)]
    if split:
        for turn in range(1, inner):
            sent = before((i + turn) % inner).astype(jnp.bfloat16)
            terms.append(lax.ppermute(sent, "seq", turn_pairs(n_seq, turn)))
    return terms, near


def causal_kernel(q_ref, k_ref, v_ref, *rest):
    out_ref = rest[-1]
    rows = q_ref.shape[0]
    half = rows // 2
    top, bottom = pl.ds(0, half), pl.ds(half, half)
    keep = lax.broadcasted_iota(jnp.int32, (half, half), 0) >= lax.broadcasted_iota(
        jnp.int32, (half, half), 1
    )

    def scores(q_rows, k_rows, columns):
        return lax.dot_general(
            q_ref[q_rows, columns],
            k_ref[k_rows, columns],
            (((1,), (1,)), ((), ())),
            preferred_element_type=jnp.float32,
        )

    for index in range(q_ref.shape[1] // DH):
        columns = pl.ds(index * DH, DH)
        first = jnp.where(keep, scores(top, top, columns), 0.0).astype(jnp.bfloat16)
        below = scores(bottom, top, columns).astype(jnp.bfloat16)
        last = jnp.where(keep, scores(bottom, bottom, columns), 0.0).astype(jnp.bfloat16)
        out_ref[top, columns] = jnp.dot(first, v_ref[top, columns], preferred_element_type=jnp.float32)
        out_ref[bottom, columns] = jnp.dot(
            jnp.concatenate([below, last], axis=1),
            v_ref[:, columns],
            preferred_element_type=jnp.float32,
        )


def causal_part(queries, key_input, value_input, first_head, heads, filled=None):
    rows, width = queries.shape
    at_once = 2 if heads % 2 == 0 and first_head % 2 == 0 else 1
    base = first_head // at_once
    spec = pl.BlockSpec((rows, at_once * DH), lambda step: (0, base + step))
    operands, specs, aliases = [queries, key_input, value_input], [spec] * 3, {}
    if filled is not None:
        operands.append(filled)
        specs.append(pl.BlockSpec(memory_space=pl.ANY))
        aliases = {3: 0}
    return pl.pallas_call(
        causal_kernel,
        grid=(heads // at_once,),
        in_specs=specs,
        out_specs=spec,
        out_shape=jax.ShapeDtypeStruct((rows, width), jnp.float32),
        input_output_aliases=aliases,
        cost_estimate=pl.CostEstimate(
            flops=4 * rows * rows * heads * DH,
            bytes_accessed=10 * rows * heads * DH,
            transcendentals=0,
        ),
    )(*operands)


def hidden_kernel(order, share, group, place_ref, q_ref, inner_ref, gate_ref, gain_ref, kv_ref, *rest):
    hidden_ref, squares_ref = rest[-2:]
    terms = rest[:group]
    state = kv_ref[0]
    if group == 1:
        state = state + terms[0][0]
    else:
        part = pl.program_id(0) // share
        for turn, term in enumerate(terms):
            covers = lax.rem(place_ref[1] - turn + group, group)
            state = state + jnp.where(part == covers, term[0].astype(jnp.float32), 0.0)
    high = state.astype(jnp.bfloat16)
    low = (state - high.astype(jnp.float32)).astype(jnp.bfloat16)
    both = jnp.concatenate([high, low], axis=0)
    size = q_ref.shape[0] // len(order)
    half_gain = gain_ref[0] * 0.5
    first = pl.program_id(0) == 0
    for position, block in enumerate(order):
        start = pl.multiple_of((place_ref[0] ^ block) * size, size)
        rows = pl.ds(start, size)
        q_rows = q_ref[rows, :]
        carried = jnp.dot(
            jnp.concatenate([q_rows, q_rows], axis=1), both, preferred_element_type=jnp.float32
        )
        attn = (carried + inner_ref[rows, :]).astype(jnp.bfloat16).astype(jnp.float32)
        gate = 1.0 + jnp.tanh(gate_ref[rows, :].astype(jnp.float32) * 0.5)
        placed = pl.ds(position * size, size)
        hidden_ref[placed, :] = (attn * (half_gain * gate)).astype(jnp.bfloat16)
        square = attn * attn
        squares_ref[placed, :] = jnp.where(first, square, squares_ref[placed, :] + square)


def gated_hidden(queries, inner_part, kv_state, terms, gate_input, norm_gain, h, i, order):
    rows, width = queries.shape
    heads = width // DH
    group = len(terms)
    share = heads // group
    columns = pl.BlockSpec((rows, DH), lambda head, place_ref: (0, head))
    return pl.pallas_call(
        functools.partial(hidden_kernel, order, share, group),
        grid_spec=pltpu.PrefetchScalarGridSpec(
            num_scalar_prefetch=1,
            grid=(heads,),
            in_specs=[
                columns,
                columns,
                columns,
                pl.BlockSpec((1, 1, DH), lambda head, place_ref: (place_ref[0] * heads + head, 0, 0)),
                pl.BlockSpec((1, DH, DH), lambda head, place_ref: (head, 0, 0)),
            ]
            + [pl.BlockSpec((1, DH, DH), lambda head, place_ref: (head % share, 0, 0))] * group,
            out_specs=[columns, pl.BlockSpec((rows, DH), lambda head, place_ref: (0, 0))],
        ),
        out_shape=[
            jax.ShapeDtypeStruct((rows, width), jnp.bfloat16),
            jax.ShapeDtypeStruct((rows, DH), jnp.float32),
        ],
        cost_estimate=pl.CostEstimate(
            flops=4 * rows * width * DH, bytes_accessed=12 * rows * width, transcendentals=rows * width
        ),
    )(
        scalars(h, i),
        queries,
        inner_part,
        gate_input,
        norm_gain.reshape(-1, 1, DH),
        kv_state,
        *terms,
    )


def project_kernel(groups, choices, flag_ref, *refs):
    rows_refs = refs[:groups]
    weight_refs = refs[groups : groups + sum(choices)]
    sent_ref, kept_ref, rows_buf, weight_buf, rows_sem, weight_sem = refs[groups + sum(choices) :]

    def rows_copy(group):
        return pltpu.make_async_copy(rows_refs[group], rows_buf.at[group % 2], rows_sem.at[group % 2])

    rows_copy(0).start()
    first = 0
    waits = []
    for index, number in enumerate(choices):
        copies = [
            pltpu.make_async_copy(weight_refs[first + k], weight_buf.at[index], weight_sem.at[index])
            for k in range(number)
        ]
        if number == 1:
            copies[0].start()
        else:
            for k in range(number):
                pl.when(flag_ref[0] == k)(copies[k].start)
        waits.append(copies[0])
        first += number
    half = sent_ref.shape[1]
    width = weight_buf.shape[2]
    for group in range(groups):
        if group + 1 < groups:
            rows_copy(group + 1).start()
        rows_copy(group).wait()
        for index in range(len(choices)):
            if group == 0:
                waits[index].wait()
            columns = pl.ds(index * width, width)
            product = jnp.dot(
                rows_buf[group % 2], weight_buf[index], preferred_element_type=jnp.float32
            )
            kept_ref[group, :, columns] = product[:half]
            sent_ref[group, :, columns] = product[half:].astype(jnp.bfloat16)


def project(rows_list, weights, flag):
    groups = len(rows_list)
    flat = [choice for weight in weights for choice in weight]
    choices = tuple(len(weight) for weight in weights)
    rows, depth = rows_list[0].shape
    width = flat[0].shape[1]
    shape = (groups, rows // 2, width * len(weights))
    return pl.pallas_call(
        functools.partial(project_kernel, groups, choices),
        in_specs=[pl.BlockSpec(memory_space=pltpu.SMEM)]
        + [pl.BlockSpec(memory_space=pl.ANY)] * (groups + len(flat)),
        out_specs=[pl.BlockSpec(memory_space=pltpu.VMEM)] * 2,
        out_shape=[
            jax.ShapeDtypeStruct(shape, jnp.bfloat16),
            jax.ShapeDtypeStruct(shape, jnp.float32),
        ],
        scratch_shapes=[
            pltpu.VMEM((2, rows, depth), jnp.bfloat16),
            pltpu.VMEM((len(weights), depth, width), jnp.bfloat16),
            pltpu.SemaphoreType.DMA((2,)),
            pltpu.SemaphoreType.DMA((len(weights),)),
        ],
        compiler_params=pltpu.CompilerParams(vmem_limit_bytes=VMEM_BYTES),
        cost_estimate=pl.CostEstimate(
            flops=2 * groups * rows * depth * width * len(weights),
            bytes_accessed=2 * depth * (groups * rows + width * len(weights)),
            transcendentals=0,
        ),
    )(flag, *rows_list, *flat)


def placed_kernel(counts, cut, starts_ref, scale_ref, *refs):
    pieces = refs[: len(counts)]
    out_ref = refs[-1]
    where = 0
    for piece, count in zip(pieces, counts):
        for index in range(count):
            part = piece[:, pl.ds(index * cut, cut)].astype(jnp.float32) * scale_ref[...]
            start = pl.multiple_of(starts_ref[where], DH)
            out_ref[:, pl.ds(start, cut)] = part.astype(out_ref.dtype)
            where += 1


def added_kernel(counts, cut, starts_ref, scale_ref, *refs):
    pieces = refs[: len(counts)]
    out_ref, buf, sem = refs[-3:]
    where = 0
    copies = []
    for piece, count in zip(pieces, counts):
        for index in range(count):
            part = piece[:, pl.ds(index * cut, cut)].astype(jnp.float32) * scale_ref[...]
            buf[where] = part.astype(out_ref.dtype)
            start = pl.multiple_of(starts_ref[where], DH)
            copy = pltpu.make_async_copy(buf.at[where], out_ref.at[:, pl.ds(start, cut)], sem.at[where])
            copy.start()
            copies.append(copy)
            where += 1
    for copy in copies:
        copy.wait()


def placed(filled, pieces, scale, cut, shape):
    counts = tuple(len(starts) for _, starts in pieces)
    starts = scalars(*[start for _, own in pieces for start in own])
    operands = [starts, scale[:, None]] + [piece for piece, _ in pieces]
    in_specs = [pl.BlockSpec(memory_space=pltpu.SMEM)] + [
        pl.BlockSpec(memory_space=pltpu.VMEM)
    ] * (len(operands) - 1)
    out_shape = jax.ShapeDtypeStruct(shape, jnp.bfloat16)
    params = pltpu.CompilerParams(vmem_limit_bytes=VMEM_BYTES)
    cost = pl.CostEstimate(
        flops=shape[0] * cut * sum(counts),
        bytes_accessed=6 * shape[0] * cut * sum(counts),
        transcendentals=0,
    )
    if filled is None:
        return pl.pallas_call(
            functools.partial(placed_kernel, counts, cut),
            in_specs=in_specs,
            out_specs=pl.BlockSpec(memory_space=pltpu.VMEM),
            out_shape=out_shape,
            compiler_params=params,
            cost_estimate=cost,
        )(*operands)
    return pl.pallas_call(
        functools.partial(added_kernel, counts, cut),
        in_specs=in_specs + [pl.BlockSpec(memory_space=pl.ANY)],
        out_specs=pl.BlockSpec(memory_space=pl.ANY),
        out_shape=out_shape,
        scratch_shapes=[
            pltpu.VMEM((sum(counts), shape[0], cut), jnp.bfloat16),
            pltpu.SemaphoreType.DMA((sum(counts),)),
        ],
        input_output_aliases={len(operands): 0},
        compiler_params=params,
        cost_estimate=cost,
    )(*operands, filled)


def shards(queries, key_input, value_input, gate_input, kv_state, norm_gain, out_weight):
    n_seq, n_head = lax.axis_size("seq"), lax.axis_size("head")
    inner = n_seq // LINE
    place, h = lax.axis_index("seq"), lax.axis_index("head")
    z, i = place // inner, place % inner
    tok_rows, local_width = queries.shape
    assert tok_rows == BLOCK
    heads = local_width // DH
    total_width = local_width * n_head
    width = out_weight.shape[1]
    cuts = 2 if width % (2 * DH) == 0 else 1
    cut = width // cuts

    def along(value, hops):
        return lax.ppermute(value, "seq", line_pairs(n_seq, hops))

    w_cuts = [out_weight[:, k * cut : (k + 1) * cut] for k in range(cuts)]
    w_pair = [along(w_cuts[0], SWAP_OUTER)]
    w_mid1 = [along(w_cuts[0], SWAP_MIDDLE)]
    terms, near = state_prefix(
        key_input, value_input, n_seq, place, [w_pair[0], w_mid1[0]]
    )
    some = heads // 2
    inner_part = causal_part(queries, key_input, value_input, 0, some)

    w_mid2, w_end1, w_end2 = [], [], []
    for k in range(cuts):
        if k:
            w_next = hold(w_cuts[k], near)
            w_pair.append(along(w_next, SWAP_OUTER))
            w_mid1.append(along(w_next, SWAP_MIDDLE))
        w_mid2.append(along(hold(w_pair[k], near), SWAP_MIDDLE))
        w_end1.append(along(hold(w_mid1[k], near), TO_ENDS))
    for k in range(cuts):
        w_end2.append(along(w_mid2[k], TO_ENDS))
    inner_part = causal_part(queries, key_input, value_input, some, heads - some, inner_part)

    bits = n_head.bit_length() - 1
    order = [int(format(j, "b").zfill(bits)[::-1], 2) for j in range(n_head)] if bits else [0]
    terms[0] = hold(terms[0], *w_pair[1:], *w_mid1[1:])
    hidden, squares = gated_hidden(
        queries, inner_part, kv_state, terms, gate_input, norm_gain, h, i, order
    )
    others = [lax.ppermute(hidden, "seq", turn_pairs(n_seq, turn)) for turn in range(1, inner)]

    squares = jnp.sum(squares, axis=1)
    out_rows = tok_rows // n_head
    half, bit = tok_rows // 2, 1
    while bit < n_head:
        squares = squares[:half] + lax.ppermute(squares[half:], "head", flip_pairs(n_head, bit))
        half //= 2
        bit *= 2
    scale = lax.rsqrt(squares / total_width + epsilon)

    is_end = (z == 0) | (z == LINE - 1)
    low = z < LINE // 2
    own_block, pair_block = z, z ^ 1
    third_block = jnp.where(low, 2, 1)
    fourth_block = jnp.where(low, 3, 0)
    flag = scalars(is_end)

    def summed(flag, rows_list, members, weights, blocks):
        sent, kept = project(rows_list, weights, flag)
        flag = hold(flag, sent)
        half, bit = tok_rows // 2, 1
        while bit < n_head:
            kept = kept + lax.ppermute(sent, "head", flip_pairs(n_head, bit)).astype(jnp.float32)
            half = half // 2
            bit *= 2
            if bit < n_head:
                sent = kept[:, half:].astype(jnp.bfloat16)
                kept = kept[:, :half]
        pieces = []
        for position, turn in enumerate(members):
            piece = kept[position]
            if turn:
                piece = lax.ppermute(piece.astype(jnp.bfloat16), "seq", turn_pairs(n_seq, -turn))
            starts = [(block * inner + (i + turn) % inner) * width + k * cut for block, k in blocks]
            pieces.append((piece, starts))
        return pieces, flag

    own_turn, other_turns = [0], list(range(1, inner))
    early_weights = [(w,) for w in w_cuts] + [(w,) for w in w_pair]
    early_blocks = [(own_block, k) for k in range(cuts)] + [(pair_block, k) for k in range(cuts)]
    third = [(w_mid1[k], w_end1[k]) for k in range(cuts)]
    fourth = [(w_mid2[k], w_end2[k]) for k in range(cuts)]
    rows_list, turns = [hidden] + others, own_turn + other_turns
    pieces, flag = summed(flag, [hidden], own_turn, early_weights, early_blocks)
    if others:
        more, flag = summed(flag, others, other_turns, early_weights, early_blocks)
        pieces += more
    more, flag = summed(flag, rows_list, turns, third, [(third_block, k) for k in range(cuts)])
    pieces += more
    for k in range(cuts):
        last, flag = summed(flag, rows_list, turns, [fourth[k]], [(fourth_block, k)])
        if k + 1 < cuts:
            pieces += last
    shape = (out_rows, width * n_seq)
    if cut % DH == 0:
        return placed(placed(None, pieces, scale, cut, shape), last, scale, cut, shape)
    output = jnp.zeros(shape, jnp.bfloat16)
    for piece, starts in pieces + last:
        piece = (piece.astype(jnp.float32) * scale[:, None]).astype(jnp.bfloat16)
        for index, start in enumerate(starts):
            part = piece[:, index * cut : (index + 1) * cut]
            output = lax.dynamic_update_slice_in_dim(output, part, start, 1)
    return output


def solution(mesh):
    in_specs = (
        P("seq", "head"),
        P("seq", "head"),
        P("seq", "head"),
        P("seq", "head"),
        P("head", None, None),
        P(),
        P("head", "seq"),
    )
    out_specs = P(("seq", "head"), None)
    return jax.shard_map(shards, mesh=mesh, in_specs=in_specs, out_specs=out_specs, check_vma=False)
```

```python
import functools

import jax
import jax.numpy as jnp
from jax import lax
from jax.experimental import pallas as pl
from jax.experimental.pallas import tpu as pltpu
from jax.sharding import PartitionSpec as P

DH = 128
BLOCK = 512
LINE = 4
VMEM_BYTES = 48 * 1024 * 1024


epsilon = 1e-05


def line_pairs(n_seq, hops):
    inner = n_seq // LINE
    return [(a * inner + i, b * inner + i) for a, b in hops for i in range(inner)]


def turn_pairs(n_seq, turn):
    inner = n_seq // LINE
    return [(a * inner + i, a * inner + (i + turn) % inner) for a in range(LINE) for i in range(inner)]


def flip_pairs(n_head, bit):
    return [(h, h ^ bit) for h in range(n_head)]


SWAP_OUTER = [(0, 1), (1, 0), (2, 3), (3, 2)]
SWAP_MIDDLE = [(1, 2), (2, 1)]
TO_ENDS = [(1, 0), (2, 3)]


def hold(value, *others):
    return lax.optimization_barrier((value, *others))[0]


def scalars(*values):
    return jnp.stack([jnp.asarray(value, jnp.int32) for value in values])


def local_call(kernel, places, operands, out_shapes, scratch=()):
    return pl.pallas_call(
        kernel,
        in_specs=[pl.BlockSpec(memory_space=pltpu.SMEM)]
        + [pl.BlockSpec(memory_space=pltpu.VMEM)] * len(operands),
        out_specs=[pl.BlockSpec(memory_space=pltpu.VMEM)] * len(out_shapes),
        out_shape=out_shapes,
        scratch_shapes=list(scratch),
        compiler_params=pltpu.CompilerParams(vmem_limit_bytes=VMEM_BYTES),
        cost_estimate=pl.CostEstimate(flops=1, bytes_accessed=1, transcendentals=0),
    )(places, *operands)


def combine_kernel(count, always, masks_ref, *refs):
    values, outs = refs[:count], refs[count:]
    total = values[0][...].astype(jnp.float32)
    for value in values[1:always]:
        total = total + value[...].astype(jnp.float32)
    for position, out in enumerate(outs):
        own = total
        for k in range(always, count):
            mask = masks_ref[position * (count - always) + k - always]
            own = own + jnp.where(mask != 0, values[k][...].astype(jnp.float32), 0.0)
        out[...] = own.astype(out.dtype)


def combine(values, dtypes, sometimes=(), masks=None):
    operands = list(values) + list(sometimes)
    masks = scalars(0) if masks is None else scalars(*masks)
    return local_call(
        functools.partial(combine_kernel, len(operands), len(values)),
        masks,
        operands,
        [jax.ShapeDtypeStruct(values[0].shape, dtype) for dtype in dtypes],
    )


def states_kernel(part_ref, k_ref, v_ref, out_ref):
    heads = out_ref.shape[0]
    for index in range(heads):
        columns = pl.ds(pl.multiple_of((part_ref[0] * heads + index) * DH, DH), DH)
        out_ref[index] = lax.dot_general(
            k_ref[:, columns],
            v_ref[:, columns],
            (((0,), (0,)), ((), ())),
            preferred_element_type=jnp.float32,
        ).astype(out_ref.dtype)


def block_states(key_input, value_input, part, heads, dtype):
    return local_call(
        states_kernel,
        scalars(part),
        [key_input, value_input],
        [jax.ShapeDtypeStruct((heads, DH, DH), dtype)],
    )[0]


def state_prefix(key_input, value_input, n_seq, place, early, later):
    inner = n_seq // LINE
    i = place % inner
    heads = key_input.shape[1] // DH
    split = heads % inner == 0
    share = heads // inner if split else heads
    if split:
        sends = [
            block_states(key_input, value_input, (i + turn) % inner, share, jnp.bfloat16)
            for turn in range(1, inner)
        ]
        own = block_states(key_input, value_input, i, share, jnp.float32)
    else:
        own = block_states(key_input, value_input, 0, share, jnp.float32)
        sends = [own.astype(jnp.bfloat16)] * (inner - 1)
    values, members = [own], [i]
    for turn in range(1, inner):
        values.append(lax.ppermute(sends[turn - 1], "seq", turn_pairs(n_seq, turn)))
        members.append((i - turn) % inner)
    (first,) = combine(values, [jnp.bfloat16])
    from_left = lax.ppermute(hold(first, *early), "seq", line_pairs(n_seq, [(0, 1), (2, 3)]))
    (second,) = combine(values + [from_left], [jnp.bfloat16])
    near = lax.ppermute(second, "seq", line_pairs(n_seq, [(1, 2)]))
    far = lax.ppermute(second, "seq", line_pairs(n_seq, [(1, 3)]))
    targets = [i] + [(i + turn) % inner for turn in range(1, inner)] if split else [i]
    masks = [owner < target for target in targets for owner in members]
    dtypes = [jnp.float32] + [jnp.bfloat16] * (len(targets) - 1)
    near = hold(near, *later(from_left))
    befores = combine([from_left, near, far], dtypes, values, masks)
    terms = [befores[0]]
    for turn in range(1, len(targets)):
        terms.append(lax.ppermute(befores[turn], "seq", turn_pairs(n_seq, turn)))
    return terms, far


def causal_kernel(first_head, place_ref, q_ref, k_ref, v_ref, out_ref):
    rows = q_ref.shape[0]
    half = rows // 2
    top, bottom = pl.ds(0, half), pl.ds(half, half)
    keep = lax.broadcasted_iota(jnp.int32, (half, half), 0) >= lax.broadcasted_iota(
        jnp.int32, (half, half), 1
    )

    def scores(q_rows, k_rows, columns):
        return lax.dot_general(
            q_ref[q_rows, columns],
            k_ref[k_rows, columns],
            (((1,), (1,)), ((), ())),
            preferred_element_type=jnp.float32,
        )

    for index in range(out_ref.shape[1] // DH):
        columns = pl.ds((first_head + index) * DH, DH)
        placed = pl.ds(index * DH, DH)
        first = jnp.where(keep, scores(top, top, columns), 0.0).astype(jnp.bfloat16)
        below = scores(bottom, top, columns).astype(jnp.bfloat16)
        last = jnp.where(keep, scores(bottom, bottom, columns), 0.0).astype(jnp.bfloat16)
        out_ref[top, placed] = jnp.dot(first, v_ref[top, columns], preferred_element_type=jnp.float32)
        out_ref[bottom, placed] = jnp.dot(
            jnp.concatenate([below, last], axis=1),
            v_ref[:, columns],
            preferred_element_type=jnp.float32,
        )


def causal_part(queries, key_input, value_input, first_head, heads):
    return local_call(
        functools.partial(causal_kernel, first_head),
        scalars(0),
        [queries, key_input, value_input],
        [jax.ShapeDtypeStruct((queries.shape[0], heads * DH), jnp.float32)],
    )[0]


def hidden_kernel(order, group, calls, place_ref, q_ref, gate_ref, gain_ref, kv_ref, *refs):
    terms, inners = refs[:group], refs[group : group + calls]
    hidden_ref, squares_ref = refs[group + calls :]
    heads = kv_ref.shape[0]
    share = heads // group
    size = q_ref.shape[0] // len(order)
    states = []
    for head in range(heads):
        state = kv_ref[head]
        for turn, term in enumerate(terms):
            value = term[head % share].astype(jnp.float32)
            if group > 1:
                covers = lax.rem(place_ref[1] - turn + group, group)
                value = jnp.where(covers == head // share, value, 0.0)
            state = state + value
        high = state.astype(jnp.bfloat16)
        low = (state - high.astype(jnp.float32)).astype(jnp.bfloat16)
        states.append(jnp.concatenate([high, low], axis=0))
    for position, block in enumerate(order):
        start = pl.multiple_of((place_ref[0] ^ block) * size, size)
        rows = pl.ds(start, size)
        placed = pl.ds(position * size, size)
        squares = jnp.zeros((size, DH), jnp.float32)
        for head in range(heads):
            columns = pl.ds(head * DH, DH)
            q_rows = q_ref[rows, columns]
            carried = jnp.dot(
                jnp.concatenate([q_rows, q_rows], axis=1),
                states[head],
                preferred_element_type=jnp.float32,
            )
            per_call = inners[0].shape[1] // DH
            inner = inners[head // per_call][rows, pl.ds(head % per_call * DH, DH)]
            attn = (carried + inner).astype(jnp.bfloat16).astype(jnp.float32)
            gate = 1.0 + jnp.tanh(gate_ref[rows, columns].astype(jnp.float32) * 0.5)
            gain = gain_ref[place_ref[0] * heads + head] * 0.5
            hidden_ref[placed, columns] = (attn * (gain * gate)).astype(jnp.bfloat16)
            squares = squares + attn * attn
        squares_ref[pl.ds(position, 1), :] = jnp.sum(jnp.transpose(squares), axis=0, keepdims=True)


def gated_hidden(queries, inners, kv_state, terms, gate_input, norm_gain, h, i, order):
    rows, width = queries.shape
    return local_call(
        functools.partial(hidden_kernel, order, len(terms), len(inners)),
        scalars(h, i),
        [queries, gate_input, norm_gain.reshape(-1, 1, DH), kv_state, *terms, *inners],
        [
            jax.ShapeDtypeStruct((rows, width), jnp.bfloat16),
            jax.ShapeDtypeStruct((len(order), rows // len(order)), jnp.float32),
        ],
    )


def project_kernel(groups, choices, flag_ref, *refs):
    rows_refs = refs[:groups]
    weight_refs = refs[groups : groups + sum(choices)]
    sent_ref, kept_ref = refs[groups + sum(choices) :]
    half = sent_ref.shape[1]
    width = weight_refs[0].shape[1]

    def products(index, weight_ref):
        columns = pl.ds(index * width, width)
        for group in range(groups):
            product = jnp.dot(
                rows_refs[group][...], weight_ref[...], preferred_element_type=jnp.float32
            )
            kept_ref[group, :, columns] = product[:half]
            sent_ref[group, :, columns] = product[half:].astype(jnp.bfloat16)

    first = 0
    for index, number in enumerate(choices):
        for k in range(number):
            one = functools.partial(products, index, weight_refs[first + k])
            if number == 1:
                one()
            else:
                pl.when(flag_ref[0] == k)(one)
        first += number


def project(rows_list, weights, flag):
    flat = [choice for weight in weights for choice in weight]
    choices = tuple(len(weight) for weight in weights)
    shape = (len(rows_list), rows_list[0].shape[0] // 2, flat[0].shape[1] * len(weights))
    return local_call(
        functools.partial(project_kernel, len(rows_list), choices),
        flag,
        [*rows_list, *flat],
        [jax.ShapeDtypeStruct(shape, jnp.bfloat16), jax.ShapeDtypeStruct(shape, jnp.float32)],
    )


def fold_kernel(flag_ref, kept_ref, got_ref, *outs):
    if len(outs) == 2 and len(outs[0].shape) == 3:
        sent_ref, left_ref = outs
        half = left_ref.shape[1]
        left_ref[...] = kept_ref[:, :half] + got_ref[:, :half].astype(jnp.float32)
        sent_ref[...] = (kept_ref[:, half:] + got_ref[:, half:].astype(jnp.float32)).astype(jnp.bfloat16)
        return
    for group, out in enumerate(outs):
        out[...] = (kept_ref[group] + got_ref[group].astype(jnp.float32)).astype(out.dtype)


def fold(kept, got, more):
    groups, rows, width = kept.shape
    if more:
        shape = (groups, rows // 2, width)
        outs = [jax.ShapeDtypeStruct(shape, jnp.bfloat16), jax.ShapeDtypeStruct(shape, jnp.float32)]
    else:
        outs = [jax.ShapeDtypeStruct((rows, width), jnp.bfloat16)] * groups
    return local_call(fold_kernel, scalars(0), [kept, got], outs)


def column(row):
    return jnp.transpose(jnp.broadcast_to(row, (row.shape[1], row.shape[1])))


def scaled_parts(counts, cut, squares_ref, pieces, total_width):
    scale = lax.rsqrt(column(squares_ref[...]) / total_width + epsilon)
    for piece, count in zip(pieces, counts):
        for index in range(count):
            for first in range(index * cut, (index + 1) * cut, DH):
                yield piece[:, pl.ds(first, DH)].astype(jnp.float32) * scale


def placed_kernel(counts, cut, total_width, starts_ref, squares_ref, *refs):
    out_ref = refs[-1]
    steps = cut // DH
    for at, part in enumerate(scaled_parts(counts, cut, squares_ref, refs[:-1], total_width)):
        start = pl.multiple_of(starts_ref[at // steps] + at % steps * DH, DH)
        out_ref[:, pl.ds(start, DH)] = part.astype(out_ref.dtype)


def added_kernel(counts, cut, total_width, starts_ref, squares_ref, *refs):
    pieces = refs[: len(counts)]
    out_ref, buf, sem = refs[-3:]
    steps = cut // DH
    copies = []
    for at, part in enumerate(scaled_parts(counts, cut, squares_ref, pieces, total_width)):
        where = at // steps
        buf[where, :, pl.ds(at % steps * DH, DH)] = part.astype(out_ref.dtype)
        if at % steps == steps - 1:
            start = pl.multiple_of(starts_ref[where], DH)
            copy = pltpu.make_async_copy(buf.at[where], out_ref.at[:, pl.ds(start, cut)], sem.at[where])
            copy.start()
            copies.append(copy)
    for copy in copies:
        copy.wait()


def placed(filled, pieces, squares, cut, shape, total_width):
    counts = tuple(len(starts) for _, starts in pieces)
    starts = scalars(*[start for _, own in pieces for start in own])
    operands = [squares] + [piece for piece, _ in pieces]
    out_shape = jax.ShapeDtypeStruct(shape, jnp.bfloat16)
    if filled is None:
        kernel = functools.partial(placed_kernel, counts, cut, total_width)
        return local_call(kernel, starts, operands, [out_shape])[0]
    return pl.pallas_call(
        functools.partial(added_kernel, counts, cut, total_width),
        in_specs=[pl.BlockSpec(memory_space=pltpu.SMEM)]
        + [pl.BlockSpec(memory_space=pltpu.VMEM)] * len(operands)
        + [pl.BlockSpec(memory_space=pl.ANY)],
        out_specs=pl.BlockSpec(memory_space=pl.ANY),
        out_shape=out_shape,
        scratch_shapes=[
            pltpu.VMEM((sum(counts), shape[0], cut), jnp.bfloat16),
            pltpu.SemaphoreType.DMA((sum(counts),)),
        ],
        input_output_aliases={len(operands) + 1: 0},
        compiler_params=pltpu.CompilerParams(vmem_limit_bytes=VMEM_BYTES),
        cost_estimate=pl.CostEstimate(flops=1, bytes_accessed=1, transcendentals=0),
    )(starts, *operands, filled)


def shards(queries, key_input, value_input, gate_input, kv_state, norm_gain, out_weight):
    n_seq, n_head = lax.axis_size("seq"), lax.axis_size("head")
    inner = n_seq // LINE
    place, h = lax.axis_index("seq"), lax.axis_index("head")
    z, i = place // inner, place % inner
    tok_rows, local_width = queries.shape
    assert tok_rows == BLOCK
    heads = local_width // DH
    total_width = local_width * n_head
    width = out_weight.shape[1]
    cuts = 2 if width % (2 * DH) == 0 else 1
    cut = width // cuts

    def along(value, hops):
        return lax.ppermute(value, "seq", line_pairs(n_seq, hops))

    w_cuts = [out_weight[:, k * cut : (k + 1) * cut] for k in range(cuts)]
    w_pair = [along(w_cuts[0], SWAP_OUTER)]
    w_mid1 = [along(w_cuts[0], SWAP_MIDDLE)]

    def later(from_left):
        for cut_columns in w_cuts[1:]:
            cut_columns = hold(cut_columns, from_left)
            w_pair.append(along(cut_columns, SWAP_OUTER))
            w_mid1.append(along(cut_columns, SWAP_MIDDLE))
        return w_pair[1:] + w_mid1[1:]

    terms, far = state_prefix(
        key_input, value_input, n_seq, place, [w_pair[0], w_mid1[0]], later
    )
    some = heads // 2
    inners = [
        causal_part(queries, key_input, value_input, 0, some),
        causal_part(queries, key_input, value_input, some, heads - some),
    ]

    w_mid2 = [along(hold(w_pair[k], far), SWAP_MIDDLE) for k in range(cuts)]
    w_end1 = [along(hold(w_mid1[k], far), TO_ENDS) for k in range(cuts)]
    w_end2 = [along(w_mid2[k], TO_ENDS) for k in range(cuts)]

    bits = n_head.bit_length() - 1
    order = [int(format(j, "b").zfill(bits)[::-1], 2) for j in range(n_head)] if bits else [0]
    hidden, squares = gated_hidden(
        queries, inners, kv_state, terms, gate_input, norm_gain, h, i, order
    )
    others = [lax.ppermute(hidden, "seq", turn_pairs(n_seq, turn)) for turn in range(1, inner)]

    out_rows = tok_rows // n_head
    half, bit, square_steps = n_head // 2, 1, []
    while bit < n_head:
        square_steps.append(lax.ppermute(squares[half:], "head", flip_pairs(n_head, bit)))
        squares = squares[:half] + square_steps[-1]
        half //= 2
        bit *= 2

    is_end = (z == 0) | (z == LINE - 1)
    low = z < LINE // 2
    flag = scalars(is_end)

    def summed(flag, rows_list, members, weights, blocks):
        sent, kept = project(rows_list, weights, flag)
        bit, steps = 1, []
        while bit < n_head:
            steps.append(lax.ppermute(sent, "head", flip_pairs(n_head, bit)))
            bit *= 2
            if bit < n_head:
                sent, kept = fold(kept, steps[-1], True)
            else:
                kept = fold(kept, steps[-1], False)
        pieces = []
        for position, turn in enumerate(members):
            piece = kept[position]
            if turn:
                piece = lax.ppermute(piece, "seq", turn_pairs(n_seq, -turn))
            starts = [(block * inner + (i + turn) % inner) * width + k * cut for block, k in blocks]
            pieces.append((piece, starts))
        return pieces, steps

    own_turn, other_turns = [0], list(range(1, inner))
    early = [(w,) for w in w_cuts] + [(w,) for w in w_pair]
    early_blocks = [(z, k) for k in range(cuts)] + [(z ^ 1, k) for k in range(cuts)]
    third = [(w_mid1[k], w_end1[k]) for k in range(cuts)]
    third_blocks = [(jnp.where(low, 2, 1), k) for k in range(cuts)]
    fourth = [(w_mid2[k], w_end2[k]) for k in range(cuts)]
    fourth_block = jnp.where(low, 3, 0)
    rows_list, turns = [hidden] + others, own_turn + other_turns
    flag = hold(flag, w_end1[0], w_mid2[0], *square_steps[:1])
    pieces, steps = summed(flag, [hidden], own_turn, early, early_blocks)
    flag = hold(flag, squares, *steps, *w_end1, *w_mid2)
    more, steps = summed(flag, [hidden], own_turn, third, third_blocks)
    pieces += more
    flag = hold(flag, *steps, w_end2[0])
    partner_steps = []
    if others:
        more, partner_steps = summed(flag, others, other_turns, early + third, early_blocks + third_blocks)
        pieces += more
    for k in range(cuts):
        flag = hold(flag, *(partner_steps if k else partner_steps[:1]))
        last, steps = summed(flag, rows_list, turns, [fourth[k]], [(fourth_block, k)])
        flag = hold(flag, *steps[:1])
        if k + 1 < cuts:
            pieces += last
    shape = (out_rows, width * n_seq)
    if cut % DH == 0 and out_rows == DH:
        filled = placed(None, pieces, squares, cut, shape, total_width)
        return placed(filled, last, squares, cut, shape, total_width)
    scale = lax.rsqrt(squares.reshape(out_rows, 1) / total_width + epsilon)
    output = jnp.zeros(shape, jnp.bfloat16)
    for piece, starts in pieces + last:
        piece = (piece.astype(jnp.float32) * scale).astype(jnp.bfloat16)
        for index, start in enumerate(starts):
            part = piece[:, index * cut : (index + 1) * cut]
            output = lax.dynamic_update_slice_in_dim(output, part, start, 1)
    return output


def solution(mesh):
    in_specs = (
        P("seq", "head"),
        P("seq", "head"),
        P("seq", "head"),
        P("seq", "head"),
        P("head", None, None),
        P(),
        P("head", "seq"),
    )
    out_specs = P(("seq", "head"), None)
    return jax.shard_map(shards, mesh=mesh, in_specs=in_specs, out_specs=out_specs, check_vma=False)
```

```python
import functools

import jax
import jax.numpy as jnp
from jax import lax
from jax.experimental import pallas as pl
from jax.experimental.pallas import tpu as pltpu
from jax.sharding import PartitionSpec as P

DH = 128
BLOCK = 512
LINE = 4
VMEM_BYTES = 16 * 1024 * 1024


epsilon = 1e-05


def line_pairs(n_seq, hops):
    inner = n_seq // LINE
    return [(a * inner + i, b * inner + i) for a, b in hops for i in range(inner)]


def turn_pairs(n_seq, turn):
    inner = n_seq // LINE
    return [(a * inner + i, a * inner + (i + turn) % inner) for a in range(LINE) for i in range(inner)]


def flip_pairs(n_head, bit):
    return [(h, h ^ bit) for h in range(n_head)]


SWAP_OUTER = [(0, 1), (1, 0), (2, 3), (3, 2)]
SWAP_MIDDLE = [(1, 2), (2, 1)]
TO_ENDS = [(1, 0), (2, 3)]


def hold(value, *others):
    return lax.optimization_barrier((value, *others))[0]


def scalars(*values):
    return jnp.stack([jnp.asarray(value, jnp.int32) for value in values])


def local_call(kernel, places, operands, out_shapes, scratch=()):
    held = sum(value.size * value.dtype.itemsize for value in [*operands, *out_shapes])
    return pl.pallas_call(
        kernel,
        in_specs=[pl.BlockSpec(memory_space=pltpu.SMEM)]
        + [pl.BlockSpec(memory_space=pltpu.VMEM)] * len(operands),
        out_specs=[pl.BlockSpec(memory_space=pltpu.VMEM)] * len(out_shapes),
        out_shape=out_shapes,
        scratch_shapes=list(scratch),
        compiler_params=pltpu.CompilerParams(vmem_limit_bytes=max(VMEM_BYTES, held + held // 2)),
        cost_estimate=pl.CostEstimate(flops=1, bytes_accessed=1, transcendentals=0),
    )(places, *operands)


def combine_kernel(count, always, masks_ref, *refs):
    values, outs = refs[:count], refs[count:]
    for index in range(values[0].shape[0]):
        total = values[0][index].astype(jnp.float32)
        for value in values[1:always]:
            total = total + value[index].astype(jnp.float32)
        for position, out in enumerate(outs):
            own = total
            for k in range(always, count):
                mask = masks_ref[position * (count - always) + k - always]
                own = own + jnp.where(mask != 0, values[k][index].astype(jnp.float32), 0.0)
            out[index] = own.astype(out.dtype)


def combine(values, dtypes, sometimes=(), masks=None):
    operands = list(values) + list(sometimes)
    masks = scalars(0) if masks is None else scalars(*masks)
    return local_call(
        functools.partial(combine_kernel, len(operands), len(values)),
        masks,
        operands,
        [jax.ShapeDtypeStruct(values[0].shape, dtype) for dtype in dtypes],
    )


def cut_kernel(first, w_ref, out_ref, sem):
    copy = pltpu.make_async_copy(w_ref.at[:, pl.ds(first, out_ref.shape[1])], out_ref, sem)
    copy.start()
    copy.wait()


def cut_columns(weight, first, width):
    if width % DH:
        return weight[:, first : first + width]
    return pl.pallas_call(
        functools.partial(cut_kernel, first),
        in_specs=[pl.BlockSpec(memory_space=pl.ANY)],
        out_specs=pl.BlockSpec(memory_space=pltpu.VMEM),
        out_shape=jax.ShapeDtypeStruct((weight.shape[0], width), weight.dtype),
        scratch_shapes=[pltpu.SemaphoreType.DMA],
        compiler_params=pltpu.CompilerParams(vmem_limit_bytes=VMEM_BYTES),
        cost_estimate=pl.CostEstimate(flops=1, bytes_accessed=1, transcendentals=0),
    )(weight)


def states_kernel(part_ref, k_ref, v_ref, out_ref):
    heads = out_ref.shape[0]
    for index in range(heads):
        columns = pl.ds(pl.multiple_of((part_ref[0] * heads + index) * DH, DH), DH)
        out_ref[index] = lax.dot_general(
            k_ref[:, columns],
            v_ref[:, columns],
            (((0,), (0,)), ((), ())),
            preferred_element_type=jnp.float32,
        ).astype(out_ref.dtype)


def block_states(key_input, value_input, part, heads, dtype):
    return local_call(
        states_kernel,
        scalars(part),
        [key_input, value_input],
        [jax.ShapeDtypeStruct((heads, DH, DH), dtype)],
    )[0]


def state_prefix(key_input, value_input, n_seq, place, early):
    inner = n_seq // LINE
    i = place % inner
    heads = key_input.shape[1] // DH
    split = heads % inner == 0
    share = heads // inner if split else heads
    if split:
        sends = [
            block_states(key_input, value_input, (i + turn) % inner, share, jnp.bfloat16)
            for turn in range(1, inner)
        ]
        own = block_states(key_input, value_input, i, share, jnp.float32)
    else:
        own = block_states(key_input, value_input, 0, share, jnp.float32)
        sends = [own.astype(jnp.bfloat16)] * (inner - 1)
    values, members = [own], [i]
    for turn in range(1, inner):
        values.append(lax.ppermute(sends[turn - 1], "seq", turn_pairs(n_seq, turn)))
        members.append((i - turn) % inner)
    (first,) = combine(values, [jnp.bfloat16])
    from_left = lax.ppermute(first, "seq", line_pairs(n_seq, [(0, 1), (2, 3)]))
    from_left = hold(from_left, *early)
    (second,) = combine(values + [from_left], [jnp.bfloat16])
    near = lax.ppermute(second, "seq", line_pairs(n_seq, [(1, 2)]))
    far = lax.ppermute(second, "seq", line_pairs(n_seq, [(1, 3)]))
    targets = [i] + [(i + turn) % inner for turn in range(1, inner)] if split else [i]
    masks = [owner < target for target in targets for owner in members]
    dtypes = [jnp.float32] + [jnp.bfloat16] * (len(targets) - 1)
    befores = combine([from_left, near, far], dtypes, values, masks)
    terms = [befores[0]]
    for turn in range(1, len(targets)):
        terms.append(lax.ppermute(befores[turn], "seq", turn_pairs(n_seq, turn)))
    return terms, [near, far]


def causal_kernel(first_head, place_ref, q_ref, k_ref, v_ref, out_ref):
    rows = q_ref.shape[0]
    half = rows // 2
    top, bottom = pl.ds(0, half), pl.ds(half, half)
    keep = lax.broadcasted_iota(jnp.int32, (half, half), 0) >= lax.broadcasted_iota(
        jnp.int32, (half, half), 1
    )

    def scores(q_rows, k_rows, columns):
        return lax.dot_general(
            q_ref[q_rows, columns],
            k_ref[k_rows, columns],
            (((1,), (1,)), ((), ())),
            preferred_element_type=jnp.float32,
        )

    for index in range(out_ref.shape[1] // DH):
        columns = pl.ds((first_head + index) * DH, DH)
        placed = pl.ds(index * DH, DH)
        first = jnp.where(keep, scores(top, top, columns), 0.0).astype(jnp.bfloat16)
        below = scores(bottom, top, columns).astype(jnp.bfloat16)
        last = jnp.where(keep, scores(bottom, bottom, columns), 0.0).astype(jnp.bfloat16)
        out_ref[top, placed] = jnp.dot(first, v_ref[top, columns], preferred_element_type=jnp.float32)
        out_ref[bottom, placed] = jnp.dot(
            jnp.concatenate([below, last], axis=1),
            v_ref[:, columns],
            preferred_element_type=jnp.float32,
        )


def causal_part(queries, key_input, value_input, first_head, heads):
    return local_call(
        functools.partial(causal_kernel, first_head),
        scalars(0),
        [queries, key_input, value_input],
        [jax.ShapeDtypeStruct((queries.shape[0], heads * DH), jnp.float32)],
    )[0]


def hidden_kernel(order, group, calls, place_ref, q_ref, gate_ref, gain_ref, kv_ref, *refs):
    terms, inners = refs[:group], refs[group : group + calls]
    hidden_ref, squares_ref = refs[group + calls :]
    heads = kv_ref.shape[0]
    share = heads // group
    size = q_ref.shape[0] // len(order)
    states = []
    for head in range(heads):
        state = kv_ref[head]
        for turn, term in enumerate(terms):
            value = term[head % share].astype(jnp.float32)
            if group > 1:
                covers = lax.rem(place_ref[1] - turn + group, group)
                value = jnp.where(covers == head // share, value, 0.0)
            state = state + value
        high = state.astype(jnp.bfloat16)
        low = (state - high.astype(jnp.float32)).astype(jnp.bfloat16)
        states.append(jnp.concatenate([high, low], axis=0))
    for position, block in enumerate(order):
        start = pl.multiple_of((place_ref[0] ^ block) * size, size)
        rows = pl.ds(start, size)
        placed = pl.ds(position * size, size)
        squares = jnp.zeros((size, DH), jnp.float32)
        for head in range(heads):
            columns = pl.ds(head * DH, DH)
            q_rows = q_ref[rows, columns]
            carried = jnp.dot(
                jnp.concatenate([q_rows, q_rows], axis=1),
                states[head],
                preferred_element_type=jnp.float32,
            )
            per_call = inners[0].shape[1] // DH
            inner = inners[head // per_call][rows, pl.ds(head % per_call * DH, DH)]
            attn = (carried + inner).astype(jnp.bfloat16).astype(jnp.float32)
            gate = 1.0 + jnp.tanh(gate_ref[rows, columns].astype(jnp.float32) * 0.5)
            gain = gain_ref[place_ref[0] * heads + head] * 0.5
            hidden_ref[placed, columns] = (attn * (gain * gate)).astype(jnp.bfloat16)
            squares = squares + attn * attn
        squares_ref[pl.ds(position, 1), :] = jnp.sum(jnp.transpose(squares), axis=0, keepdims=True)


def gated_hidden(queries, inners, kv_state, terms, gate_input, norm_gain, h, i, order):
    rows, width = queries.shape
    return local_call(
        functools.partial(hidden_kernel, order, len(terms), len(inners)),
        scalars(h, i),
        [queries, gate_input, norm_gain.reshape(-1, 1, DH), kv_state, *terms, *inners],
        [
            jax.ShapeDtypeStruct((rows, width), jnp.bfloat16),
            jax.ShapeDtypeStruct((len(order), rows // len(order)), jnp.float32),
        ],
    )


def project_kernel(jobs, n_rows, choices, flag_ref, *refs):
    rows_refs = refs[:n_rows]
    weight_refs = refs[n_rows : n_rows + sum(choices)]
    sent_ref, kept_ref = refs[n_rows + sum(choices) :]
    half = sent_ref.shape[0]
    width = weight_refs[0].shape[1]

    def products(index, weight_ref):
        for position, (rows, weight) in enumerate(jobs):
            if weight == index:
                columns = pl.ds(position * width, width)
                product = jnp.dot(
                    rows_refs[rows][...], weight_ref[...], preferred_element_type=jnp.float32
                )
                kept_ref[:, columns] = product[:half]
                sent_ref[:, columns] = product[half:].astype(jnp.bfloat16)

    first = 0
    for index, number in enumerate(choices):
        for k in range(number):
            one = functools.partial(products, index, weight_refs[first + k])
            if number == 1:
                one()
            else:
                pl.when(flag_ref[0] == k)(one)
        first += number


def project(jobs, rows_list, weights, flag):
    flat = [choice for weight in weights for choice in weight]
    choices = tuple(len(weight) for weight in weights)
    shape = (rows_list[0].shape[0] // 2, flat[0].shape[1] * len(jobs))
    return local_call(
        functools.partial(project_kernel, tuple(jobs), len(rows_list), choices),
        flag,
        [*rows_list, *flat],
        [jax.ShapeDtypeStruct(shape, jnp.bfloat16), jax.ShapeDtypeStruct(shape, jnp.float32)],
    )


def fold_kernel(more, flag_ref, kept_ref, got_ref, *outs):
    if more:
        sent_ref, left_ref = outs
        half = left_ref.shape[0]
        left_ref[...] = kept_ref[:half] + got_ref[:half].astype(jnp.float32)
        sent_ref[...] = (kept_ref[half:] + got_ref[half:].astype(jnp.float32)).astype(jnp.bfloat16)
        return
    first = 0
    for out in outs:
        columns = pl.ds(first, out.shape[1])
        out[...] = (kept_ref[:, columns] + got_ref[:, columns].astype(jnp.float32)).astype(out.dtype)
        first += out.shape[1]


def fold(kept, got, widths=None):
    rows, width = kept.shape
    if widths is None:
        shape = (rows // 2, width)
        outs = [jax.ShapeDtypeStruct(shape, jnp.bfloat16), jax.ShapeDtypeStruct(shape, jnp.float32)]
    else:
        outs = [jax.ShapeDtypeStruct((rows, some), jnp.bfloat16) for some in widths]
    return local_call(functools.partial(fold_kernel, widths is None), scalars(0), [kept, got], outs)


def column(row):
    return jnp.transpose(jnp.broadcast_to(row, (row.shape[1], row.shape[1])))


def scaled_parts(counts, cut, squares_ref, pieces, total_width):
    scale = lax.rsqrt(column(squares_ref[...]) / total_width + epsilon)
    for piece, count in zip(pieces, counts):
        for index in range(count):
            for first in range(index * cut, (index + 1) * cut, DH):
                yield piece[:, pl.ds(first, DH)].astype(jnp.float32) * scale


def placed_kernel(counts, cut, total_width, starts_ref, squares_ref, *refs):
    out_ref = refs[-1]
    steps = cut // DH
    for at, part in enumerate(scaled_parts(counts, cut, squares_ref, refs[:-1], total_width)):
        start = pl.multiple_of(starts_ref[at // steps] + at % steps * DH, DH)
        out_ref[:, pl.ds(start, DH)] = part.astype(out_ref.dtype)


def added_kernel(counts, cut, total_width, starts_ref, squares_ref, *refs):
    pieces = refs[: len(counts)]
    out_ref, buf, sem = refs[-3:]
    steps = cut // DH
    copies = []
    for at, part in enumerate(scaled_parts(counts, cut, squares_ref, pieces, total_width)):
        where = at // steps
        buf[where, :, pl.ds(at % steps * DH, DH)] = part.astype(out_ref.dtype)
        if at % steps == steps - 1:
            start = pl.multiple_of(starts_ref[where], DH)
            copy = pltpu.make_async_copy(buf.at[where], out_ref.at[:, pl.ds(start, cut)], sem.at[where])
            copy.start()
            copies.append(copy)
    for copy in copies:
        copy.wait()


def placed(filled, pieces, squares, cut, shape, total_width):
    counts = tuple(len(starts) for _, starts in pieces)
    starts = scalars(*[start for _, own in pieces for start in own])
    operands = [squares] + [piece for piece, _ in pieces]
    out_shape = jax.ShapeDtypeStruct(shape, jnp.bfloat16)
    if filled is None:
        kernel = functools.partial(placed_kernel, counts, cut, total_width)
        return local_call(kernel, starts, operands, [out_shape])[0]
    return pl.pallas_call(
        functools.partial(added_kernel, counts, cut, total_width),
        in_specs=[pl.BlockSpec(memory_space=pltpu.SMEM)]
        + [pl.BlockSpec(memory_space=pltpu.VMEM)] * len(operands)
        + [pl.BlockSpec(memory_space=pl.ANY)],
        out_specs=pl.BlockSpec(memory_space=pl.ANY),
        out_shape=out_shape,
        scratch_shapes=[
            pltpu.VMEM((sum(counts), shape[0], cut), jnp.bfloat16),
            pltpu.SemaphoreType.DMA((sum(counts),)),
        ],
        input_output_aliases={len(operands) + 1: 0},
        compiler_params=pltpu.CompilerParams(vmem_limit_bytes=VMEM_BYTES),
        cost_estimate=pl.CostEstimate(flops=1, bytes_accessed=1, transcendentals=0),
    )(starts, *operands, filled)


def shards(queries, key_input, value_input, gate_input, kv_state, norm_gain, out_weight):
    n_seq, n_head = lax.axis_size("seq"), lax.axis_size("head")
    inner = n_seq // LINE
    place, h = lax.axis_index("seq"), lax.axis_index("head")
    z, i = place // inner, place % inner
    tok_rows, local_width = queries.shape
    assert tok_rows == BLOCK
    heads = local_width // DH
    total_width = local_width * n_head
    width = out_weight.shape[1]
    cuts = 2 if width % (2 * DH) == 0 else 1
    cut = width // cuts

    def along(value, hops):
        return lax.ppermute(value, "seq", line_pairs(n_seq, hops))

    w_cuts = [cut_columns(out_weight, k * cut, cut) for k in range(cuts)]
    w_pair = [along(w_cuts[0], SWAP_OUTER)]
    w_mid1 = [along(w_cuts[0], SWAP_MIDDLE)]
    terms, steps = state_prefix(key_input, value_input, n_seq, place, [w_pair[0], w_mid1[0]])
    some = heads // 2
    inners = [
        causal_part(queries, key_input, value_input, 0, some),
        causal_part(queries, key_input, value_input, some, heads - some),
    ]

    for k in range(1, cuts):
        w_pair.append(along(hold(w_cuts[k], *steps), SWAP_OUTER))
        w_mid1.append(along(hold(w_cuts[k], *steps), SWAP_MIDDLE))
    w_mid2 = [along(hold(w_pair[k], *steps), SWAP_MIDDLE) for k in range(cuts)]
    w_end1 = [along(hold(w_mid1[k], *steps), TO_ENDS) for k in range(cuts)]
    w_end2 = [along(w_mid2[k], TO_ENDS) for k in range(cuts)]

    bits = n_head.bit_length() - 1
    order = [int(format(j, "b").zfill(bits)[::-1], 2) for j in range(n_head)] if bits else [0]
    hidden, squares = gated_hidden(
        queries, inners, kv_state, terms, gate_input, norm_gain, h, i, order
    )
    others = [lax.ppermute(hidden, "seq", turn_pairs(n_seq, turn)) for turn in range(1, inner)]

    out_rows = tok_rows // n_head
    half, bit = n_head // 2, 1
    while bit < n_head:
        squares = squares[:half] + lax.ppermute(squares[half:], "head", flip_pairs(n_head, bit))
        half //= 2
        bit *= 2

    is_end = (z == 0) | (z == LINE - 1)
    low = z < LINE // 2
    flag = scalars(is_end)

    rows_list = [hidden] + others

    def summed(flag, parts):
        blocks = sorted({block for _, own in parts for block in own})
        turns = [turn for turn, _ in parts]
        jobs = [(p, blocks.index(block)) for p, (_, own) in enumerate(parts) for block in own]
        sent, kept = project(
            jobs, [rows_list[turn] for turn in turns], [weights[block] for block in blocks], flag
        )
        widths = [cut * len(own) for _, own in parts]
        bit, steps = 1, []
        while bit < n_head:
            steps.append(lax.ppermute(sent, "head", flip_pairs(n_head, bit)))
            bit *= 2
            if bit < n_head:
                sent, kept = fold(kept, steps[-1])
            else:
                kept = fold(kept, steps[-1], widths)
        pieces = []
        for piece, (turn, own) in zip(kept, parts):
            if turn:
                piece = lax.ppermute(piece, "seq", turn_pairs(n_seq, -turn))
            starts = [
                (owners[block] * inner + (i + turn) % inner) * width + k * cut for block, k in own
            ]
            pieces.append((piece, starts))
        return pieces, steps

    owners = [z, z ^ 1, jnp.where(low, 2, 1), jnp.where(low, 3, 0)]
    weights = {}
    for k in range(cuts):
        weights[0, k] = (w_cuts[k],)
        weights[1, k] = (w_pair[k],)
        weights[2, k] = (w_mid1[k], w_end1[k])
        weights[3, k] = (w_mid2[k], w_end2[k])
    cut_range = range(cuts)
    early = [(block, k) for block in (0, 1) for k in cut_range]
    third = [(2, k) for k in cut_range]
    other_turns = list(range(1, inner))
    flag = hold(flag, w_end1[0], w_mid2[0])
    pieces, steps = summed(flag, [(0, early)])
    flag = hold(flag, squares, *steps, *w_end1, *w_mid2)
    more, late_steps = summed(flag, [(0, third)] + [(turn, early + third) for turn in other_turns])
    pieces += more
    flag = hold(flag, late_steps[0])
    for k in cut_range:
        last, steps = summed(flag, [(turn, [(3, k)]) for turn in [0] + other_turns])
        flag = hold(flag, steps[0], *late_steps)
        if k + 1 < cuts:
            pieces += last
    shape = (out_rows, width * n_seq)
    if cut % DH == 0 and out_rows == DH:
        filled = placed(None, pieces, squares, cut, shape, total_width)
        return placed(filled, last, squares, cut, shape, total_width)
    scale = lax.rsqrt(squares.reshape(out_rows, 1) / total_width + epsilon)
    output = jnp.zeros(shape, jnp.bfloat16)
    for piece, starts in pieces + last:
        piece = (piece.astype(jnp.float32) * scale).astype(jnp.bfloat16)
        for index, start in enumerate(starts):
            part = piece[:, index * cut : (index + 1) * cut]
            output = lax.dynamic_update_slice_in_dim(output, part, start, 1)
    return output


def solution(mesh):
    in_specs = (
        P("seq", "head"),
        P("seq", "head"),
        P("seq", "head"),
        P("seq", "head"),
        P("head", None, None),
        P(),
        P("head", "seq"),
    )
    out_specs = P(("seq", "head"), None)
    return jax.shard_map(shards, mesh=mesh, in_specs=in_specs, out_specs=out_specs, check_vma=False)
```

```python
import functools

import jax
import jax.numpy as jnp
from jax import lax
from jax.experimental import pallas as pl
from jax.experimental.pallas import tpu as pltpu
from jax.sharding import PartitionSpec as P

DH = 128
BLOCK = 512
LINE = 4
VMEM_BYTES = 16 * 1024 * 1024


epsilon = 1e-05


def line_pairs(n_seq, hops):
    inner = n_seq // LINE
    return [(a * inner + i, b * inner + i) for a, b in hops for i in range(inner)]


def turn_pairs(n_seq, turn):
    inner = n_seq // LINE
    return [(a * inner + i, a * inner + (i + turn) % inner) for a in range(LINE) for i in range(inner)]


def flip_pairs(n_head, bit):
    return [(h, h ^ bit) for h in range(n_head)]


SWAP_OUTER = [(0, 1), (1, 0), (2, 3), (3, 2)]
SWAP_MIDDLE = [(1, 2), (2, 1)]
TO_ENDS = [(1, 0), (2, 3)]


def hold(value, *others):
    return lax.optimization_barrier((value, *others))[0]


def scalars(*values):
    return jnp.stack([jnp.asarray(value, jnp.int32) for value in values])


def local_call(kernel, places, operands, out_shapes, scratch=()):
    held = sum(value.size * value.dtype.itemsize for value in [*operands, *out_shapes])
    return pl.pallas_call(
        kernel,
        in_specs=[pl.BlockSpec(memory_space=pltpu.SMEM)]
        + [pl.BlockSpec(memory_space=pltpu.VMEM)] * len(operands),
        out_specs=[pl.BlockSpec(memory_space=pltpu.VMEM)] * len(out_shapes),
        out_shape=out_shapes,
        scratch_shapes=list(scratch),
        compiler_params=pltpu.CompilerParams(vmem_limit_bytes=max(VMEM_BYTES, held + held // 2)),
        cost_estimate=pl.CostEstimate(flops=1, bytes_accessed=1, transcendentals=0),
    )(places, *operands)


def combine_kernel(count, always, masks_ref, *refs):
    values, outs = refs[:count], refs[count:]
    for index in range(values[0].shape[0]):
        total = values[0][index].astype(jnp.float32)
        for value in values[1:always]:
            total = total + value[index].astype(jnp.float32)
        for position, out in enumerate(outs):
            own = total
            for k in range(always, count):
                mask = masks_ref[position * (count - always) + k - always]
                own = own + jnp.where(mask != 0, values[k][index].astype(jnp.float32), 0.0)
            out[index] = own.astype(out.dtype)


def combine(values, dtypes, sometimes=(), masks=None):
    operands = list(values) + list(sometimes)
    masks = scalars(0) if masks is None else scalars(*masks)
    return local_call(
        functools.partial(combine_kernel, len(operands), len(values)),
        masks,
        operands,
        [jax.ShapeDtypeStruct(values[0].shape, dtype) for dtype in dtypes],
    )


def cut_kernel(first, w_ref, out_ref, sem):
    copy = pltpu.make_async_copy(w_ref.at[:, pl.ds(first, out_ref.shape[1])], out_ref, sem)
    copy.start()
    copy.wait()


def cut_columns(weight, first, width):
    if width % DH:
        return weight[:, first : first + width]
    return pl.pallas_call(
        functools.partial(cut_kernel, first),
        in_specs=[pl.BlockSpec(memory_space=pl.ANY)],
        out_specs=pl.BlockSpec(memory_space=pltpu.VMEM),
        out_shape=jax.ShapeDtypeStruct((weight.shape[0], width), weight.dtype),
        scratch_shapes=[pltpu.SemaphoreType.DMA],
        compiler_params=pltpu.CompilerParams(vmem_limit_bytes=VMEM_BYTES),
        cost_estimate=pl.CostEstimate(flops=1, bytes_accessed=1, transcendentals=0),
    )(weight)


def states_kernel(part_ref, k_ref, v_ref, out_ref, k_buf, v_buf, sems):
    heads = out_ref.shape[0]
    copies = []
    for index in range(heads):
        source = pl.ds(pl.multiple_of((part_ref[0] * heads + index) * DH, DH), DH)
        target = pl.ds(index * DH, DH)
        for which, (ref, buf) in enumerate(((k_ref, k_buf), (v_ref, v_buf))):
            copies.append(
                pltpu.make_async_copy(ref.at[:, source], buf.at[:, target], sems.at[which, index])
            )
            copies[-1].start()
    for index in range(heads):
        columns = pl.ds(index * DH, DH)
        copies[2 * index].wait()
        copies[2 * index + 1].wait()
        out_ref[index] = lax.dot_general(
            k_buf[:, columns],
            v_buf[:, columns],
            (((0,), (0,)), ((), ())),
            preferred_element_type=jnp.float32,
        ).astype(out_ref.dtype)


def block_states(key_input, value_input, part, heads, dtype):
    rows = key_input.shape[0]
    return pl.pallas_call(
        states_kernel,
        in_specs=[pl.BlockSpec(memory_space=pltpu.SMEM)] + [pl.BlockSpec(memory_space=pl.ANY)] * 2,
        out_specs=pl.BlockSpec(memory_space=pltpu.VMEM),
        out_shape=jax.ShapeDtypeStruct((heads, DH, DH), dtype),
        scratch_shapes=[
            pltpu.VMEM((rows, heads * DH), key_input.dtype),
            pltpu.VMEM((rows, heads * DH), value_input.dtype),
            pltpu.SemaphoreType.DMA((2, heads)),
        ],
        compiler_params=pltpu.CompilerParams(vmem_limit_bytes=VMEM_BYTES),
        cost_estimate=pl.CostEstimate(flops=1, bytes_accessed=1, transcendentals=0),
    )(scalars(part), key_input, value_input)


def state_prefix(key_input, value_input, n_seq, place, early):
    inner = n_seq // LINE
    i = place % inner
    heads = key_input.shape[1] // DH
    split = heads % inner == 0
    share = heads // inner if split else heads
    if split:
        sends = [
            block_states(key_input, value_input, (i + turn) % inner, share, jnp.bfloat16)
            for turn in range(1, inner)
        ]
        own = block_states(key_input, value_input, i, share, jnp.float32)
    else:
        own = block_states(key_input, value_input, 0, share, jnp.float32)
        sends = [own.astype(jnp.bfloat16)] * (inner - 1)
    values, members = [own], [i]
    for turn in range(1, inner):
        values.append(lax.ppermute(sends[turn - 1], "seq", turn_pairs(n_seq, turn)))
        members.append((i - turn) % inner)
    (first,) = combine(values, [jnp.bfloat16])
    from_left = lax.ppermute(first, "seq", line_pairs(n_seq, [(0, 1), (2, 3)]))
    from_left = hold(from_left, *early)
    (second,) = combine(values + [from_left], [jnp.bfloat16])
    near = lax.ppermute(second, "seq", line_pairs(n_seq, [(1, 2)]))
    far = lax.ppermute(second, "seq", line_pairs(n_seq, [(1, 3)]))
    targets = [i] + [(i + turn) % inner for turn in range(1, inner)] if split else [i]
    masks = [owner < target for target in targets for owner in members]
    dtypes = [jnp.float32] + [jnp.bfloat16] * (len(targets) - 1)
    befores = combine([from_left, near, far], dtypes, values, masks)
    terms = [befores[0]]
    for turn in range(1, len(targets)):
        terms.append(lax.ppermute(befores[turn], "seq", turn_pairs(n_seq, turn)))
    return terms, befores[0]


def causal_kernel(first_head, place_ref, q_ref, k_ref, v_ref, out_ref):
    rows = q_ref.shape[0]
    half = rows // 2
    top, bottom = pl.ds(0, half), pl.ds(half, half)
    keep = lax.broadcasted_iota(jnp.int32, (half, half), 0) >= lax.broadcasted_iota(
        jnp.int32, (half, half), 1
    )

    def scores(q_rows, k_rows, columns):
        return lax.dot_general(
            q_ref[q_rows, columns],
            k_ref[k_rows, columns],
            (((1,), (1,)), ((), ())),
            preferred_element_type=jnp.float32,
        )

    for index in range(out_ref.shape[1] // DH):
        columns = pl.ds((first_head + index) * DH, DH)
        placed = pl.ds(index * DH, DH)
        first = jnp.where(keep, scores(top, top, columns), 0.0).astype(jnp.bfloat16)
        below = scores(bottom, top, columns).astype(jnp.bfloat16)
        last = jnp.where(keep, scores(bottom, bottom, columns), 0.0).astype(jnp.bfloat16)
        out_ref[top, placed] = jnp.dot(first, v_ref[top, columns], preferred_element_type=jnp.float32)
        out_ref[bottom, placed] = jnp.dot(
            jnp.concatenate([below, last], axis=1),
            v_ref[:, columns],
            preferred_element_type=jnp.float32,
        )


def causal_part(queries, key_input, value_input, first_head, heads):
    return local_call(
        functools.partial(causal_kernel, first_head),
        scalars(0),
        [queries, key_input, value_input],
        [jax.ShapeDtypeStruct((queries.shape[0], heads * DH), jnp.float32)],
    )[0]


def hidden_kernel(order, group, calls, place_ref, q_ref, gate_ref, gain_ref, kv_ref, *refs):
    terms, inners = refs[:group], refs[group : group + calls]
    hidden_ref, squares_ref = refs[group + calls :]
    heads = kv_ref.shape[0]
    share = heads // group
    size = q_ref.shape[0] // len(order)
    states = []
    for head in range(heads):
        state = kv_ref[head]
        for turn, term in enumerate(terms):
            value = term[head % share].astype(jnp.float32)
            if group > 1:
                covers = lax.rem(place_ref[1] - turn + group, group)
                value = jnp.where(covers == head // share, value, 0.0)
            state = state + value
        high = state.astype(jnp.bfloat16)
        low = (state - high.astype(jnp.float32)).astype(jnp.bfloat16)
        states.append(jnp.concatenate([high, low], axis=0))
    for position, block in enumerate(order):
        start = pl.multiple_of((place_ref[0] ^ block) * size, size)
        rows = pl.ds(start, size)
        placed = pl.ds(position * size, size)
        squares = jnp.zeros((size, DH), jnp.float32)
        for head in range(heads):
            columns = pl.ds(head * DH, DH)
            q_rows = q_ref[rows, columns]
            carried = jnp.dot(
                jnp.concatenate([q_rows, q_rows], axis=1),
                states[head],
                preferred_element_type=jnp.float32,
            )
            per_call = inners[0].shape[1] // DH
            inner = inners[head // per_call][rows, pl.ds(head % per_call * DH, DH)]
            attn = (carried + inner).astype(jnp.bfloat16).astype(jnp.float32)
            gate = 1.0 + jnp.tanh(gate_ref[rows, columns].astype(jnp.float32) * 0.5)
            gain = gain_ref[place_ref[0] * heads + head] * 0.5
            hidden_ref[placed, columns] = (attn * (gain * gate)).astype(jnp.bfloat16)
            squares = squares + attn * attn
        squares_ref[pl.ds(position, 1), :] = jnp.sum(jnp.transpose(squares), axis=0, keepdims=True)


def gated_hidden(queries, inners, kv_state, terms, gate_input, norm_gain, h, i, order):
    rows, width = queries.shape
    return local_call(
        functools.partial(hidden_kernel, order, len(terms), len(inners)),
        scalars(h, i),
        [queries, gate_input, norm_gain.reshape(-1, 1, DH), kv_state, *terms, *inners],
        [
            jax.ShapeDtypeStruct((rows, width), jnp.bfloat16),
            jax.ShapeDtypeStruct((len(order), rows // len(order)), jnp.float32),
        ],
    )


def project_kernel(jobs, n_rows, choices, flag_ref, *refs):
    rows_refs = refs[:n_rows]
    weight_refs = refs[n_rows : n_rows + sum(choices)]
    sent_ref, kept_ref = refs[n_rows + sum(choices) :]
    half = sent_ref.shape[0]
    width = weight_refs[0].shape[1]

    def products(index, weight_ref):
        for position, (rows, weight) in enumerate(jobs):
            if weight == index:
                columns = pl.ds(position * width, width)
                product = jnp.dot(
                    rows_refs[rows][...], weight_ref[...], preferred_element_type=jnp.float32
                )
                kept_ref[:, columns] = product[:half]
                sent_ref[:, columns] = product[half:].astype(jnp.bfloat16)

    first = 0
    for index, number in enumerate(choices):
        for k in range(number):
            one = functools.partial(products, index, weight_refs[first + k])
            if number == 1:
                one()
            else:
                pl.when(flag_ref[0] == k)(one)
        first += number


def project(jobs, rows_list, weights, flag):
    flat = [choice for weight in weights for choice in weight]
    choices = tuple(len(weight) for weight in weights)
    shape = (rows_list[0].shape[0] // 2, flat[0].shape[1] * len(jobs))
    return local_call(
        functools.partial(project_kernel, tuple(jobs), len(rows_list), choices),
        flag,
        [*rows_list, *flat],
        [jax.ShapeDtypeStruct(shape, jnp.bfloat16), jax.ShapeDtypeStruct(shape, jnp.float32)],
    )


def fold_kernel(more, flag_ref, kept_ref, got_ref, *outs):
    if more:
        sent_ref, left_ref = outs
        half = left_ref.shape[0]
        left_ref[...] = kept_ref[:half] + got_ref[:half].astype(jnp.float32)
        sent_ref[...] = (kept_ref[half:] + got_ref[half:].astype(jnp.float32)).astype(jnp.bfloat16)
        return
    first = 0
    for out in outs:
        columns = pl.ds(first, out.shape[1])
        out[...] = (kept_ref[:, columns] + got_ref[:, columns].astype(jnp.float32)).astype(out.dtype)
        first += out.shape[1]


def fold(kept, got, widths=None):
    rows, width = kept.shape
    if widths is None:
        shape = (rows // 2, width)
        outs = [jax.ShapeDtypeStruct(shape, jnp.bfloat16), jax.ShapeDtypeStruct(shape, jnp.float32)]
    else:
        outs = [jax.ShapeDtypeStruct((rows, some), jnp.bfloat16) for some in widths]
    return local_call(functools.partial(fold_kernel, widths is None), scalars(0), [kept, got], outs)


def column(row):
    return jnp.transpose(jnp.broadcast_to(row, (row.shape[1], row.shape[1])))


def scaled_parts(counts, cut, squares_ref, pieces, total_width):
    scale = lax.rsqrt(column(squares_ref[...]) / total_width + epsilon)
    for piece, count in zip(pieces, counts):
        for index in range(count):
            for first in range(index * cut, (index + 1) * cut, DH):
                yield piece[:, pl.ds(first, DH)].astype(jnp.float32) * scale


def placed_kernel(counts, cut, total_width, starts_ref, squares_ref, *refs):
    out_ref = refs[-1]
    steps = cut // DH
    for at, part in enumerate(scaled_parts(counts, cut, squares_ref, refs[:-1], total_width)):
        start = pl.multiple_of(starts_ref[at // steps] + at % steps * DH, DH)
        out_ref[:, pl.ds(start, DH)] = part.astype(out_ref.dtype)


def added_kernel(counts, cut, total_width, starts_ref, squares_ref, *refs):
    pieces = refs[: len(counts)]
    out_ref, buf, sem = refs[-3:]
    steps = cut // DH
    copies = []
    for at, part in enumerate(scaled_parts(counts, cut, squares_ref, pieces, total_width)):
        where = at // steps
        buf[where, :, pl.ds(at % steps * DH, DH)] = part.astype(out_ref.dtype)
        if at % steps == steps - 1:
            start = pl.multiple_of(starts_ref[where], DH)
            copy = pltpu.make_async_copy(buf.at[where], out_ref.at[:, pl.ds(start, cut)], sem.at[where])
            copy.start()
            copies.append(copy)
    for copy in copies:
        copy.wait()


def placed(filled, pieces, squares, cut, shape, total_width):
    counts = tuple(len(starts) for _, starts in pieces)
    starts = scalars(*[start for _, own in pieces for start in own])
    operands = [squares] + [piece for piece, _ in pieces]
    out_shape = jax.ShapeDtypeStruct(shape, jnp.bfloat16)
    if filled is None:
        kernel = functools.partial(placed_kernel, counts, cut, total_width)
        return local_call(kernel, starts, operands, [out_shape])[0]
    return pl.pallas_call(
        functools.partial(added_kernel, counts, cut, total_width),
        in_specs=[pl.BlockSpec(memory_space=pltpu.SMEM)]
        + [pl.BlockSpec(memory_space=pltpu.VMEM)] * len(operands)
        + [pl.BlockSpec(memory_space=pl.ANY)],
        out_specs=pl.BlockSpec(memory_space=pl.ANY),
        out_shape=out_shape,
        scratch_shapes=[
            pltpu.VMEM((sum(counts), shape[0], cut), jnp.bfloat16),
            pltpu.SemaphoreType.DMA((sum(counts),)),
        ],
        input_output_aliases={len(operands) + 1: 0},
        compiler_params=pltpu.CompilerParams(vmem_limit_bytes=VMEM_BYTES),
        cost_estimate=pl.CostEstimate(flops=1, bytes_accessed=1, transcendentals=0),
    )(starts, *operands, filled)


def shards(queries, key_input, value_input, gate_input, kv_state, norm_gain, out_weight):
    n_seq, n_head = lax.axis_size("seq"), lax.axis_size("head")
    inner = n_seq // LINE
    place, h = lax.axis_index("seq"), lax.axis_index("head")
    z, i = place // inner, place % inner
    tok_rows, local_width = queries.shape
    assert tok_rows == BLOCK
    heads = local_width // DH
    total_width = local_width * n_head
    width = out_weight.shape[1]
    cuts = 2 if width % (2 * DH) == 0 else 1
    cut = width // cuts

    def along(value, hops):
        return lax.ppermute(value, "seq", line_pairs(n_seq, hops))

    w_cuts = [cut_columns(out_weight, k * cut, cut) for k in range(cuts)]
    w_pair = [along(w_cuts[0], SWAP_OUTER)]
    w_mid1 = [along(w_cuts[0], SWAP_MIDDLE)]
    terms, stepped = state_prefix(key_input, value_input, n_seq, place, [w_pair[0], w_mid1[0]])
    some = heads // 2
    inners = [
        causal_part(queries, key_input, value_input, 0, some),
        causal_part(queries, key_input, value_input, some, heads - some),
    ]

    for k in range(1, cuts):
        w_pair.append(along(hold(w_cuts[k], stepped), SWAP_OUTER))
        w_mid1.append(along(hold(w_cuts[k], stepped), SWAP_MIDDLE))
    w_mid2 = [along(hold(w_pair[k], stepped), SWAP_MIDDLE) for k in range(cuts)]
    w_end1 = [along(hold(w_mid1[k], stepped), TO_ENDS) for k in range(cuts)]
    w_end2 = [along(w_mid2[k], TO_ENDS) for k in range(cuts)]

    bits = n_head.bit_length() - 1
    order = [int(format(j, "b").zfill(bits)[::-1], 2) for j in range(n_head)] if bits else [0]
    terms[0] = hold(terms[0], *w_pair[1:], *w_mid1[1:])
    hidden, squares = gated_hidden(
        queries, inners, kv_state, terms, gate_input, norm_gain, h, i, order
    )
    others = [lax.ppermute(hidden, "seq", turn_pairs(n_seq, turn)) for turn in range(1, inner)]

    out_rows = tok_rows // n_head
    half, bit = n_head // 2, 1
    while bit < n_head:
        squares = squares[:half] + lax.ppermute(squares[half:], "head", flip_pairs(n_head, bit))
        half //= 2
        bit *= 2

    is_end = (z == 0) | (z == LINE - 1)
    low = z < LINE // 2
    flag = scalars(is_end)

    rows_list = [hidden] + others

    def summed(flag, parts):
        blocks = sorted({block for _, own in parts for block in own})
        turns = [turn for turn, _ in parts]
        jobs = [(p, blocks.index(block)) for p, (_, own) in enumerate(parts) for block in own]
        sent, kept = project(
            jobs, [rows_list[turn] for turn in turns], [weights[block] for block in blocks], flag
        )
        sent_first = sent
        widths = [cut * len(own) for _, own in parts]
        bit, steps = 1, []
        while bit < n_head:
            steps.append(lax.ppermute(sent, "head", flip_pairs(n_head, bit)))
            bit *= 2
            if bit < n_head:
                sent, kept = fold(kept, steps[-1])
            else:
                kept = fold(kept, steps[-1], widths)
        pieces = []
        for piece, (turn, own) in zip(kept, parts):
            if turn:
                piece = lax.ppermute(piece, "seq", turn_pairs(n_seq, -turn))
            starts = [
                (owners[block] * inner + (i + turn) % inner) * width + k * cut for block, k in own
            ]
            pieces.append((piece, starts))
        return pieces, sent_first, steps

    owners = [z, z ^ 1, jnp.where(low, 2, 1), jnp.where(low, 3, 0)]
    weights = {}
    for k in range(cuts):
        weights[0, k] = (w_cuts[k],)
        weights[1, k] = (w_pair[k],)
        weights[2, k] = (w_mid1[k], w_end1[k])
        weights[3, k] = (w_mid2[k], w_end2[k])
    turns = list(range(inner))
    pieces = []

    def group(members, block, pins):
        more, sent, steps = summed(
            hold(flag, *pins), [(turn, [(block, k) for k in range(cuts)]) for turn in members]
        )
        pieces.extend(more)
        return sent, steps

    shape = (out_rows, width * n_seq)
    in_kernel = cut % DH == 0 and out_rows == DH

    pins = [w_end1[0], w_mid2[0]]
    sent, steps_own = group(turns[:1], 0, pins)
    sent, steps_pair = group(turns[:1], 1, [sent])
    steps_other = []
    for block in (0, 1) if inner > 1 else ():
        sent, steps = group(turns[1:], block, [sent, squares])
        steps_other += steps
    sent, steps_third = group(turns[:1], 2, [sent, *w_end1, *w_mid2, *steps_own, *steps_pair])
    if inner > 1:
        sent, steps = group(turns[1:], 2, [sent])
        steps_third += steps
    pins = [sent, *steps_other]
    filled = None
    for k in range(cuts):
        if k + 1 == cuts and in_kernel:
            filled = placed(None, pieces, squares, cut, shape, total_width)
            pins = [filled]
        last, sent, steps = summed(hold(flag, *pins), [(turn, [(3, k)]) for turn in turns])
        if k + 1 < cuts:
            pieces += last
            pins = [sent]
    if in_kernel:
        return placed(filled, last, squares, cut, shape, total_width)
    scale = lax.rsqrt(squares.reshape(out_rows, 1) / total_width + epsilon)
    output = jnp.zeros(shape, jnp.bfloat16)
    for piece, starts in pieces + last:
        piece = (piece.astype(jnp.float32) * scale).astype(jnp.bfloat16)
        for index, start in enumerate(starts):
            part = piece[:, index * cut : (index + 1) * cut]
            output = lax.dynamic_update_slice_in_dim(output, part, start, 1)
    return output


def solution(mesh):
    in_specs = (
        P("seq", "head"),
        P("seq", "head"),
        P("seq", "head"),
        P("seq", "head"),
        P("head", None, None),
        P(),
        P("head", "seq"),
    )
    out_specs = P(("seq", "head"), None)
    return jax.shard_map(shards, mesh=mesh, in_specs=in_specs, out_specs=out_specs, check_vma=False)
```

```python
import functools

import jax
import jax.numpy as jnp
from jax import lax
from jax.experimental import pallas as pl
from jax.experimental.pallas import tpu as pltpu
from jax.sharding import PartitionSpec as P

DH = 128
BLOCK = 512
LINE = 4
VMEM_BYTES = 16 * 1024 * 1024


epsilon = 1e-05


def line_pairs(n_seq, hops):
    inner = n_seq // LINE
    return [(a * inner + i, b * inner + i) for a, b in hops for i in range(inner)]


def turn_pairs(n_seq, turn):
    inner = n_seq // LINE
    return [(a * inner + i, a * inner + (i + turn) % inner) for a in range(LINE) for i in range(inner)]


def flip_pairs(n_head, bit):
    return [(h, h ^ bit) for h in range(n_head)]


SWAP_OUTER = [(0, 1), (1, 0), (2, 3), (3, 2)]
SWAP_MIDDLE = [(1, 2), (2, 1)]
TO_ENDS = [(1, 0), (2, 3)]


def hold(value, *others):
    return lax.optimization_barrier((value, *others))[0]


def scalars(*values):
    return jnp.stack([jnp.asarray(value, jnp.int32) for value in values])


def local_call(kernel, places, operands, out_shapes, flops=0):
    held = sum(value.size * value.dtype.itemsize for value in [*operands, *out_shapes])
    return pl.pallas_call(
        kernel,
        in_specs=[pl.BlockSpec(memory_space=pltpu.SMEM)]
        + [pl.BlockSpec(memory_space=pltpu.VMEM)] * len(operands),
        out_specs=[pl.BlockSpec(memory_space=pltpu.VMEM)] * len(out_shapes),
        out_shape=out_shapes,
        compiler_params=pltpu.CompilerParams(vmem_limit_bytes=max(VMEM_BYTES, held + held // 2)),
        cost_estimate=pl.CostEstimate(flops=flops, bytes_accessed=held, transcendentals=0),
    )(places, *operands)


def combine_kernel(count, always, masks_ref, *refs):
    values, outs = refs[:count], refs[count:]
    for index in range(values[0].shape[0]):
        total = values[0][index].astype(jnp.float32)
        for value in values[1:always]:
            total = total + value[index].astype(jnp.float32)
        for position, out in enumerate(outs):
            own = total
            for k in range(always, count):
                mask = masks_ref[position * (count - always) + k - always]
                own = own + jnp.where(mask != 0, values[k][index].astype(jnp.float32), 0.0)
            out[index] = own.astype(out.dtype)


def combine(values, dtypes, sometimes=(), masks=None):
    operands = list(values) + list(sometimes)
    masks = scalars(0) if masks is None else scalars(*masks)
    return local_call(
        functools.partial(combine_kernel, len(operands), len(values)),
        masks,
        operands,
        [jax.ShapeDtypeStruct(values[0].shape, dtype) for dtype in dtypes],
    )


def cut_kernel(first, w_ref, out_ref, sem):
    copy = pltpu.make_async_copy(w_ref.at[:, pl.ds(first, out_ref.shape[1])], out_ref, sem)
    copy.start()
    copy.wait()


def cut_columns(weight, first, width):
    if width % DH:
        return weight[:, first : first + width]
    return pl.pallas_call(
        functools.partial(cut_kernel, first),
        in_specs=[pl.BlockSpec(memory_space=pltpu.HBM)],
        out_specs=pl.BlockSpec(memory_space=pltpu.VMEM),
        out_shape=jax.ShapeDtypeStruct((weight.shape[0], width), weight.dtype),
        scratch_shapes=[pltpu.SemaphoreType.DMA],
        compiler_params=pltpu.CompilerParams(vmem_limit_bytes=VMEM_BYTES),
        cost_estimate=pl.CostEstimate(
            flops=0, bytes_accessed=4 * weight.shape[0] * width, transcendentals=0
        ),
    )(weight)


def states_kernel(part_ref, k_ref, v_ref, out_ref, k_buf, v_buf, sems):
    heads = out_ref.shape[0]
    copies = []
    for index in range(heads):
        source = pl.ds(pl.multiple_of((part_ref[0] * heads + index) * DH, DH), DH)
        target = pl.ds(index * DH, DH)
        for which, (ref, buf) in enumerate(((k_ref, k_buf), (v_ref, v_buf))):
            copies.append(
                pltpu.make_async_copy(ref.at[:, source], buf.at[:, target], sems.at[which, index])
            )
            copies[-1].start()
    for index in range(heads):
        columns = pl.ds(index * DH, DH)
        copies[2 * index].wait()
        copies[2 * index + 1].wait()
        out_ref[index] = lax.dot_general(
            k_buf[:, columns],
            v_buf[:, columns],
            (((0,), (0,)), ((), ())),
            preferred_element_type=jnp.float32,
        ).astype(out_ref.dtype)


def block_states(key_input, value_input, part, heads, dtype):
    rows = key_input.shape[0]
    return pl.pallas_call(
        states_kernel,
        in_specs=[pl.BlockSpec(memory_space=pltpu.SMEM)] + [pl.BlockSpec(memory_space=pltpu.HBM)] * 2,
        out_specs=pl.BlockSpec(memory_space=pltpu.VMEM),
        out_shape=jax.ShapeDtypeStruct((heads, DH, DH), dtype),
        scratch_shapes=[
            pltpu.VMEM((rows, heads * DH), key_input.dtype),
            pltpu.VMEM((rows, heads * DH), value_input.dtype),
            pltpu.SemaphoreType.DMA((2, heads)),
        ],
        compiler_params=pltpu.CompilerParams(vmem_limit_bytes=VMEM_BYTES),
        cost_estimate=pl.CostEstimate(
            flops=2 * rows * heads * DH * DH, bytes_accessed=4 * rows * heads * DH, transcendentals=0
        ),
    )(scalars(part), key_input, value_input)


def state_prefix(key_input, value_input, n_seq, place, early):
    inner = n_seq // LINE
    i = place % inner
    heads = key_input.shape[1] // DH
    split = heads % inner == 0
    share = heads // inner if split else heads
    if split:
        sends = [
            block_states(key_input, value_input, (i + turn) % inner, share, jnp.bfloat16)
            for turn in range(1, inner)
        ]
        own = block_states(key_input, value_input, i, share, jnp.float32)
    else:
        own = block_states(key_input, value_input, 0, share, jnp.float32)
        sends = [own.astype(jnp.bfloat16)] * (inner - 1)
    values, members = [own], [i]
    for turn in range(1, inner):
        values.append(lax.ppermute(sends[turn - 1], "seq", turn_pairs(n_seq, turn)))
        members.append((i - turn) % inner)
    (first,) = combine(values, [jnp.bfloat16])
    from_left = lax.ppermute(first, "seq", line_pairs(n_seq, [(0, 1), (2, 3)]))
    from_left = hold(from_left, *early)
    (second,) = combine(values + [from_left], [jnp.bfloat16])
    near = lax.ppermute(second, "seq", line_pairs(n_seq, [(1, 2)]))
    far = lax.ppermute(second, "seq", line_pairs(n_seq, [(1, 3)]))
    targets = [i] + [(i + turn) % inner for turn in range(1, inner)] if split else [i]
    masks = [owner < target for target in targets for owner in members]
    dtypes = [jnp.float32] + [jnp.bfloat16] * (len(targets) - 1)
    befores = combine([from_left, near, far], dtypes, values, masks)
    terms = [befores[0]]
    for turn in range(1, len(targets)):
        terms.append(lax.ppermute(befores[turn], "seq", turn_pairs(n_seq, turn)))
    return terms, befores[0]


def causal_kernel(first_head, place_ref, q_ref, k_ref, v_ref, out_ref):
    rows = q_ref.shape[0]
    half = rows // 2
    top, bottom = pl.ds(0, half), pl.ds(half, half)
    keep = lax.broadcasted_iota(jnp.int32, (half, half), 0) >= lax.broadcasted_iota(
        jnp.int32, (half, half), 1
    )

    def scores(q_rows, k_rows, columns):
        return lax.dot_general(
            q_ref[q_rows, columns],
            k_ref[k_rows, columns],
            (((1,), (1,)), ((), ())),
            preferred_element_type=jnp.float32,
        )

    for index in range(out_ref.shape[1] // DH):
        columns = pl.ds((first_head + index) * DH, DH)
        placed = pl.ds(index * DH, DH)
        first = jnp.where(keep, scores(top, top, columns), 0.0).astype(jnp.bfloat16)
        below = scores(bottom, top, columns).astype(jnp.bfloat16)
        last = jnp.where(keep, scores(bottom, bottom, columns), 0.0).astype(jnp.bfloat16)
        out_ref[top, placed] = jnp.dot(first, v_ref[top, columns], preferred_element_type=jnp.float32)
        out_ref[bottom, placed] = jnp.dot(
            jnp.concatenate([below, last], axis=1),
            v_ref[:, columns],
            preferred_element_type=jnp.float32,
        )


def causal_part(queries, key_input, value_input, first_head, heads):
    return local_call(
        functools.partial(causal_kernel, first_head),
        scalars(0),
        [queries, key_input, value_input],
        [jax.ShapeDtypeStruct((queries.shape[0], heads * DH), jnp.float32)],
        3 * queries.shape[0] ** 2 * heads * DH,
    )[0]


def hidden_kernel(order, group, calls, place_ref, q_ref, gate_ref, gain_ref, kv_ref, *refs):
    terms, inners = refs[:group], refs[group : group + calls]
    hidden_ref, squares_ref = refs[group + calls :]
    heads = kv_ref.shape[0]
    share = heads // group
    size = q_ref.shape[0] // len(order)
    states = []
    for head in range(heads):
        state = kv_ref[head]
        for turn, term in enumerate(terms):
            value = term[head % share].astype(jnp.float32)
            if group > 1:
                covers = lax.rem(place_ref[1] - turn + group, group)
                value = jnp.where(covers == head // share, value, 0.0)
            state = state + value
        high = state.astype(jnp.bfloat16)
        low = (state - high.astype(jnp.float32)).astype(jnp.bfloat16)
        states.append(jnp.concatenate([high, low], axis=0))
    for position, block in enumerate(order):
        start = pl.multiple_of((place_ref[0] ^ block) * size, size)
        rows = pl.ds(start, size)
        placed = pl.ds(position * size, size)
        squares = jnp.zeros((size, DH), jnp.float32)
        for head in range(heads):
            columns = pl.ds(head * DH, DH)
            q_rows = q_ref[rows, columns]
            carried = jnp.dot(
                jnp.concatenate([q_rows, q_rows], axis=1),
                states[head],
                preferred_element_type=jnp.float32,
            )
            per_call = inners[0].shape[1] // DH
            inner = inners[head // per_call][rows, pl.ds(head % per_call * DH, DH)]
            attn = (carried + inner).astype(jnp.bfloat16).astype(jnp.float32)
            gate = 1.0 + jnp.tanh(gate_ref[rows, columns].astype(jnp.float32) * 0.5)
            gain = gain_ref[place_ref[0] * heads + head] * 0.5
            hidden_ref[placed, columns] = (attn * (gain * gate)).astype(jnp.bfloat16)
            squares = squares + attn * attn
        squares_ref[pl.ds(position, 1), :] = jnp.sum(jnp.transpose(squares), axis=0, keepdims=True)


def gated_hidden(queries, inners, kv_state, terms, gate_input, norm_gain, h, i, order):
    rows, width = queries.shape
    return local_call(
        functools.partial(hidden_kernel, order, len(terms), len(inners)),
        scalars(h, i),
        [queries, gate_input, norm_gain.reshape(-1, 1, DH), kv_state, *terms, *inners],
        [
            jax.ShapeDtypeStruct((rows, width), jnp.bfloat16),
            jax.ShapeDtypeStruct((len(order), rows // len(order)), jnp.float32),
        ],
        4 * rows * width * DH,
    )


def project_kernel(jobs, n_rows, choices, flag_ref, *refs):
    rows_refs = refs[:n_rows]
    weight_refs = refs[n_rows : n_rows + sum(choices)]
    sent_ref, kept_ref = refs[n_rows + sum(choices) :]
    half = sent_ref.shape[0]

    def products(index, weight_ref):
        for rows, weight, first in jobs:
            if weight == index:
                columns = pl.ds(first, weight_ref.shape[1])
                product = jnp.dot(
                    rows_refs[rows][...], weight_ref[...], preferred_element_type=jnp.float32
                )
                kept_ref[:, columns] = product[:half]
                sent_ref[:, columns] = product[half:].astype(jnp.bfloat16)

    first = 0
    for index, number in enumerate(choices):
        for k in range(number):
            one = functools.partial(products, index, weight_refs[first + k])
            if number == 1:
                one()
            else:
                pl.when(flag_ref[0] == k)(one)
        first += number


def project(jobs, rows_list, weights, flag):
    flat = [choice for weight in weights for choice in weight]
    choices = tuple(len(weight) for weight in weights)
    placed_jobs, total = [], 0
    for rows, weight in jobs:
        placed_jobs.append((rows, weight, total))
        total += weights[weight][0].shape[1]
    height, depth = rows_list[0].shape
    shape = (height // 2, total)
    return local_call(
        functools.partial(project_kernel, tuple(placed_jobs), len(rows_list), choices),
        flag,
        [*rows_list, *flat],
        [jax.ShapeDtypeStruct(shape, jnp.bfloat16), jax.ShapeDtypeStruct(shape, jnp.float32)],
        2 * height * depth * total,
    )


def fold_kernel(more, flag_ref, kept_ref, got_ref, *outs):
    if more:
        sent_ref, left_ref = outs
        half = left_ref.shape[0]
        left_ref[...] = kept_ref[:half] + got_ref[:half].astype(jnp.float32)
        sent_ref[...] = (kept_ref[half:] + got_ref[half:].astype(jnp.float32)).astype(jnp.bfloat16)
        return
    first = 0
    for out in outs:
        columns = pl.ds(first, out.shape[1])
        out[...] = (kept_ref[:, columns] + got_ref[:, columns].astype(jnp.float32)).astype(out.dtype)
        first += out.shape[1]


def fold(kept, got, widths=None):
    rows, width = kept.shape
    if widths is None:
        shape = (rows // 2, width)
        outs = [jax.ShapeDtypeStruct(shape, jnp.bfloat16), jax.ShapeDtypeStruct(shape, jnp.float32)]
    else:
        outs = [jax.ShapeDtypeStruct((rows, some), jnp.bfloat16) for some in widths]
    return local_call(functools.partial(fold_kernel, widths is None), scalars(0), [kept, got], outs)


def column(row):
    return jnp.transpose(jnp.broadcast_to(row, (row.shape[1], row.shape[1])))


def scaled_parts(widths, starts_ref, squares_ref, pieces, total_width):
    scale = lax.rsqrt(column(squares_ref[...]) / total_width + epsilon)
    where = 0
    for piece, own in zip(pieces, widths):
        first = 0
        for width in own:
            for at in range(0, width, DH):
                part = piece[:, pl.ds(first + at, DH)].astype(jnp.float32) * scale
                yield part, pl.multiple_of(starts_ref[where] + at, DH)
            first += width
            where += 1


def placed_kernel(widths, total_width, starts_ref, squares_ref, *refs):
    out_ref = refs[-1]
    for part, start in scaled_parts(widths, starts_ref, squares_ref, refs[:-1], total_width):
        out_ref[:, pl.ds(start, DH)] = part.astype(out_ref.dtype)


def added_kernel(widths, total_width, starts_ref, squares_ref, *refs):
    out_ref, buf, sem = refs[-3:]
    copies = []
    parts = scaled_parts(widths, starts_ref, squares_ref, refs[: len(widths)], total_width)
    for at, (part, start) in enumerate(parts):
        buf[at] = part.astype(out_ref.dtype)
        copies.append(pltpu.make_async_copy(buf.at[at], out_ref.at[:, pl.ds(start, DH)], sem.at[at]))
        copies[-1].start()
    for copy in copies:
        copy.wait()


def placed(filled, pieces, squares, shape, total_width):
    widths = tuple(tuple(own) for _, _, own in pieces)
    starts = scalars(*[start for _, own, _ in pieces for start in own])
    operands = [squares] + [piece for piece, _, _ in pieces]
    out_shape = jax.ShapeDtypeStruct(shape, jnp.bfloat16)
    columns = sum(sum(own) for own in widths)
    if filled is None:
        kernel = functools.partial(placed_kernel, widths, total_width)
        return local_call(kernel, starts, operands, [out_shape])[0]
    return pl.pallas_call(
        functools.partial(added_kernel, widths, total_width),
        in_specs=[pl.BlockSpec(memory_space=pltpu.SMEM)]
        + [pl.BlockSpec(memory_space=pltpu.VMEM)] * len(operands)
        + [pl.BlockSpec(memory_space=pl.ANY)],
        out_specs=pl.BlockSpec(memory_space=pl.ANY),
        out_shape=out_shape,
        scratch_shapes=[
            pltpu.VMEM((columns // DH, shape[0], DH), jnp.bfloat16),
            pltpu.SemaphoreType.DMA((columns // DH,)),
        ],
        input_output_aliases={len(operands) + 1: 0},
        compiler_params=pltpu.CompilerParams(vmem_limit_bytes=VMEM_BYTES),
        cost_estimate=pl.CostEstimate(
            flops=0, bytes_accessed=4 * shape[0] * columns, transcendentals=0
        ),
    )(starts, *operands, filled)


def shards(queries, key_input, value_input, gate_input, kv_state, norm_gain, out_weight):
    n_seq, n_head = lax.axis_size("seq"), lax.axis_size("head")
    inner = n_seq // LINE
    place, h = lax.axis_index("seq"), lax.axis_index("head")
    z, i = place // inner, place % inner
    tok_rows, local_width = queries.shape
    assert tok_rows == BLOCK
    heads = local_width // DH
    total_width = local_width * n_head
    width = out_weight.shape[1]
    cuts = 2 if width % (2 * DH) == 0 else 1
    cut = width // cuts

    def along(value, hops):
        return lax.ppermute(value, "seq", line_pairs(n_seq, hops))

    w_mid1 = along(out_weight, SWAP_MIDDLE)
    w_pair = along(out_weight, SWAP_OUTER)
    terms, stepped = state_prefix(key_input, value_input, n_seq, place, [w_mid1, w_pair])
    some = heads // 2
    inners = [
        causal_part(queries, key_input, value_input, 0, some),
        causal_part(queries, key_input, value_input, some, heads - some),
    ]

    w_end1 = along(hold(w_mid1, stepped), TO_ENDS)
    w_cuts = [cut_columns(w_pair, k * cut, cut) for k in range(cuts)]
    w_mid2 = [along(hold(w_cut, stepped), SWAP_MIDDLE) for w_cut in w_cuts]
    w_end2 = [along(w, TO_ENDS) for w in w_mid2]

    bits = n_head.bit_length() - 1
    order = [int(format(j, "b").zfill(bits)[::-1], 2) for j in range(n_head)] if bits else [0]
    hidden, squares = gated_hidden(
        queries, inners, kv_state, terms, gate_input, norm_gain, h, i, order
    )
    others = [lax.ppermute(hidden, "seq", turn_pairs(n_seq, turn)) for turn in range(1, inner)]

    out_rows = tok_rows // n_head
    half, bit = n_head // 2, 1
    while bit < n_head:
        squares = squares[:half] + lax.ppermute(squares[half:], "head", flip_pairs(n_head, bit))
        half //= 2
        bit *= 2

    is_end = (z == 0) | (z == LINE - 1)
    low = z < LINE // 2
    flag = scalars(is_end)

    rows_list = [hidden] + others

    owners = [z, z ^ 1, jnp.where(low, 2, 1), jnp.where(low, 3, 0)]
    blocks = {"own": [(out_weight,)], "pair": [(w_pair,)], "third": [(w_mid1, w_end1)]}
    blocks["last"] = list(zip(w_mid2, w_end2))
    places = {name: owners[k] for k, name in enumerate(blocks)}

    def summed(parts, pins, pin_end=None):
        weights, jobs, widths, starts = [], [], [], []
        for p, (turn, own) in enumerate(parts):
            member = (i + turn) % inner
            widths.append([])
            starts.append([])
            for name, first, last in own:
                for k in range(first, last):
                    weight = blocks[name][k]
                    known = [n for n, other in enumerate(weights) if other[0] is weight[0]]
                    if not known:
                        weights.append(weight)
                    jobs.append((p, known[0] if known else len(weights) - 1))
                    size = weight[0].shape[1]
                    widths[-1].append(size)
                    starts[-1].append((places[name] * inner + member) * width + k * size)
        sent, kept = project(jobs, [rows_list[turn] for turn, _ in parts], weights, hold(flag, *pins))
        first_sent, steps, bit = sent, [], 1
        while bit < n_head:
            steps.append(lax.ppermute(sent, "head", flip_pairs(n_head, bit)))
            bit *= 2
            if bit < n_head:
                sent, kept = fold(kept, steps[-1])
            else:
                got = steps[-1] if pin_end is None else hold(steps[-1], pin_end)
                kept = fold(kept, got, [sum(own) for own in widths])
        pieces = []
        for piece, (turn, _), own_starts, own_widths in zip(kept, parts, starts, widths):
            if turn:
                piece = lax.ppermute(piece, "seq", turn_pairs(n_seq, -turn))
            pieces.append((piece, own_starts, own_widths))
        return pieces, first_sent, steps

    turns = list(range(inner))
    shape = (out_rows, width * n_seq)
    in_kernel = cut % DH == 0 and out_rows == DH
    ahead = [("own", 0, 1), ("pair", 0, 1)]

    pieces, sent, steps_own = summed([(0, ahead + [("third", 0, 1)])], [w_end1, *w_mid2])
    pins = [sent, squares, w_end2[0]]
    for some in (ahead, [("third", 0, 1)]) if inner > 1 else ():
        more, sent, steps = summed([(turn, some) for turn in turns[1:]], pins)
        pieces += more
        pins = [sent]
    pins += steps_own
    filled = None
    for k in range(cuts):
        if k + 1 == cuts and in_kernel:
            filled = placed(None, pieces, squares, shape, total_width)
        last, sent, _ = summed([(turn, [("last", k, k + 1)]) for turn in turns], pins, filled)
        pins = [sent]
        if k + 1 < cuts:
            pieces += last
    if in_kernel:
        return placed(filled, last, squares, shape, total_width)
    scale = lax.rsqrt(squares.reshape(out_rows, 1) / total_width + epsilon)
    output = jnp.zeros(shape, jnp.bfloat16)
    for piece, starts, widths in pieces + last:
        piece = (piece.astype(jnp.float32) * scale).astype(jnp.bfloat16)
        first = 0
        for start, size in zip(starts, widths):
            output = lax.dynamic_update_slice_in_dim(output, piece[:, first : first + size], start, 1)
            first += size
    return output


def solution(mesh):
    in_specs = (
        P("seq", "head"),
        P("seq", "head"),
        P("seq", "head"),
        P("seq", "head"),
        P("head", None, None),
        P(),
        P("head", "seq"),
    )
    out_specs = P(("seq", "head"), None)
    return jax.shard_map(shards, mesh=mesh, in_specs=in_specs, out_specs=out_specs, check_vma=False)
```

```python
import functools

import jax
import jax.numpy as jnp
from jax import lax
from jax.experimental import pallas as pl
from jax.experimental.pallas import tpu as pltpu
from jax.sharding import PartitionSpec as P

DH = 128
BLOCK = 512
LINE = 4
VMEM_BYTES = 16 * 1024 * 1024


epsilon = 1e-05


def line_pairs(n_seq, hops):
    inner = n_seq // LINE
    return [(a * inner + i, b * inner + i) for a, b in hops for i in range(inner)]


def turn_pairs(n_seq, turn):
    inner = n_seq // LINE
    return [(a * inner + i, a * inner + (i + turn) % inner) for a in range(LINE) for i in range(inner)]


def flip_pairs(n_head, bit):
    return [(h, h ^ bit) for h in range(n_head)]


SWAP_OUTER = [(0, 1), (1, 0), (2, 3), (3, 2)]
SWAP_MIDDLE = [(1, 2), (2, 1)]
TO_ENDS = [(1, 0), (2, 3)]


def hold(value, *others):
    return lax.optimization_barrier((value, *others))[0]


def scalars(*values):
    return jnp.stack([jnp.asarray(value, jnp.int32) for value in values])


def local_call(kernel, places, operands, out_shapes, flops=0):
    held = sum(value.size * value.dtype.itemsize for value in [*operands, *out_shapes])
    return pl.pallas_call(
        kernel,
        in_specs=[pl.BlockSpec(memory_space=pltpu.SMEM)]
        + [pl.BlockSpec(memory_space=pltpu.VMEM)] * len(operands),
        out_specs=[pl.BlockSpec(memory_space=pltpu.VMEM)] * len(out_shapes),
        out_shape=out_shapes,
        compiler_params=pltpu.CompilerParams(vmem_limit_bytes=max(VMEM_BYTES, held + held // 2)),
        cost_estimate=pl.CostEstimate(flops=flops, bytes_accessed=held, transcendentals=0),
    )(places, *operands)


def combine_kernel(count, always, masks_ref, *refs):
    values, outs = refs[:count], refs[count:]
    for index in range(values[0].shape[0]):
        total = values[0][index].astype(jnp.float32)
        for value in values[1:always]:
            total = total + value[index].astype(jnp.float32)
        for position, out in enumerate(outs):
            own = total
            for k in range(always, count):
                mask = masks_ref[position * (count - always) + k - always]
                own = own + jnp.where(mask != 0, values[k][index].astype(jnp.float32), 0.0)
            out[index] = own.astype(out.dtype)


def combine(values, dtypes, sometimes=(), masks=None):
    operands = list(values) + list(sometimes)
    masks = scalars(0) if masks is None else scalars(*masks)
    return local_call(
        functools.partial(combine_kernel, len(operands), len(values)),
        masks,
        operands,
        [jax.ShapeDtypeStruct(values[0].shape, dtype) for dtype in dtypes],
    )


def states_kernel(part_ref, k_ref, v_ref, out_ref):
    heads = out_ref.shape[0]
    for index in range(heads):
        columns = pl.ds(pl.multiple_of((part_ref[0] * heads + index) * DH, DH), DH)
        out_ref[index] = lax.dot_general(
            k_ref[:, columns],
            v_ref[:, columns],
            (((0,), (0,)), ((), ())),
            preferred_element_type=jnp.float32,
        ).astype(out_ref.dtype)


def block_states(key_input, value_input, part, heads, dtype):
    return local_call(
        states_kernel,
        scalars(part),
        [key_input, value_input],
        [jax.ShapeDtypeStruct((heads, DH, DH), dtype)],
        2 * key_input.shape[0] * heads * DH * DH,
    )[0]


def state_prefix(key_input, value_input, n_seq, place, early):
    inner = n_seq // LINE
    i = place % inner
    heads = key_input.shape[1] // DH
    split = heads % inner == 0
    share = heads // inner if split else heads
    if split:
        sends = [
            block_states(key_input, value_input, (i + turn) % inner, share, jnp.bfloat16)
            for turn in range(1, inner)
        ]
        own = block_states(key_input, value_input, i, share, jnp.float32)
    else:
        own = block_states(key_input, value_input, 0, share, jnp.float32)
        sends = [own.astype(jnp.bfloat16)] * (inner - 1)
    values, members = [own], [i]
    for turn in range(1, inner):
        values.append(lax.ppermute(sends[turn - 1], "seq", turn_pairs(n_seq, turn)))
        members.append((i - turn) % inner)
    (first,) = combine(values, [jnp.bfloat16])
    from_left = lax.ppermute(first, "seq", line_pairs(n_seq, [(0, 1), (2, 3)]))
    from_left = hold(from_left, *early)
    (second,) = combine(values + [from_left], [jnp.bfloat16])
    near = lax.ppermute(second, "seq", line_pairs(n_seq, [(1, 2)]))
    far = lax.ppermute(second, "seq", line_pairs(n_seq, [(1, 3)]))
    targets = [i] + [(i + turn) % inner for turn in range(1, inner)] if split else [i]
    masks = [owner < target for target in targets for owner in members]
    dtypes = [jnp.float32] + [jnp.bfloat16] * (len(targets) - 1)
    befores = combine([from_left, near, far], dtypes, values, masks)
    terms = [befores[0]]
    for turn in range(1, len(targets)):
        terms.append(lax.ppermute(befores[turn], "seq", turn_pairs(n_seq, turn)))
    return terms, [near, far]


def causal_kernel(first_head, place_ref, q_ref, k_ref, v_ref, out_ref):
    rows = q_ref.shape[0]
    half = rows // 2
    top, bottom = pl.ds(0, half), pl.ds(half, half)
    keep = lax.broadcasted_iota(jnp.int32, (half, half), 0) >= lax.broadcasted_iota(
        jnp.int32, (half, half), 1
    )

    def scores(q_rows, k_rows, columns):
        return lax.dot_general(
            q_ref[q_rows, columns],
            k_ref[k_rows, columns],
            (((1,), (1,)), ((), ())),
            preferred_element_type=jnp.float32,
        )

    for index in range(out_ref.shape[1] // DH):
        columns = pl.ds((first_head + index) * DH, DH)
        placed = pl.ds(index * DH, DH)
        first = jnp.where(keep, scores(top, top, columns), 0.0).astype(jnp.bfloat16)
        below = scores(bottom, top, columns).astype(jnp.bfloat16)
        last = jnp.where(keep, scores(bottom, bottom, columns), 0.0).astype(jnp.bfloat16)
        out_ref[top, placed] = jnp.dot(first, v_ref[top, columns], preferred_element_type=jnp.float32)
        out_ref[bottom, placed] = jnp.dot(
            jnp.concatenate([below, last], axis=1),
            v_ref[:, columns],
            preferred_element_type=jnp.float32,
        )


def causal_part(queries, key_input, value_input, first_head, heads):
    return local_call(
        functools.partial(causal_kernel, first_head),
        scalars(0),
        [queries, key_input, value_input],
        [jax.ShapeDtypeStruct((queries.shape[0], heads * DH), jnp.float32)],
        3 * queries.shape[0] ** 2 * heads * DH,
    )[0]


def hidden_kernel(order, group, calls, place_ref, q_ref, gate_ref, gain_ref, kv_ref, *refs):
    terms, inners = refs[:group], refs[group : group + calls]
    hidden_ref, squares_ref = refs[group + calls :]
    heads = kv_ref.shape[0]
    share = heads // group
    size = q_ref.shape[0] // len(order)
    states = []
    for head in range(heads):
        state = kv_ref[head]
        for turn, term in enumerate(terms):
            value = term[head % share].astype(jnp.float32)
            if group > 1:
                covers = lax.rem(place_ref[1] - turn + group, group)
                value = jnp.where(covers == head // share, value, 0.0)
            state = state + value
        high = state.astype(jnp.bfloat16)
        low = (state - high.astype(jnp.float32)).astype(jnp.bfloat16)
        states.append(jnp.concatenate([high, low], axis=0))
    for position, block in enumerate(order):
        start = pl.multiple_of((place_ref[0] ^ block) * size, size)
        rows = pl.ds(start, size)
        placed = pl.ds(position * size, size)
        squares = jnp.zeros((size, DH), jnp.float32)
        for head in range(heads):
            columns = pl.ds(head * DH, DH)
            q_rows = q_ref[rows, columns]
            carried = jnp.dot(
                jnp.concatenate([q_rows, q_rows], axis=1),
                states[head],
                preferred_element_type=jnp.float32,
            )
            per_call = inners[0].shape[1] // DH
            inner = inners[head // per_call][rows, pl.ds(head % per_call * DH, DH)]
            attn = (carried + inner).astype(jnp.bfloat16).astype(jnp.float32)
            gate = 1.0 + jnp.tanh(gate_ref[rows, columns].astype(jnp.float32) * 0.5)
            gain = gain_ref[place_ref[0] * heads + head] * 0.5
            hidden_ref[placed, columns] = (attn * (gain * gate)).astype(jnp.bfloat16)
            squares = squares + attn * attn
        squares_ref[pl.ds(position, 1), :] = jnp.sum(jnp.transpose(squares), axis=0, keepdims=True)


def gated_hidden(queries, inners, kv_state, terms, gate_input, norm_gain, h, i, order):
    rows, width = queries.shape
    return local_call(
        functools.partial(hidden_kernel, order, len(terms), len(inners)),
        scalars(h, i),
        [queries, gate_input, norm_gain.reshape(-1, 1, DH), kv_state, *terms, *inners],
        [
            jax.ShapeDtypeStruct((rows, width), jnp.bfloat16),
            jax.ShapeDtypeStruct((len(order), rows // len(order)), jnp.float32),
        ],
        4 * rows * width * DH,
    )


def project_kernel(jobs, n_rows, choices, flag_ref, *refs):
    rows_refs = refs[:n_rows]
    weight_refs = refs[n_rows : n_rows + sum(choices)]
    sent_ref, kept_ref = refs[n_rows + sum(choices) :]
    half = sent_ref.shape[0]

    def products(index, weight_ref):
        for rows, weight, first in jobs:
            if weight == index:
                columns = pl.ds(first, weight_ref.shape[1])
                product = jnp.dot(
                    rows_refs[rows][...], weight_ref[...], preferred_element_type=jnp.float32
                )
                kept_ref[:, columns] = product[:half]
                sent_ref[:, columns] = product[half:].astype(jnp.bfloat16)

    first = 0
    for index, number in enumerate(choices):
        for k in range(number):
            one = functools.partial(products, index, weight_refs[first + k])
            if number == 1:
                one()
            else:
                pl.when(flag_ref[0] == k)(one)
        first += number


def project(jobs, rows_list, weights, flag):
    flat = [choice for weight in weights for choice in weight]
    choices = tuple(len(weight) for weight in weights)
    placed_jobs, total = [], 0
    for rows, weight in jobs:
        placed_jobs.append((rows, weight, total))
        total += weights[weight][0].shape[1]
    height, depth = rows_list[0].shape
    shape = (height // 2, total)
    return local_call(
        functools.partial(project_kernel, tuple(placed_jobs), len(rows_list), choices),
        flag,
        [*rows_list, *flat],
        [jax.ShapeDtypeStruct(shape, jnp.bfloat16), jax.ShapeDtypeStruct(shape, jnp.float32)],
        2 * height * depth * total,
    )


def fold_kernel(more, flag_ref, kept_ref, got_ref, *outs):
    if more:
        sent_ref, left_ref = outs
        half = left_ref.shape[0]
        left_ref[...] = kept_ref[:half] + got_ref[:half].astype(jnp.float32)
        sent_ref[...] = (kept_ref[half:] + got_ref[half:].astype(jnp.float32)).astype(jnp.bfloat16)
        return
    first = 0
    for out in outs:
        columns = pl.ds(first, out.shape[1])
        out[...] = (kept_ref[:, columns] + got_ref[:, columns].astype(jnp.float32)).astype(out.dtype)
        first += out.shape[1]


def fold(kept, got, widths=None):
    rows, width = kept.shape
    if widths is None:
        shape = (rows // 2, width)
        outs = [jax.ShapeDtypeStruct(shape, jnp.bfloat16), jax.ShapeDtypeStruct(shape, jnp.float32)]
    else:
        outs = [jax.ShapeDtypeStruct((rows, some), jnp.bfloat16) for some in widths]
    return local_call(functools.partial(fold_kernel, widths is None), scalars(0), [kept, got], outs)


def column(row):
    return jnp.transpose(jnp.broadcast_to(row, (row.shape[1], row.shape[1])))


def scaled_parts(counts, width, starts_ref, squares_ref, pieces, total_width):
    scale = lax.rsqrt(column(squares_ref[...]) / total_width + epsilon)
    where = 0
    for piece, count in zip(pieces, counts):
        for index in range(count):
            for at in range(0, width, DH):
                part = piece[:, pl.ds(index * width + at, DH)].astype(jnp.float32) * scale
                yield part, pl.multiple_of(starts_ref[where] + at, DH)
            where += 1


def placed_kernel(counts, width, total_width, starts_ref, squares_ref, *refs):
    out_ref = refs[-1]
    for part, start in scaled_parts(counts, width, starts_ref, squares_ref, refs[:-1], total_width):
        out_ref[:, pl.ds(start, DH)] = part.astype(out_ref.dtype)


def added_kernel(counts, width, total_width, starts_ref, squares_ref, *refs):
    out_ref, buf, sem = refs[-3:]
    copies = []
    parts = scaled_parts(counts, width, starts_ref, squares_ref, refs[: len(counts)], total_width)
    for at, (part, start) in enumerate(parts):
        buf[at] = part.astype(out_ref.dtype)
        copies.append(pltpu.make_async_copy(buf.at[at], out_ref.at[:, pl.ds(start, DH)], sem.at[at]))
        copies[-1].start()
    for copy in copies:
        copy.wait()


def placed(filled, pieces, squares, width, shape, total_width):
    counts = tuple(len(starts) for _, starts in pieces)
    starts = scalars(*[start for _, own in pieces for start in own])
    operands = [squares] + [piece for piece, _ in pieces]
    out_shape = jax.ShapeDtypeStruct(shape, jnp.bfloat16)
    columns = width * sum(counts)
    if filled is None:
        kernel = functools.partial(placed_kernel, counts, width, total_width)
        return local_call(kernel, starts, operands, [out_shape])[0]
    return pl.pallas_call(
        functools.partial(added_kernel, counts, width, total_width),
        in_specs=[pl.BlockSpec(memory_space=pltpu.SMEM)]
        + [pl.BlockSpec(memory_space=pltpu.VMEM)] * len(operands)
        + [pl.BlockSpec(memory_space=pl.ANY)],
        out_specs=pl.BlockSpec(memory_space=pl.ANY),
        out_shape=out_shape,
        scratch_shapes=[
            pltpu.VMEM((columns // DH, shape[0], DH), jnp.bfloat16),
            pltpu.SemaphoreType.DMA((columns // DH,)),
        ],
        input_output_aliases={len(operands) + 1: 0},
        compiler_params=pltpu.CompilerParams(vmem_limit_bytes=VMEM_BYTES),
        cost_estimate=pl.CostEstimate(
            flops=0, bytes_accessed=4 * shape[0] * columns, transcendentals=0
        ),
    )(starts, *operands, filled)


def shards(queries, key_input, value_input, gate_input, kv_state, norm_gain, out_weight):
    n_seq, n_head = lax.axis_size("seq"), lax.axis_size("head")
    inner = n_seq // LINE
    place, h = lax.axis_index("seq"), lax.axis_index("head")
    z, i = place // inner, place % inner
    tok_rows, local_width = queries.shape
    assert tok_rows == BLOCK
    heads = local_width // DH
    total_width = local_width * n_head
    width = out_weight.shape[1]

    def along(value, hops):
        return lax.ppermute(value, "seq", line_pairs(n_seq, hops))

    w_mid1 = along(out_weight, SWAP_MIDDLE)
    w_pair = along(out_weight, SWAP_OUTER)
    terms, stepped = state_prefix(key_input, value_input, n_seq, place, [w_mid1, w_pair])
    some = heads // 2
    inners = [
        causal_part(queries, key_input, value_input, 0, some),
        causal_part(queries, key_input, value_input, some, heads - some),
    ]

    w_end1 = along(hold(w_mid1, *stepped), TO_ENDS)
    w_mid2 = along(hold(w_pair, *stepped), SWAP_MIDDLE)
    w_end2 = along(w_mid2, TO_ENDS)

    bits = n_head.bit_length() - 1
    order = [int(format(j, "b").zfill(bits)[::-1], 2) for j in range(n_head)] if bits else [0]
    hidden, squares = gated_hidden(
        queries, inners, kv_state, terms, gate_input, norm_gain, h, i, order
    )
    others = [lax.ppermute(hidden, "seq", turn_pairs(n_seq, turn)) for turn in range(1, inner)]

    out_rows = tok_rows // n_head
    half, bit = n_head // 2, 1
    while bit < n_head:
        squares = squares[:half] + lax.ppermute(squares[half:], "head", flip_pairs(n_head, bit))
        half //= 2
        bit *= 2

    is_end = (z == 0) | (z == LINE - 1)
    low = z < LINE // 2
    flag = scalars(is_end)

    rows_list = [hidden] + others

    owners = [z, z ^ 1, jnp.where(low, 2, 1), jnp.where(low, 3, 0)]
    blocks = [(out_weight,), (w_pair,), (w_mid1, w_end1), (w_mid2, w_end2)]

    def summed(parts, pins, pin_end=None):
        weights = sorted({block for _, own in parts for block in own})
        jobs = [(p, weights.index(block)) for p, (_, own) in enumerate(parts) for block in own]
        sent, kept = project(
            jobs,
            [rows_list[turn] for turn, _ in parts],
            [blocks[block] for block in weights],
            hold(flag, *pins),
        )
        first_sent, bit = sent, 1
        while bit < n_head:
            got = lax.ppermute(sent, "head", flip_pairs(n_head, bit))
            bit *= 2
            if bit < n_head:
                sent, kept = fold(kept, got)
            else:
                got = got if pin_end is None else hold(got, pin_end)
                kept = fold(kept, got, [width * len(own) for _, own in parts])
        pieces = []
        for piece, (turn, own) in zip(kept, parts):
            if turn:
                piece = lax.ppermute(piece, "seq", turn_pairs(n_seq, -turn))
            starts = [(owners[block] * inner + (i + turn) % inner) * width for block in own]
            pieces.append((piece, starts))
        return pieces, first_sent, got

    turns = list(range(inner))
    shape = (out_rows, width * n_seq)
    in_kernel = width % DH == 0 and out_rows == DH

    pieces, pins, ends = [], [], []
    groups = [(turns[:1], [0, 1]), (turns[:1], [2]), (turns[1:], [0, 1]), (turns[1:], [2])]
    for members, some in groups:
        if members:
            more, sent, end = summed([(turn, some) for turn in members], pins)
            pieces += more
            ends.append(end)
            pins = [sent, squares, w_mid2]
    filled = placed(None, pieces, squares, width, shape, total_width) if in_kernel else None
    last, _, _ = summed([(turn, [3]) for turn in turns], [sent, *ends], filled)
    if in_kernel:
        return placed(filled, last, squares, width, shape, total_width)
    scale = lax.rsqrt(squares.reshape(out_rows, 1) / total_width + epsilon)
    output = jnp.zeros(shape, jnp.bfloat16)
    for piece, starts in pieces + last:
        piece = (piece.astype(jnp.float32) * scale).astype(jnp.bfloat16)
        for index, start in enumerate(starts):
            part = piece[:, index * width : (index + 1) * width]
            output = lax.dynamic_update_slice_in_dim(output, part, start, 1)
    return output


def solution(mesh):
    in_specs = (
        P("seq", "head"),
        P("seq", "head"),
        P("seq", "head"),
        P("seq", "head"),
        P("head", None, None),
        P(),
        P("head", "seq"),
    )
    out_specs = P(("seq", "head"), None)
    return jax.shard_map(shards, mesh=mesh, in_specs=in_specs, out_specs=out_specs, check_vma=False)
```

```python
import functools

import jax
import jax.numpy as jnp
from jax import lax
from jax.experimental import pallas as pl
from jax.experimental.pallas import tpu as pltpu
from jax.sharding import PartitionSpec as P

DH = 128
BLOCK = 512
LINE = 4
VMEM_BYTES = 16 * 1024 * 1024


epsilon = 1e-05


def line_pairs(n_seq, hops):
    inner = n_seq // LINE
    return [(a * inner + i, b * inner + i) for a, b in hops for i in range(inner)]


def turn_pairs(n_seq, turn):
    inner = n_seq // LINE
    return [(a * inner + i, a * inner + (i + turn) % inner) for a in range(LINE) for i in range(inner)]


def flip_pairs(n_head, bit):
    return [(h, h ^ bit) for h in range(n_head)]


SWAP_NEXT = [(z, z ^ 1) for z in range(LINE)]
SWAP_HALVES = [(z, z ^ 2) for z in range(LINE)]
SWAP_MIDDLE = [(1, 2), (2, 1)]
TO_ENDS = [(1, 0), (2, 3)]


def hold(value, *others):
    return lax.optimization_barrier((value, *others))[0]


def scalars(*values):
    return jnp.stack([jnp.asarray(value, jnp.int32) for value in values])


def local_call(kernel, places, operands, out_shapes, flops=0):
    held = sum(value.size * value.dtype.itemsize for value in [*operands, *out_shapes])
    return pl.pallas_call(
        kernel,
        in_specs=[pl.BlockSpec(memory_space=pltpu.SMEM)]
        + [pl.BlockSpec(memory_space=pltpu.VMEM)] * len(operands),
        out_specs=[pl.BlockSpec(memory_space=pltpu.VMEM)] * len(out_shapes),
        out_shape=out_shapes,
        compiler_params=pltpu.CompilerParams(vmem_limit_bytes=max(VMEM_BYTES, held + held // 2)),
        cost_estimate=pl.CostEstimate(flops=flops, bytes_accessed=held, transcendentals=0),
    )(places, *operands)


def combine_kernel(count, always, masks_ref, *refs):
    values, outs = refs[:count], refs[count:]
    for index in range(values[0].shape[0]):
        total = values[0][index].astype(jnp.float32)
        for value in values[1:always]:
            total = total + value[index].astype(jnp.float32)
        for position, out in enumerate(outs):
            own = total
            for k in range(always, count):
                mask = masks_ref[position * (count - always) + k - always]
                own = own + jnp.where(mask != 0, values[k][index].astype(jnp.float32), 0.0)
            out[index] = own.astype(out.dtype)


def combine(values, dtypes, sometimes=(), masks=None):
    operands = list(values) + list(sometimes)
    masks = scalars(0) if masks is None else scalars(*masks)
    return local_call(
        functools.partial(combine_kernel, len(operands), len(values)),
        masks,
        operands,
        [jax.ShapeDtypeStruct(values[0].shape, dtype) for dtype in dtypes],
    )


def states_kernel(part_ref, k_ref, v_ref, out_ref):
    heads = out_ref.shape[0]
    for index in range(heads):
        columns = pl.ds(pl.multiple_of((part_ref[0] * heads + index) * DH, DH), DH)
        out_ref[index] = lax.dot_general(
            k_ref[:, columns],
            v_ref[:, columns],
            (((0,), (0,)), ((), ())),
            preferred_element_type=jnp.float32,
        ).astype(out_ref.dtype)


def block_states(key_input, value_input, part, heads, dtype):
    return local_call(
        states_kernel,
        scalars(part),
        [key_input, value_input],
        [jax.ShapeDtypeStruct((heads, DH, DH), dtype)],
        2 * key_input.shape[0] * heads * DH * DH,
    )[0]


def state_prefix(key_input, value_input, n_seq, place):
    inner = n_seq // LINE
    i = place % inner
    heads = key_input.shape[1] // DH
    split = heads % inner == 0
    share = heads // inner if split else heads
    if split:
        sends = [
            block_states(key_input, value_input, (i + turn) % inner, share, jnp.bfloat16)
            for turn in range(1, inner)
        ]
        own = block_states(key_input, value_input, i, share, jnp.float32)
    else:
        own = block_states(key_input, value_input, 0, share, jnp.float32)
        sends = [own.astype(jnp.bfloat16)] * (inner - 1)
    values, members = [own], [i]
    for turn in range(1, inner):
        values.append(lax.ppermute(sends[turn - 1], "seq", turn_pairs(n_seq, turn)))
        members.append((i - turn) % inner)
    (first,) = combine(values, [jnp.bfloat16])
    from_left = lax.ppermute(first, "seq", line_pairs(n_seq, [(0, 1), (2, 3)]))
    (second,) = combine(values + [from_left], [jnp.bfloat16])
    near = lax.ppermute(second, "seq", line_pairs(n_seq, [(1, 2)]))
    far = lax.ppermute(second, "seq", line_pairs(n_seq, [(1, 3)]))
    targets = [i] + [(i + turn) % inner for turn in range(1, inner)] if split else [i]
    masks = [owner < target for target in targets for owner in members]
    dtypes = [jnp.float32] + [jnp.bfloat16] * (len(targets) - 1)
    befores = combine([from_left, near, far], dtypes, values, masks)
    terms = [befores[0]]
    for turn in range(1, len(targets)):
        terms.append(lax.ppermute(befores[turn], "seq", turn_pairs(n_seq, turn)))
    return terms, [near, far]


def causal_kernel(first_head, place_ref, q_ref, k_ref, v_ref, out_ref):
    rows = q_ref.shape[0]
    half = rows // 2
    top, bottom = pl.ds(0, half), pl.ds(half, half)
    keep = lax.broadcasted_iota(jnp.int32, (half, half), 0) >= lax.broadcasted_iota(
        jnp.int32, (half, half), 1
    )

    def scores(q_rows, k_rows, columns):
        return lax.dot_general(
            q_ref[q_rows, columns],
            k_ref[k_rows, columns],
            (((1,), (1,)), ((), ())),
            preferred_element_type=jnp.float32,
        )

    for index in range(out_ref.shape[1] // DH):
        columns = pl.ds((first_head + index) * DH, DH)
        placed = pl.ds(index * DH, DH)
        first = jnp.where(keep, scores(top, top, columns), 0.0).astype(jnp.bfloat16)
        below = scores(bottom, top, columns).astype(jnp.bfloat16)
        last = jnp.where(keep, scores(bottom, bottom, columns), 0.0).astype(jnp.bfloat16)
        out_ref[top, placed] = jnp.dot(first, v_ref[top, columns], preferred_element_type=jnp.float32)
        out_ref[bottom, placed] = jnp.dot(
            jnp.concatenate([below, last], axis=1),
            v_ref[:, columns],
            preferred_element_type=jnp.float32,
        )


def causal_part(queries, key_input, value_input, first_head, heads):
    return local_call(
        functools.partial(causal_kernel, first_head),
        scalars(0),
        [queries, key_input, value_input],
        [jax.ShapeDtypeStruct((queries.shape[0], heads * DH), jnp.float32)],
        3 * queries.shape[0] ** 2 * heads * DH,
    )[0]


def hidden_kernel(order, group, calls, place_ref, q_ref, gate_ref, gain_ref, kv_ref, *refs):
    terms, inners = refs[:group], refs[group : group + calls]
    hidden_ref, squares_ref = refs[group + calls :]
    heads = kv_ref.shape[0]
    share = heads // group
    size = q_ref.shape[0] // len(order)
    states = []
    for head in range(heads):
        state = kv_ref[head]
        for turn, term in enumerate(terms):
            value = term[head % share].astype(jnp.float32)
            if group > 1:
                covers = lax.rem(place_ref[1] - turn + group, group)
                value = jnp.where(covers == head // share, value, 0.0)
            state = state + value
        high = state.astype(jnp.bfloat16)
        low = (state - high.astype(jnp.float32)).astype(jnp.bfloat16)
        states.append(jnp.concatenate([high, low], axis=0))
    for position, block in enumerate(order):
        start = pl.multiple_of((place_ref[0] ^ block) * size, size)
        rows = pl.ds(start, size)
        placed = pl.ds(position * size, size)
        squares = jnp.zeros((size, DH), jnp.float32)
        for head in range(heads):
            columns = pl.ds(head * DH, DH)
            q_rows = q_ref[rows, columns]
            carried = jnp.dot(
                jnp.concatenate([q_rows, q_rows], axis=1),
                states[head],
                preferred_element_type=jnp.float32,
            )
            per_call = inners[0].shape[1] // DH
            inner = inners[head // per_call][rows, pl.ds(head % per_call * DH, DH)]
            attn = (carried + inner).astype(jnp.bfloat16).astype(jnp.float32)
            gate = 1.0 + jnp.tanh(gate_ref[rows, columns].astype(jnp.float32) * 0.5)
            gain = gain_ref[place_ref[0] * heads + head] * 0.5
            hidden_ref[placed, columns] = (attn * (gain * gate)).astype(jnp.bfloat16)
            squares = squares + attn * attn
        squares_ref[pl.ds(position, 1), :] = jnp.sum(jnp.transpose(squares), axis=0, keepdims=True)


def gated_hidden(queries, inners, kv_state, terms, gate_input, norm_gain, h, i, order):
    rows, width = queries.shape
    return local_call(
        functools.partial(hidden_kernel, order, len(terms), len(inners)),
        scalars(h, i),
        [queries, gate_input, norm_gain.reshape(-1, 1, DH), kv_state, *terms, *inners],
        [
            jax.ShapeDtypeStruct((rows, width), jnp.bfloat16),
            jax.ShapeDtypeStruct((len(order), rows // len(order)), jnp.float32),
        ],
        4 * rows * width * DH,
    )


def project_kernel(jobs, n_rows, choices, flag_ref, *refs):
    rows_refs = refs[:n_rows]
    weight_refs = refs[n_rows : n_rows + sum(choices)]
    sent_ref, kept_ref = refs[n_rows + sum(choices) :]
    half = sent_ref.shape[0]

    def products(index, weight_ref):
        for rows, weight, first in jobs:
            if weight == index:
                columns = pl.ds(first, weight_ref.shape[1])
                product = jnp.dot(
                    rows_refs[rows][...], weight_ref[...], preferred_element_type=jnp.float32
                )
                kept_ref[:, columns] = product[:half]
                sent_ref[:, columns] = product[half:].astype(jnp.bfloat16)

    first = 0
    for index, number in enumerate(choices):
        for k in range(number):
            one = functools.partial(products, index, weight_refs[first + k])
            if number == 1:
                one()
            else:
                pl.when(flag_ref[0] == k)(one)
        first += number


def project(jobs, rows_list, weights, flag):
    flat = [choice for weight in weights for choice in weight]
    choices = tuple(len(weight) for weight in weights)
    placed_jobs, total = [], 0
    for rows, weight in jobs:
        placed_jobs.append((rows, weight, total))
        total += weights[weight][0].shape[1]
    height, depth = rows_list[0].shape
    shape = (height // 2, total)
    return local_call(
        functools.partial(project_kernel, tuple(placed_jobs), len(rows_list), choices),
        flag,
        [*rows_list, *flat],
        [jax.ShapeDtypeStruct(shape, jnp.bfloat16), jax.ShapeDtypeStruct(shape, jnp.float32)],
        2 * height * depth * total,
    )


def fold_kernel(more, flag_ref, kept_ref, got_ref, *outs):
    if more:
        sent_ref, left_ref = outs
        half = left_ref.shape[0]
        left_ref[...] = kept_ref[:half] + got_ref[:half].astype(jnp.float32)
        sent_ref[...] = (kept_ref[half:] + got_ref[half:].astype(jnp.float32)).astype(jnp.bfloat16)
        return
    first = 0
    for out in outs:
        columns = pl.ds(first, out.shape[1])
        out[...] = (kept_ref[:, columns] + got_ref[:, columns].astype(jnp.float32)).astype(out.dtype)
        first += out.shape[1]


def fold(kept, got, widths=None):
    rows, width = kept.shape
    if widths is None:
        shape = (rows // 2, width)
        outs = [jax.ShapeDtypeStruct(shape, jnp.bfloat16), jax.ShapeDtypeStruct(shape, jnp.float32)]
    else:
        outs = [jax.ShapeDtypeStruct((rows, some), jnp.bfloat16) for some in widths]
    return local_call(functools.partial(fold_kernel, widths is None), scalars(0), [kept, got], outs)


def column(row):
    return jnp.transpose(jnp.broadcast_to(row, (row.shape[1], row.shape[1])))


def scaled_parts(counts, width, starts_ref, squares_ref, pieces, total_width):
    scale = lax.rsqrt(column(squares_ref[...]) / total_width + epsilon)
    where = 0
    for piece, count in zip(pieces, counts):
        for index in range(count):
            for at in range(0, width, DH):
                part = piece[:, pl.ds(index * width + at, DH)].astype(jnp.float32) * scale
                yield part, pl.multiple_of(starts_ref[where] + at, DH)
            where += 1


def placed_kernel(counts, width, total_width, starts_ref, squares_ref, *refs):
    out_ref = refs[-1]
    for part, start in scaled_parts(counts, width, starts_ref, squares_ref, refs[:-1], total_width):
        out_ref[:, pl.ds(start, DH)] = part.astype(out_ref.dtype)


def added_kernel(counts, width, total_width, starts_ref, squares_ref, *refs):
    out_ref, buf, sem = refs[-3:]
    copies = []
    parts = scaled_parts(counts, width, starts_ref, squares_ref, refs[: len(counts)], total_width)
    for at, (part, start) in enumerate(parts):
        buf[at] = part.astype(out_ref.dtype)
        copies.append(pltpu.make_async_copy(buf.at[at], out_ref.at[:, pl.ds(start, DH)], sem.at[at]))
        copies[-1].start()
    for copy in copies:
        copy.wait()


def placed(filled, pieces, squares, width, shape, total_width):
    counts = tuple(len(starts) for _, starts in pieces)
    starts = scalars(*[start for _, own in pieces for start in own])
    operands = [squares] + [piece for piece, _ in pieces]
    out_shape = jax.ShapeDtypeStruct(shape, jnp.bfloat16)
    columns = width * sum(counts)
    if filled is None:
        kernel = functools.partial(placed_kernel, counts, width, total_width)
        return local_call(kernel, starts, operands, [out_shape])[0]
    return pl.pallas_call(
        functools.partial(added_kernel, counts, width, total_width),
        in_specs=[pl.BlockSpec(memory_space=pltpu.SMEM)]
        + [pl.BlockSpec(memory_space=pltpu.VMEM)] * len(operands)
        + [pl.BlockSpec(memory_space=pl.ANY)],
        out_specs=pl.BlockSpec(memory_space=pl.ANY),
        out_shape=out_shape,
        scratch_shapes=[
            pltpu.VMEM((columns // DH, shape[0], DH), jnp.bfloat16),
            pltpu.SemaphoreType.DMA((columns // DH,)),
        ],
        input_output_aliases={len(operands) + 1: 0},
        compiler_params=pltpu.CompilerParams(vmem_limit_bytes=VMEM_BYTES),
        cost_estimate=pl.CostEstimate(
            flops=0, bytes_accessed=4 * shape[0] * columns, transcendentals=0
        ),
    )(starts, *operands, filled)


def shards(queries, key_input, value_input, gate_input, kv_state, norm_gain, out_weight):
    n_seq, n_head = lax.axis_size("seq"), lax.axis_size("head")
    inner = n_seq // LINE
    place, h = lax.axis_index("seq"), lax.axis_index("head")
    z, i = place // inner, place % inner
    tok_rows, local_width = queries.shape
    assert tok_rows == BLOCK
    heads = local_width // DH
    total_width = local_width * n_head
    width = out_weight.shape[1]

    def along(value, hops):
        return lax.ppermute(value, "seq", line_pairs(n_seq, hops))

    terms, stepped = state_prefix(key_input, value_input, n_seq, place)
    some = heads // 2
    inners = [
        causal_part(queries, key_input, value_input, 0, some),
        causal_part(queries, key_input, value_input, some, heads - some),
    ]

    own_columns = hold(out_weight, *stepped)
    w_halves = along(own_columns, SWAP_HALVES)
    w_next = along(own_columns, SWAP_NEXT)
    w_middle = along(own_columns, SWAP_MIDDLE)

    bits = n_head.bit_length() - 1
    order = [int(format(j, "b").zfill(bits)[::-1], 2) for j in range(n_head)] if bits else [0]
    hidden, squares = gated_hidden(
        queries, inners, kv_state, terms, gate_input, norm_gain, h, i, order
    )
    others = [lax.ppermute(hidden, "seq", turn_pairs(n_seq, turn)) for turn in range(1, inner)]

    out_rows = tok_rows // n_head
    half, bit = n_head // 2, 1
    while bit < n_head:
        squares = squares[:half] + lax.ppermute(squares[half:], "head", flip_pairs(n_head, bit))
        half //= 2
        bit *= 2

    is_end = (z == 0) | (z == LINE - 1)
    flag = scalars(is_end)

    rows_list = [hidden] + others

    owners = [z ^ block for block in range(LINE)]
    blocks = [(out_weight,), (w_next,), (w_halves,)]

    def summed(parts, pins, pin_end=None):
        weights = sorted({block for _, own in parts for block in own})
        jobs = [(p, weights.index(block)) for p, (_, own) in enumerate(parts) for block in own]
        sent, kept = project(
            jobs,
            [rows_list[turn] for turn, _ in parts],
            [blocks[block] for block in weights],
            hold(flag, *pins),
        )
        first_sent, bit = sent, 1
        while bit < n_head:
            got = lax.ppermute(sent, "head", flip_pairs(n_head, bit))
            bit *= 2
            if bit < n_head:
                sent, kept = fold(kept, got)
            else:
                got = got if pin_end is None else hold(got, pin_end)
                kept = fold(kept, got, [width * len(own) for _, own in parts])
        pieces = []
        for piece, (turn, own) in zip(kept, parts):
            if turn:
                piece = lax.ppermute(piece, "seq", turn_pairs(n_seq, -turn))
            starts = [(owners[block] * inner + (i + turn) % inner) * width for block in own]
            pieces.append((piece, starts))
        return pieces, first_sent, got

    turns = list(range(inner))
    shape = (out_rows, width * n_seq)
    in_kernel = width % DH == 0 and out_rows == DH

    pieces, pins, ends = [], [], []

    def group(members, some):
        if members:
            more, sent, end = summed([(turn, some) for turn in members], pins)
            pieces.extend(more)
            ends.append(end)
            pins[:] = [sent, squares]

    group(turns[:1], [0])
    group(turns[1:], [0])
    w_ends = along(hold(w_halves, *ends), TO_ENDS)
    blocks.append((w_middle, w_ends))
    group(turns[:1], [1, 2])
    group(turns[1:], [1, 2])
    filled = placed(None, pieces, squares, width, shape, total_width) if in_kernel else None
    last, _, _ = summed([(turn, [3]) for turn in turns], [*pins, *ends], filled)
    if in_kernel:
        return placed(filled, last, squares, width, shape, total_width)
    scale = lax.rsqrt(squares.reshape(out_rows, 1) / total_width + epsilon)
    output = jnp.zeros(shape, jnp.bfloat16)
    for piece, starts in pieces + last:
        piece = (piece.astype(jnp.float32) * scale).astype(jnp.bfloat16)
        for index, start in enumerate(starts):
            part = piece[:, index * width : (index + 1) * width]
            output = lax.dynamic_update_slice_in_dim(output, part, start, 1)
    return output


def solution(mesh):
    in_specs = (
        P("seq", "head"),
        P("seq", "head"),
        P("seq", "head"),
        P("seq", "head"),
        P("head", None, None),
        P(),
        P("head", "seq"),
    )
    out_specs = P(("seq", "head"), None)
    return jax.shard_map(shards, mesh=mesh, in_specs=in_specs, out_specs=out_specs, check_vma=False)
```

```python
import functools

import jax
import jax.numpy as jnp
from jax import lax
from jax.experimental import pallas as pl
from jax.experimental.pallas import tpu as pltpu
from jax.sharding import PartitionSpec as P

DH = 128
BLOCK = 512
LINE = 4
VMEM_BYTES = 16 * 1024 * 1024


epsilon = 1e-05


def line_pairs(n_seq, hops):
    inner = n_seq // LINE
    return [(a * inner + i, b * inner + i) for a, b in hops for i in range(inner)]


def turn_pairs(n_seq, turn):
    inner = n_seq // LINE
    return [(a * inner + i, a * inner + (i + turn) % inner) for a in range(LINE) for i in range(inner)]


def flip_pairs(n_head, bit):
    return [(h, h ^ bit) for h in range(n_head)]


SWAP_NEXT = [(z, z ^ 1) for z in range(LINE)]
SWAP_HALVES = [(z, z ^ 2) for z in range(LINE)]
SWAP_MIDDLE = [(1, 2), (2, 1)]
TO_ENDS = [(1, 0), (2, 3)]


def hold(value, *others):
    return lax.optimization_barrier((value, *others))[0]


def scalars(*values):
    return jnp.stack([jnp.asarray(value, jnp.int32) for value in values])


def local_call(kernel, places, operands, out_shapes, flops=0):
    held = sum(value.size * value.dtype.itemsize for value in [*operands, *out_shapes])
    return pl.pallas_call(
        kernel,
        in_specs=[pl.BlockSpec(memory_space=pltpu.SMEM)]
        + [pl.BlockSpec(memory_space=pltpu.VMEM)] * len(operands),
        out_specs=[pl.BlockSpec(memory_space=pltpu.VMEM)] * len(out_shapes),
        out_shape=out_shapes,
        compiler_params=pltpu.CompilerParams(vmem_limit_bytes=max(VMEM_BYTES, held + held // 2)),
        cost_estimate=pl.CostEstimate(flops=flops, bytes_accessed=held, transcendentals=0),
    )(places, *operands)


def combine_kernel(count, always, masks_ref, *refs):
    values, outs = refs[:count], refs[count:]
    for index in range(values[0].shape[0]):
        total = values[0][index].astype(jnp.float32)
        for value in values[1:always]:
            total = total + value[index].astype(jnp.float32)
        for position, out in enumerate(outs):
            own = total
            for k in range(always, count):
                mask = masks_ref[position * (count - always) + k - always]
                own = own + jnp.where(mask != 0, values[k][index].astype(jnp.float32), 0.0)
            out[index] = own.astype(out.dtype)


def combine(values, dtypes, sometimes=(), masks=None):
    operands = list(values) + list(sometimes)
    masks = scalars(0) if masks is None else scalars(*masks)
    return local_call(
        functools.partial(combine_kernel, len(operands), len(values)),
        masks,
        operands,
        [jax.ShapeDtypeStruct(values[0].shape, dtype) for dtype in dtypes],
    )


def states_kernel(part_ref, k_ref, v_ref, out_ref):
    heads = out_ref.shape[0]
    for index in range(heads):
        columns = pl.ds(pl.multiple_of((part_ref[0] * heads + index) * DH, DH), DH)
        out_ref[index] = lax.dot_general(
            k_ref[:, columns],
            v_ref[:, columns],
            (((0,), (0,)), ((), ())),
            preferred_element_type=jnp.float32,
        ).astype(out_ref.dtype)


def block_states(key_input, value_input, part, heads, dtype):
    return local_call(
        states_kernel,
        scalars(part),
        [key_input, value_input],
        [jax.ShapeDtypeStruct((heads, DH, DH), dtype)],
        2 * key_input.shape[0] * heads * DH * DH,
    )[0]


def state_prefix(key_input, value_input, n_seq, place):
    inner = n_seq // LINE
    i = place % inner
    heads = key_input.shape[1] // DH
    split = heads % inner == 0
    share = heads // inner if split else heads
    if split:
        sends = [
            block_states(key_input, value_input, (i + turn) % inner, share, jnp.bfloat16)
            for turn in range(1, inner)
        ]
        own = block_states(key_input, value_input, i, share, jnp.float32)
    else:
        own = block_states(key_input, value_input, 0, share, jnp.float32)
        sends = [own.astype(jnp.bfloat16)] * (inner - 1)
    values, members = [own], [i]
    for turn in range(1, inner):
        values.append(lax.ppermute(sends[turn - 1], "seq", turn_pairs(n_seq, turn)))
        members.append((i - turn) % inner)
    (first,) = combine(values, [jnp.bfloat16])
    from_left = lax.ppermute(first, "seq", line_pairs(n_seq, [(0, 1), (2, 3)]))
    (second,) = combine(values + [from_left], [jnp.bfloat16])
    near = lax.ppermute(second, "seq", line_pairs(n_seq, [(1, 2)]))
    far = lax.ppermute(second, "seq", line_pairs(n_seq, [(1, 3)]))
    targets = [i] + [(i + turn) % inner for turn in range(1, inner)] if split else [i]
    masks = [owner < target for target in targets for owner in members]
    dtypes = [jnp.float32] + [jnp.bfloat16] * (len(targets) - 1)
    befores = combine([from_left, near, far], dtypes, values, masks)
    terms = [befores[0]]
    for turn in range(1, len(targets)):
        terms.append(lax.ppermute(befores[turn], "seq", turn_pairs(n_seq, turn)))
    return terms, [near, far]


def causal_kernel(first_head, place_ref, q_ref, k_ref, v_ref, out_ref):
    rows = q_ref.shape[0]
    half = rows // 2
    top, bottom = pl.ds(0, half), pl.ds(half, half)
    keep = lax.broadcasted_iota(jnp.int32, (half, half), 0) >= lax.broadcasted_iota(
        jnp.int32, (half, half), 1
    )

    def scores(q_rows, k_rows, columns):
        return lax.dot_general(
            q_ref[q_rows, columns],
            k_ref[k_rows, columns],
            (((1,), (1,)), ((), ())),
            preferred_element_type=jnp.float32,
        )

    for index in range(out_ref.shape[1] // DH):
        columns = pl.ds((first_head + index) * DH, DH)
        placed = pl.ds(index * DH, DH)
        first = jnp.where(keep, scores(top, top, columns), 0.0).astype(jnp.bfloat16)
        below = scores(bottom, top, columns).astype(jnp.bfloat16)
        last = jnp.where(keep, scores(bottom, bottom, columns), 0.0).astype(jnp.bfloat16)
        out_ref[top, placed] = jnp.dot(first, v_ref[top, columns], preferred_element_type=jnp.float32)
        out_ref[bottom, placed] = jnp.dot(
            jnp.concatenate([below, last], axis=1),
            v_ref[:, columns],
            preferred_element_type=jnp.float32,
        )


def causal_part(queries, key_input, value_input, first_head, heads):
    return local_call(
        functools.partial(causal_kernel, first_head),
        scalars(0),
        [queries, key_input, value_input],
        [jax.ShapeDtypeStruct((queries.shape[0], heads * DH), jnp.float32)],
        3 * queries.shape[0] ** 2 * heads * DH,
    )[0]


def hidden_kernel(order, group, calls, place_ref, q_ref, gate_ref, gain_ref, kv_ref, *refs):
    terms, inners = refs[:group], refs[group : group + calls]
    hidden_ref, squares_ref = refs[group + calls :]
    heads = kv_ref.shape[0]
    share = heads // group
    size = q_ref.shape[0] // len(order)
    states = []
    for head in range(heads):
        state = kv_ref[head]
        for turn, term in enumerate(terms):
            value = term[head % share].astype(jnp.float32)
            if group > 1:
                covers = lax.rem(place_ref[1] - turn + group, group)
                value = jnp.where(covers == head // share, value, 0.0)
            state = state + value
        high = state.astype(jnp.bfloat16)
        low = (state - high.astype(jnp.float32)).astype(jnp.bfloat16)
        states.append(jnp.concatenate([high, low], axis=0))
    for position, block in enumerate(order):
        start = pl.multiple_of((place_ref[0] ^ block) * size, size)
        rows = pl.ds(start, size)
        placed = pl.ds(position * size, size)
        squares = jnp.zeros((size, DH), jnp.float32)
        for head in range(heads):
            columns = pl.ds(head * DH, DH)
            q_rows = q_ref[rows, columns]
            carried = jnp.dot(
                jnp.concatenate([q_rows, q_rows], axis=1),
                states[head],
                preferred_element_type=jnp.float32,
            )
            per_call = inners[0].shape[1] // DH
            inner = inners[head // per_call][rows, pl.ds(head % per_call * DH, DH)]
            attn = (carried + inner).astype(jnp.bfloat16).astype(jnp.float32)
            gate = 1.0 + jnp.tanh(gate_ref[rows, columns].astype(jnp.float32) * 0.5)
            gain = gain_ref[place_ref[0] * heads + head] * 0.5
            hidden_ref[placed, columns] = (attn * (gain * gate)).astype(jnp.bfloat16)
            squares = squares + attn * attn
        squares_ref[pl.ds(position, 1), :] = jnp.sum(jnp.transpose(squares), axis=0, keepdims=True)


def gated_hidden(queries, inners, kv_state, terms, gate_input, norm_gain, h, i, order):
    rows, width = queries.shape
    return local_call(
        functools.partial(hidden_kernel, order, len(terms), len(inners)),
        scalars(h, i),
        [queries, gate_input, norm_gain.reshape(-1, 1, DH), kv_state, *terms, *inners],
        [
            jax.ShapeDtypeStruct((rows, width), jnp.bfloat16),
            jax.ShapeDtypeStruct((len(order), rows // len(order)), jnp.float32),
        ],
        4 * rows * width * DH,
    )


def project_kernel(jobs, n_rows, choices, flag_ref, *refs):
    rows_refs = refs[:n_rows]
    weight_refs = refs[n_rows : n_rows + sum(choices)]
    sent_ref, kept_ref = refs[n_rows + sum(choices) :]
    half = sent_ref.shape[0]

    def products(index, weight_ref):
        for rows, weight, first in jobs:
            if weight == index:
                columns = pl.ds(first, weight_ref.shape[1])
                product = jnp.dot(
                    rows_refs[rows][...], weight_ref[...], preferred_element_type=jnp.float32
                )
                kept_ref[:, columns] = product[:half]
                sent_ref[:, columns] = product[half:].astype(jnp.bfloat16)

    first = 0
    for index, number in enumerate(choices):
        for k in range(number):
            one = functools.partial(products, index, weight_refs[first + k])
            if number == 1:
                one()
            else:
                pl.when(flag_ref[0] == k)(one)
        first += number


def project(jobs, rows_list, weights, flag):
    flat = [choice for weight in weights for choice in weight]
    choices = tuple(len(weight) for weight in weights)
    placed_jobs, total = [], 0
    for rows, weight in jobs:
        placed_jobs.append((rows, weight, total))
        total += weights[weight][0].shape[1]
    height, depth = rows_list[0].shape
    shape = (height // 2, total)
    return local_call(
        functools.partial(project_kernel, tuple(placed_jobs), len(rows_list), choices),
        flag,
        [*rows_list, *flat],
        [jax.ShapeDtypeStruct(shape, jnp.bfloat16), jax.ShapeDtypeStruct(shape, jnp.float32)],
        2 * height * depth * total,
    )


def fold_kernel(more, flag_ref, kept_ref, got_ref, *outs):
    if more:
        sent_ref, left_ref = outs
        half = left_ref.shape[0]
        left_ref[...] = kept_ref[:half] + got_ref[:half].astype(jnp.float32)
        sent_ref[...] = (kept_ref[half:] + got_ref[half:].astype(jnp.float32)).astype(jnp.bfloat16)
        return
    first = 0
    for out in outs:
        columns = pl.ds(first, out.shape[1])
        out[...] = (kept_ref[:, columns] + got_ref[:, columns].astype(jnp.float32)).astype(out.dtype)
        first += out.shape[1]


def fold(kept, got, widths=None):
    rows, width = kept.shape
    if widths is None:
        shape = (rows // 2, width)
        outs = [jax.ShapeDtypeStruct(shape, jnp.bfloat16), jax.ShapeDtypeStruct(shape, jnp.float32)]
    else:
        outs = [jax.ShapeDtypeStruct((rows, some), jnp.bfloat16) for some in widths]
    return local_call(functools.partial(fold_kernel, widths is None), scalars(0), [kept, got], outs)


def column(row):
    return jnp.transpose(jnp.broadcast_to(row, (row.shape[1], row.shape[1])))


def scaled_parts(counts, width, starts_ref, squares_ref, pieces, total_width):
    scale = lax.rsqrt(column(squares_ref[...]) / total_width + epsilon)
    where = 0
    for piece, count in zip(pieces, counts):
        for index in range(count):
            for at in range(0, width, DH):
                part = piece[:, pl.ds(index * width + at, DH)].astype(jnp.float32) * scale
                yield part, pl.multiple_of(starts_ref[where] + at, DH)
            where += 1


def placed_kernel(counts, width, total_width, starts_ref, squares_ref, *refs):
    out_ref = refs[-1]
    for part, start in scaled_parts(counts, width, starts_ref, squares_ref, refs[:-1], total_width):
        out_ref[:, pl.ds(start, DH)] = part.astype(out_ref.dtype)


def added_kernel(counts, width, total_width, starts_ref, squares_ref, *refs):
    out_ref, buf, sem = refs[-3:]
    copies = []
    parts = scaled_parts(counts, width, starts_ref, squares_ref, refs[: len(counts)], total_width)
    for at, (part, start) in enumerate(parts):
        buf[at] = part.astype(out_ref.dtype)
        copies.append(pltpu.make_async_copy(buf.at[at], out_ref.at[:, pl.ds(start, DH)], sem.at[at]))
        copies[-1].start()
    for copy in copies:
        copy.wait()


def placed(filled, pieces, squares, width, shape, total_width):
    counts = tuple(len(starts) for _, starts in pieces)
    starts = scalars(*[start for _, own in pieces for start in own])
    operands = [squares] + [piece for piece, _ in pieces]
    out_shape = jax.ShapeDtypeStruct(shape, jnp.bfloat16)
    columns = width * sum(counts)
    if filled is None:
        kernel = functools.partial(placed_kernel, counts, width, total_width)
        return local_call(kernel, starts, operands, [out_shape])[0]
    return pl.pallas_call(
        functools.partial(added_kernel, counts, width, total_width),
        in_specs=[pl.BlockSpec(memory_space=pltpu.SMEM)]
        + [pl.BlockSpec(memory_space=pltpu.VMEM)] * len(operands)
        + [pl.BlockSpec(memory_space=pl.ANY)],
        out_specs=pl.BlockSpec(memory_space=pl.ANY),
        out_shape=out_shape,
        scratch_shapes=[
            pltpu.VMEM((columns // DH, shape[0], DH), jnp.bfloat16),
            pltpu.SemaphoreType.DMA((columns // DH,)),
        ],
        input_output_aliases={len(operands) + 1: 0},
        compiler_params=pltpu.CompilerParams(vmem_limit_bytes=VMEM_BYTES),
        cost_estimate=pl.CostEstimate(
            flops=0, bytes_accessed=4 * shape[0] * columns, transcendentals=0
        ),
    )(starts, *operands, filled)


def shards(queries, key_input, value_input, gate_input, kv_state, norm_gain, out_weight):
    n_seq, n_head = lax.axis_size("seq"), lax.axis_size("head")
    inner = n_seq // LINE
    place, h = lax.axis_index("seq"), lax.axis_index("head")
    z, i = place // inner, place % inner
    tok_rows, local_width = queries.shape
    assert tok_rows == BLOCK
    heads = local_width // DH
    total_width = local_width * n_head
    width = out_weight.shape[1]

    def along(value, hops):
        return lax.ppermute(value, "seq", line_pairs(n_seq, hops))

    terms, stepped = state_prefix(key_input, value_input, n_seq, place)
    some = heads // 2
    inners = [
        causal_part(queries, key_input, value_input, 0, some),
        causal_part(queries, key_input, value_input, some, heads - some),
    ]

    own_columns = hold(out_weight, *stepped)
    w_halves = along(own_columns, SWAP_HALVES)
    w_next = along(own_columns, SWAP_NEXT)
    w_middle = along(own_columns, SWAP_MIDDLE)

    bits = n_head.bit_length() - 1
    order = [int(format(j, "b").zfill(bits)[::-1], 2) for j in range(n_head)] if bits else [0]
    hidden, squares = gated_hidden(
        queries, inners, kv_state, terms, gate_input, norm_gain, h, i, order
    )
    others = [lax.ppermute(hidden, "seq", turn_pairs(n_seq, turn)) for turn in range(1, inner)]

    out_rows = tok_rows // n_head
    half, bit = n_head // 2, 1
    while bit < n_head:
        squares = squares[:half] + lax.ppermute(squares[half:], "head", flip_pairs(n_head, bit))
        half //= 2
        bit *= 2

    is_end = (z == 0) | (z == LINE - 1)
    flag = scalars(is_end)

    rows_list = [hidden] + others

    owners = [z ^ block for block in range(LINE)]
    blocks = [(out_weight,), (w_next,), (w_halves,)]

    def summed(parts, pins, pin_end=None):
        weights = sorted({block for _, own in parts for block in own})
        jobs = [(p, weights.index(block)) for p, (_, own) in enumerate(parts) for block in own]
        sent, kept = project(
            jobs,
            [rows_list[turn] for turn, _ in parts],
            [blocks[block] for block in weights],
            hold(flag, *pins),
        )
        first_sent, bit = sent, 1
        while bit < n_head:
            got = lax.ppermute(sent, "head", flip_pairs(n_head, bit))
            bit *= 2
            if bit < n_head:
                sent, kept = fold(kept, got)
            else:
                got = got if pin_end is None else hold(got, pin_end)
                kept = fold(kept, got, [width * len(own) for _, own in parts])
        pieces = []
        for piece, (turn, own) in zip(kept, parts):
            if turn:
                piece = lax.ppermute(piece, "seq", turn_pairs(n_seq, -turn))
            starts = [(owners[block] * inner + (i + turn) % inner) * width for block in own]
            pieces.append((piece, starts))
        return pieces, first_sent, got

    turns = list(range(inner))
    shape = (out_rows, width * n_seq)
    in_kernel = width % DH == 0 and out_rows == DH

    pieces, pins, ends = [], [w_halves, w_next], []

    def group(members, some):
        more, sent, end = summed([(turn, some) for turn in members], pins)
        pieces.extend(more)
        ends.append(end)
        pins[:] = [sent, squares]
        return [piece for piece, _ in more]

    group(turns[:1], [0])
    returned = group(turns[1:], [0]) if inner > 1 else []
    w_ends = along(w_halves, TO_ENDS)
    blocks.append((w_middle, w_ends))
    group(turns[:1], [1, 2])
    if inner > 1:
        group(turns[1:], [1, 2])
    filled = placed(None, pieces, squares, width, shape, total_width) if in_kernel else None
    last, _, _ = summed(
        [(turn, [3]) for turn in turns], [*pins, *ends, *returned], filled
    )
    if in_kernel:
        return placed(filled, last, squares, width, shape, total_width)
    scale = lax.rsqrt(squares.reshape(out_rows, 1) / total_width + epsilon)
    output = jnp.zeros(shape, jnp.bfloat16)
    for piece, starts in pieces + last:
        piece = (piece.astype(jnp.float32) * scale).astype(jnp.bfloat16)
        for index, start in enumerate(starts):
            part = piece[:, index * width : (index + 1) * width]
            output = lax.dynamic_update_slice_in_dim(output, part, start, 1)
    return output


def solution(mesh):
    in_specs = (
        P("seq", "head"),
        P("seq", "head"),
        P("seq", "head"),
        P("seq", "head"),
        P("head", None, None),
        P(),
        P("head", "seq"),
    )
    out_specs = P(("seq", "head"), None)
    return jax.shard_map(shards, mesh=mesh, in_specs=in_specs, out_specs=out_specs, check_vma=False)
```

```python
import functools

import jax
import jax.numpy as jnp
from jax import lax
from jax.experimental import pallas as pl
from jax.experimental.pallas import tpu as pltpu
from jax.sharding import PartitionSpec as P

DH = 128
BLOCK = 512
LINE = 4
VMEM_BYTES = 16 * 1024 * 1024


epsilon = 1e-05


def line_pairs(n_seq, hops):
    inner = n_seq // LINE
    return [(a * inner + i, b * inner + i) for a, b in hops for i in range(inner)]


def turn_pairs(n_seq, turn):
    inner = n_seq // LINE
    return [(a * inner + i, a * inner + (i + turn) % inner) for a in range(LINE) for i in range(inner)]


def flip_pairs(n_head, bit):
    return [(h, h ^ bit) for h in range(n_head)]


SWAP_NEXT = [(z, z ^ 1) for z in range(LINE)]
SWAP_HALVES = [(z, z ^ 2) for z in range(LINE)]
SWAP_MIDDLE = [(1, 2), (2, 1)]
TO_ENDS = [(1, 0), (2, 3)]


def hold(value, *others):
    return lax.optimization_barrier((value, *others))[0]


def scalars(*values):
    return jnp.stack([jnp.asarray(value, jnp.int32) for value in values])


def local_call(kernel, places, operands, out_shapes, flops=0):
    held = sum(value.size * value.dtype.itemsize for value in [*operands, *out_shapes])
    return pl.pallas_call(
        kernel,
        in_specs=[pl.BlockSpec(memory_space=pltpu.SMEM)]
        + [pl.BlockSpec(memory_space=pltpu.VMEM)] * len(operands),
        out_specs=[pl.BlockSpec(memory_space=pltpu.VMEM)] * len(out_shapes),
        out_shape=out_shapes,
        compiler_params=pltpu.CompilerParams(vmem_limit_bytes=max(VMEM_BYTES, held + held // 2)),
        cost_estimate=pl.CostEstimate(flops=flops, bytes_accessed=held, transcendentals=0),
    )(places, *operands)


def combine_kernel(count, always, masks_ref, *refs):
    values, outs = refs[:count], refs[count:]
    for index in range(values[0].shape[0]):
        total = values[0][index].astype(jnp.float32)
        for value in values[1:always]:
            total = total + value[index].astype(jnp.float32)
        for position, out in enumerate(outs):
            own = total
            for k in range(always, count):
                mask = masks_ref[position * (count - always) + k - always]
                own = own + jnp.where(mask != 0, values[k][index].astype(jnp.float32), 0.0)
            out[index] = own.astype(out.dtype)


def combine(values, dtypes, sometimes=(), masks=None):
    operands = list(values) + list(sometimes)
    masks = scalars(0) if masks is None else scalars(*masks)
    return local_call(
        functools.partial(combine_kernel, len(operands), len(values)),
        masks,
        operands,
        [jax.ShapeDtypeStruct(values[0].shape, dtype) for dtype in dtypes],
    )


def cut_kernel(places_ref, weight_ref, *outs):
    first = 0
    for out in outs:
        out[...] = weight_ref[:, pl.ds(first, out.shape[1])]
        first += out.shape[1]


def cut_columns(weight, widths):
    shapes = [jax.ShapeDtypeStruct((weight.shape[0], width), weight.dtype) for width in widths]
    return local_call(cut_kernel, scalars(0), [weight], shapes)


def states_kernel(part_ref, k_ref, v_ref, out_ref):
    heads = out_ref.shape[0]
    for index in range(heads):
        columns = pl.ds(pl.multiple_of((part_ref[0] * heads + index) * DH, DH), DH)
        out_ref[index] = lax.dot_general(
            k_ref[:, columns],
            v_ref[:, columns],
            (((0,), (0,)), ((), ())),
            preferred_element_type=jnp.float32,
        ).astype(out_ref.dtype)


def block_states(key_input, value_input, part, heads, dtype):
    return local_call(
        states_kernel,
        scalars(part),
        [key_input, value_input],
        [jax.ShapeDtypeStruct((heads, DH, DH), dtype)],
        2 * key_input.shape[0] * heads * DH * DH,
    )[0]


def state_prefix(key_input, value_input, n_seq, place):
    inner = n_seq // LINE
    i = place % inner
    heads = key_input.shape[1] // DH
    split = heads % inner == 0
    share = heads // inner if split else heads
    if split:
        sends = [
            block_states(key_input, value_input, (i + turn) % inner, share, jnp.bfloat16)
            for turn in range(1, inner)
        ]
        own = block_states(key_input, value_input, i, share, jnp.float32)
    else:
        own = block_states(key_input, value_input, 0, share, jnp.float32)
        sends = [own.astype(jnp.bfloat16)] * (inner - 1)
    values, members = [own], [i]
    for turn in range(1, inner):
        values.append(lax.ppermute(sends[turn - 1], "seq", turn_pairs(n_seq, turn)))
        members.append((i - turn) % inner)
    (first,) = combine(values, [jnp.bfloat16])
    from_left = lax.ppermute(first, "seq", line_pairs(n_seq, [(0, 1), (2, 3)]))
    (second,) = combine(values + [from_left], [jnp.bfloat16])
    near = lax.ppermute(second, "seq", line_pairs(n_seq, [(1, 2)]))
    far = lax.ppermute(second, "seq", line_pairs(n_seq, [(1, 3)]))
    targets = [i] + [(i + turn) % inner for turn in range(1, inner)] if split else [i]
    masks = [owner < target for target in targets for owner in members]
    dtypes = [jnp.float32] + [jnp.bfloat16] * (len(targets) - 1)
    befores = combine([from_left, near, far], dtypes, values, masks)
    terms = [befores[0]]
    for turn in range(1, len(targets)):
        terms.append(lax.ppermute(befores[turn], "seq", turn_pairs(n_seq, turn)))
    return terms, [near, far]


def causal_kernel(first_head, place_ref, q_ref, k_ref, v_ref, out_ref):
    rows = q_ref.shape[0]
    half = rows // 2
    top, bottom = pl.ds(0, half), pl.ds(half, half)
    keep = lax.broadcasted_iota(jnp.int32, (half, half), 0) >= lax.broadcasted_iota(
        jnp.int32, (half, half), 1
    )

    def scores(q_rows, k_rows, columns):
        return lax.dot_general(
            q_ref[q_rows, columns],
            k_ref[k_rows, columns],
            (((1,), (1,)), ((), ())),
            preferred_element_type=jnp.float32,
        )

    for index in range(out_ref.shape[1] // DH):
        columns = pl.ds((first_head + index) * DH, DH)
        placed = pl.ds(index * DH, DH)
        first = jnp.where(keep, scores(top, top, columns), 0.0).astype(jnp.bfloat16)
        below = scores(bottom, top, columns).astype(jnp.bfloat16)
        last = jnp.where(keep, scores(bottom, bottom, columns), 0.0).astype(jnp.bfloat16)
        out_ref[top, placed] = jnp.dot(first, v_ref[top, columns], preferred_element_type=jnp.float32)
        out_ref[bottom, placed] = jnp.dot(
            jnp.concatenate([below, last], axis=1),
            v_ref[:, columns],
            preferred_element_type=jnp.float32,
        )


def causal_part(queries, key_input, value_input, first_head, heads):
    return local_call(
        functools.partial(causal_kernel, first_head),
        scalars(0),
        [queries, key_input, value_input],
        [jax.ShapeDtypeStruct((queries.shape[0], heads * DH), jnp.float32)],
        3 * queries.shape[0] ** 2 * heads * DH,
    )[0]


def hidden_kernel(order, group, calls, place_ref, q_ref, gate_ref, gain_ref, kv_ref, *refs):
    terms, inners = refs[:group], refs[group : group + calls]
    hidden_ref, squares_ref = refs[group + calls :]
    heads = kv_ref.shape[0]
    share = heads // group
    size = q_ref.shape[0] // len(order)
    states = []
    for head in range(heads):
        state = kv_ref[head]
        for turn, term in enumerate(terms):
            value = term[head % share].astype(jnp.float32)
            if group > 1:
                covers = lax.rem(place_ref[1] - turn + group, group)
                value = jnp.where(covers == head // share, value, 0.0)
            state = state + value
        high = state.astype(jnp.bfloat16)
        low = (state - high.astype(jnp.float32)).astype(jnp.bfloat16)
        states.append(jnp.concatenate([high, low], axis=0))
    for position, block in enumerate(order):
        start = pl.multiple_of((place_ref[0] ^ block) * size, size)
        rows = pl.ds(start, size)
        placed = pl.ds(position * size, size)
        squares = jnp.zeros((size, DH), jnp.float32)
        for head in range(heads):
            columns = pl.ds(head * DH, DH)
            q_rows = q_ref[rows, columns]
            carried = jnp.dot(
                jnp.concatenate([q_rows, q_rows], axis=1),
                states[head],
                preferred_element_type=jnp.float32,
            )
            per_call = inners[0].shape[1] // DH
            inner = inners[head // per_call][rows, pl.ds(head % per_call * DH, DH)]
            attn = (carried + inner).astype(jnp.bfloat16).astype(jnp.float32)
            gate = 1.0 + jnp.tanh(gate_ref[rows, columns].astype(jnp.float32) * 0.5)
            gain = gain_ref[place_ref[0] * heads + head] * 0.5
            hidden_ref[placed, columns] = (attn * (gain * gate)).astype(jnp.bfloat16)
            squares = squares + attn * attn
        squares_ref[pl.ds(position, 1), :] = jnp.sum(jnp.transpose(squares), axis=0, keepdims=True)


def gated_hidden(queries, inners, kv_state, terms, gate_input, norm_gain, h, i, order):
    rows, width = queries.shape
    return local_call(
        functools.partial(hidden_kernel, order, len(terms), len(inners)),
        scalars(h, i),
        [queries, gate_input, norm_gain.reshape(-1, 1, DH), kv_state, *terms, *inners],
        [
            jax.ShapeDtypeStruct((rows, width), jnp.bfloat16),
            jax.ShapeDtypeStruct((len(order), rows // len(order)), jnp.float32),
        ],
        4 * rows * width * DH,
    )


def project_kernel(jobs, n_rows, choices, flag_ref, *refs):
    rows_refs = refs[:n_rows]
    weight_refs = refs[n_rows:-2]
    sent_ref, kept_ref = refs[-2:]
    half = sent_ref.shape[0]

    def products(rows, ref, source, target, width):
        columns = pl.ds(target, width)
        product = jnp.dot(
            rows_refs[rows][...],
            weight_refs[ref][:, pl.ds(source, width)],
            preferred_element_type=jnp.float32,
        )
        kept_ref[:, columns] = product[:half]
        sent_ref[:, columns] = product[half:].astype(jnp.bfloat16)

    target = 0
    for rows, weight in jobs:
        width = choices[weight][0][2]
        for k, (ref, source, _) in enumerate(choices[weight]):
            one = functools.partial(products, rows, ref, source, target, width)
            if len(choices[weight]) == 1:
                one()
            else:
                pl.when(flag_ref[0] == k)(one)
        target += width


def project(jobs, rows_list, weights, flag):
    arrays, choices = [], []
    for weight in weights:
        choices.append([])
        for array, first, width in weight:
            known = [n for n, other in enumerate(arrays) if other is array]
            if not known:
                arrays.append(array)
            choices[-1].append((known[0] if known else len(arrays) - 1, first, width))
    height, depth = rows_list[0].shape
    total = sum(choices[weight][0][2] for _, weight in jobs)
    shape = (height // 2, total)
    return local_call(
        functools.partial(project_kernel, tuple(jobs), len(rows_list), choices),
        flag,
        [*rows_list, *arrays],
        [jax.ShapeDtypeStruct(shape, jnp.bfloat16), jax.ShapeDtypeStruct(shape, jnp.float32)],
        2 * height * depth * total,
    )


def fold_kernel(more, flag_ref, kept_ref, got_ref, *outs):
    if more:
        sent_ref, left_ref = outs
        half = left_ref.shape[0]
        left_ref[...] = kept_ref[:half] + got_ref[:half].astype(jnp.float32)
        sent_ref[...] = (kept_ref[half:] + got_ref[half:].astype(jnp.float32)).astype(jnp.bfloat16)
        return
    first = 0
    for out in outs:
        columns = pl.ds(first, out.shape[1])
        out[...] = (kept_ref[:, columns] + got_ref[:, columns].astype(jnp.float32)).astype(out.dtype)
        first += out.shape[1]


def fold(kept, got, widths=None):
    rows, width = kept.shape
    if widths is None:
        shape = (rows // 2, width)
        outs = [jax.ShapeDtypeStruct(shape, jnp.bfloat16), jax.ShapeDtypeStruct(shape, jnp.float32)]
    else:
        outs = [jax.ShapeDtypeStruct((rows, some), jnp.bfloat16) for some in widths]
    return local_call(functools.partial(fold_kernel, widths is None), scalars(0), [kept, got], outs)


def column(row):
    return jnp.transpose(jnp.broadcast_to(row, (row.shape[1], row.shape[1])))


def scaled_parts(counts, width, starts_ref, squares_ref, pieces, total_width):
    scale = lax.rsqrt(column(squares_ref[...]) / total_width + epsilon)
    where = 0
    for piece, count in zip(pieces, counts):
        for index in range(count):
            for at in range(0, width, DH):
                part = piece[:, pl.ds(index * width + at, DH)].astype(jnp.float32) * scale
                yield part, pl.multiple_of(starts_ref[where] + at, DH)
            where += 1


def placed_kernel(counts, width, total_width, starts_ref, squares_ref, *refs):
    out_ref = refs[-1]
    for part, start in scaled_parts(counts, width, starts_ref, squares_ref, refs[:-1], total_width):
        out_ref[:, pl.ds(start, DH)] = part.astype(out_ref.dtype)


def added_kernel(counts, width, total_width, starts_ref, squares_ref, *refs):
    out_ref, buf, sem = refs[-3:]
    copies = []
    parts = scaled_parts(counts, width, starts_ref, squares_ref, refs[: len(counts)], total_width)
    for at, (part, start) in enumerate(parts):
        buf[at] = part.astype(out_ref.dtype)
        copies.append(pltpu.make_async_copy(buf.at[at], out_ref.at[:, pl.ds(start, DH)], sem.at[at]))
        copies[-1].start()
    for copy in copies:
        copy.wait()


def placed(filled, pieces, squares, width, shape, total_width):
    counts = tuple(len(starts) for _, starts in pieces)
    starts = scalars(*[start for _, own in pieces for start in own])
    operands = [squares] + [piece for piece, _ in pieces]
    out_shape = jax.ShapeDtypeStruct(shape, jnp.bfloat16)
    columns = width * sum(counts)
    if filled is None:
        kernel = functools.partial(placed_kernel, counts, width, total_width)
        return local_call(kernel, starts, operands, [out_shape])[0]
    return pl.pallas_call(
        functools.partial(added_kernel, counts, width, total_width),
        in_specs=[pl.BlockSpec(memory_space=pltpu.SMEM)]
        + [pl.BlockSpec(memory_space=pltpu.VMEM)] * len(operands)
        + [pl.BlockSpec(memory_space=pl.ANY)],
        out_specs=pl.BlockSpec(memory_space=pl.ANY),
        out_shape=out_shape,
        scratch_shapes=[
            pltpu.VMEM((columns // DH, shape[0], DH), jnp.bfloat16),
            pltpu.SemaphoreType.DMA((columns // DH,)),
        ],
        input_output_aliases={len(operands) + 1: 0},
        compiler_params=pltpu.CompilerParams(vmem_limit_bytes=VMEM_BYTES),
        cost_estimate=pl.CostEstimate(
            flops=0, bytes_accessed=4 * shape[0] * columns, transcendentals=0
        ),
    )(starts, *operands, filled)


def shards(queries, key_input, value_input, gate_input, kv_state, norm_gain, out_weight):
    n_seq, n_head = lax.axis_size("seq"), lax.axis_size("head")
    inner = n_seq // LINE
    place, h = lax.axis_index("seq"), lax.axis_index("head")
    z, i = place // inner, place % inner
    tok_rows, local_width = queries.shape
    assert tok_rows == BLOCK
    heads = local_width // DH
    total_width = local_width * n_head
    width = out_weight.shape[1]

    def along(value, hops):
        return lax.ppermute(value, "seq", line_pairs(n_seq, hops))

    terms, stepped = state_prefix(key_input, value_input, n_seq, place)
    some = heads // 2
    inners = [
        causal_part(queries, key_input, value_input, 0, some),
        causal_part(queries, key_input, value_input, some, heads - some),
    ]

    if width % DH == 0 and width > DH:
        cuts = [(0, DH), (DH, width - DH)]
        w_cuts = list(cut_columns(out_weight, [size for _, size in cuts]))
    else:
        cuts, w_cuts = [(0, width)], [out_weight]
    w_cuts[0] = hold(w_cuts[0], *stepped)
    w_halves = [along(w_cuts[0], SWAP_HALVES)]
    w_next = [along(w_cuts[0], SWAP_NEXT)]
    if len(cuts) > 1:
        terms[0] = hold(terms[0], w_halves[0], w_next[0])

    bits = n_head.bit_length() - 1
    order = [int(format(j, "b").zfill(bits)[::-1], 2) for j in range(n_head)] if bits else [0]
    hidden, squares = gated_hidden(
        queries, inners, kv_state, terms, gate_input, norm_gain, h, i, order
    )
    for w_cut in w_cuts[1:]:
        w_cut = hold(w_cut, *w_halves, *w_next)
        w_next.append(along(w_cut, SWAP_NEXT))
        w_halves.append(along(w_cut, SWAP_HALVES))
    w_middle = along(hold(out_weight, *stepped), SWAP_MIDDLE)
    others = [lax.ppermute(hidden, "seq", turn_pairs(n_seq, turn)) for turn in range(1, inner)]

    out_rows = tok_rows // n_head
    half, bit = n_head // 2, 1
    while bit < n_head:
        squares = squares[:half] + lax.ppermute(squares[half:], "head", flip_pairs(n_head, bit))
        half //= 2
        bit *= 2

    is_end = (z == 0) | (z == LINE - 1)
    flag = scalars(is_end)

    rows_list = [hidden] + others

    owners = [z ^ block for block in range(LINE)]
    blocks = [
        [((out_weight, 0, width),)],
        [((w, 0, size),) for w, (_, size) in zip(w_next, cuts)],
        [((w, 0, size),) for w, (_, size) in zip(w_halves, cuts)],
    ]

    def summed(parts, pins, pin_end=None):
        weights, jobs = [], []
        where = {}
        for p, (_, own) in enumerate(parts):
            for block in own:
                if block not in where:
                    where[block] = range(len(weights), len(weights) + len(blocks[block]))
                    weights += blocks[block]
                jobs += [(p, n) for n in where[block]]
        sent, kept = project(jobs, [rows_list[turn] for turn, _ in parts], weights, hold(flag, *pins))
        first_sent, steps, bit = sent, [], 1
        while bit < n_head:
            got = lax.ppermute(sent, "head", flip_pairs(n_head, bit))
            steps.append(got)
            bit *= 2
            if bit < n_head:
                sent, kept = fold(kept, got)
            else:
                got = got if pin_end is None else hold(got, pin_end)
                kept = fold(kept, got, [width * len(own) for _, own in parts])
        pieces = []
        for piece, (turn, own) in zip(kept, parts):
            if turn:
                piece = lax.ppermute(piece, "seq", turn_pairs(n_seq, -turn))
            starts = [(owners[block] * inner + (i + turn) % inner) * width for block in own]
            pieces.append((piece, starts))
        return pieces, first_sent, steps

    turns = list(range(inner))
    shape = (out_rows, width * n_seq)
    in_kernel = width % DH == 0 and out_rows == DH

    pieces, pins, ends = [], [], []

    def group(members, some):
        more, sent, steps = summed([(turn, some) for turn in members], pins)
        pieces.extend(more)
        ends.append(steps[-1])
        pins[:] = [sent, squares]
        return [piece for piece, _ in more]

    w_ends = [along(w, TO_ENDS) for w in w_halves[:-1]]
    group(turns[:1], [0])
    pins += w_ends
    returned = group(turns[1:], [0]) if inner > 1 else []
    w_ends.append(along(hold(w_halves[-1], *ends), TO_ENDS))
    blocks.append([((w_middle, first, size), (w, 0, size)) for w, (first, size) in zip(w_ends, cuts)])
    for block in (1, 2):
        group(turns[:1], [block])
        if inner > 1:
            group(turns[1:], [block])
    filled = placed(None, pieces, squares, width, shape, total_width) if in_kernel else None
    last, _, _ = summed(
        [(turn, [3]) for turn in turns], [*pins, *ends, *returned], filled
    )
    if in_kernel:
        return placed(filled, last, squares, width, shape, total_width)
    scale = lax.rsqrt(squares.reshape(out_rows, 1) / total_width + epsilon)
    output = jnp.zeros(shape, jnp.bfloat16)
    for piece, starts in pieces + last:
        piece = (piece.astype(jnp.float32) * scale).astype(jnp.bfloat16)
        for index, start in enumerate(starts):
            part = piece[:, index * width : (index + 1) * width]
            output = lax.dynamic_update_slice_in_dim(output, part, start, 1)
    return output


def solution(mesh):
    in_specs = (
        P("seq", "head"),
        P("seq", "head"),
        P("seq", "head"),
        P("seq", "head"),
        P("head", None, None),
        P(),
        P("head", "seq"),
    )
    out_specs = P(("seq", "head"), None)
    return jax.shard_map(shards, mesh=mesh, in_specs=in_specs, out_specs=out_specs, check_vma=False)
```

```python
import functools

import jax
import jax.numpy as jnp
from jax import lax
from jax.experimental import pallas as pl
from jax.experimental.pallas import tpu as pltpu
from jax.sharding import PartitionSpec as P

DH = 128
BLOCK = 512
LINE = 4
VMEM_BYTES = 16 * 1024 * 1024


epsilon = 1e-05


def line_pairs(n_seq, hops):
    inner = n_seq // LINE
    return [(a * inner + i, b * inner + i) for a, b in hops for i in range(inner)]


def turn_pairs(n_seq, turn):
    inner = n_seq // LINE
    return [(a * inner + i, a * inner + (i + turn) % inner) for a in range(LINE) for i in range(inner)]


def flip_pairs(n_head, bit):
    return [(h, h ^ bit) for h in range(n_head)]


SWAP_NEXT = [(z, z ^ 1) for z in range(LINE)]
SWAP_HALVES = [(z, z ^ 2) for z in range(LINE)]
SWAP_MIDDLE = [(1, 2), (2, 1)]
TO_ENDS = [(1, 0), (2, 3)]


def hold(value, *others):
    return lax.optimization_barrier((value, *others))[0]


def scalars(*values):
    return jnp.stack([jnp.asarray(value, jnp.int32) for value in values])


def local_call(kernel, places, operands, out_shapes, flops=0):
    held = sum(value.size * value.dtype.itemsize for value in [*operands, *out_shapes])
    return pl.pallas_call(
        kernel,
        in_specs=[pl.BlockSpec(memory_space=pltpu.SMEM)]
        + [pl.BlockSpec(memory_space=pltpu.VMEM)] * len(operands),
        out_specs=[pl.BlockSpec(memory_space=pltpu.VMEM)] * len(out_shapes),
        out_shape=out_shapes,
        compiler_params=pltpu.CompilerParams(vmem_limit_bytes=max(VMEM_BYTES, held + held // 2)),
        cost_estimate=pl.CostEstimate(flops=flops, bytes_accessed=held, transcendentals=0),
    )(places, *operands)


def combine_kernel(count, always, masks_ref, *refs):
    values, outs = refs[:count], refs[count:]
    for index in range(values[0].shape[0]):
        total = values[0][index].astype(jnp.float32)
        for value in values[1:always]:
            total = total + value[index].astype(jnp.float32)
        for position, out in enumerate(outs):
            own = total
            for k in range(always, count):
                mask = masks_ref[position * (count - always) + k - always]
                own = own + jnp.where(mask != 0, values[k][index].astype(jnp.float32), 0.0)
            out[index] = own.astype(out.dtype)


def combine(values, dtypes, sometimes=(), masks=None):
    operands = list(values) + list(sometimes)
    masks = scalars(0) if masks is None else scalars(*masks)
    return local_call(
        functools.partial(combine_kernel, len(operands), len(values)),
        masks,
        operands,
        [jax.ShapeDtypeStruct(values[0].shape, dtype) for dtype in dtypes],
    )


def states_kernel(part_ref, k_ref, v_ref, out_ref):
    heads = out_ref.shape[0]
    for index in range(heads):
        columns = pl.ds(pl.multiple_of((part_ref[0] * heads + index) * DH, DH), DH)
        out_ref[index] = lax.dot_general(
            k_ref[:, columns],
            v_ref[:, columns],
            (((0,), (0,)), ((), ())),
            preferred_element_type=jnp.float32,
        ).astype(out_ref.dtype)


def block_states(key_input, value_input, part, heads, dtype):
    return local_call(
        states_kernel,
        scalars(part),
        [key_input, value_input],
        [jax.ShapeDtypeStruct((heads, DH, DH), dtype)],
        2 * key_input.shape[0] * heads * DH * DH,
    )[0]


def state_prefix(key_input, value_input, n_seq, place):
    inner = n_seq // LINE
    i = place % inner
    heads = key_input.shape[1] // DH
    split = heads % inner == 0
    share = heads // inner if split else heads
    if split:
        sends = [
            block_states(key_input, value_input, (i + turn) % inner, share, jnp.bfloat16)
            for turn in range(1, inner)
        ]
        own = block_states(key_input, value_input, i, share, jnp.float32)
    else:
        own = block_states(key_input, value_input, 0, share, jnp.float32)
        sends = [own.astype(jnp.bfloat16)] * (inner - 1)
    values, members = [own], [i]
    for turn in range(1, inner):
        values.append(lax.ppermute(sends[turn - 1], "seq", turn_pairs(n_seq, turn)))
        members.append((i - turn) % inner)
    (first,) = combine(values, [jnp.bfloat16])
    from_left = lax.ppermute(first, "seq", line_pairs(n_seq, [(0, 1), (2, 3)]))
    (second,) = combine(values + [from_left], [jnp.bfloat16])
    near = lax.ppermute(second, "seq", line_pairs(n_seq, [(1, 2)]))
    far = lax.ppermute(second, "seq", line_pairs(n_seq, [(1, 3)]))
    targets = [i] + [(i + turn) % inner for turn in range(1, inner)] if split else [i]
    masks = [owner < target for target in targets for owner in members]
    dtypes = [jnp.float32] + [jnp.bfloat16] * (len(targets) - 1)
    befores = combine([from_left, near, far], dtypes, values, masks)
    terms = [befores[0]]
    for turn in range(1, len(targets)):
        terms.append(lax.ppermute(befores[turn], "seq", turn_pairs(n_seq, turn)))
    return terms, [near, far]


def causal_kernel(first_head, place_ref, q_ref, k_ref, v_ref, out_ref):
    rows = q_ref.shape[0]
    half = rows // 2
    top, bottom = pl.ds(0, half), pl.ds(half, half)
    keep = lax.broadcasted_iota(jnp.int32, (half, half), 0) >= lax.broadcasted_iota(
        jnp.int32, (half, half), 1
    )

    def scores(q_rows, k_rows, columns):
        return lax.dot_general(
            q_ref[q_rows, columns],
            k_ref[k_rows, columns],
            (((1,), (1,)), ((), ())),
            preferred_element_type=jnp.float32,
        )

    for index in range(out_ref.shape[1] // DH):
        columns = pl.ds((first_head + index) * DH, DH)
        placed = pl.ds(index * DH, DH)
        first = jnp.where(keep, scores(top, top, columns), 0.0).astype(jnp.bfloat16)
        below = scores(bottom, top, columns).astype(jnp.bfloat16)
        last = jnp.where(keep, scores(bottom, bottom, columns), 0.0).astype(jnp.bfloat16)
        out_ref[top, placed] = jnp.dot(first, v_ref[top, columns], preferred_element_type=jnp.float32)
        out_ref[bottom, placed] = jnp.dot(
            jnp.concatenate([below, last], axis=1),
            v_ref[:, columns],
            preferred_element_type=jnp.float32,
        )


def causal_part(queries, key_input, value_input, first_head, heads):
    return local_call(
        functools.partial(causal_kernel, first_head),
        scalars(0),
        [queries, key_input, value_input],
        [jax.ShapeDtypeStruct((queries.shape[0], heads * DH), jnp.float32)],
        3 * queries.shape[0] ** 2 * heads * DH,
    )[0]


def hidden_kernel(order, group, calls, place_ref, q_ref, gate_ref, gain_ref, kv_ref, *refs):
    terms, inners = refs[:group], refs[group : group + calls]
    kept_ref, sent_ref, squares_ref = refs[group + calls :]
    half = kept_ref.shape[0]
    heads = kv_ref.shape[0]
    share = heads // group
    size = q_ref.shape[0] // len(order)
    states = []
    for head in range(heads):
        state = kv_ref[head]
        for turn, term in enumerate(terms):
            value = term[head % share].astype(jnp.float32)
            if group > 1:
                covers = lax.rem(place_ref[1] - turn + group, group)
                value = jnp.where(covers == head // share, value, 0.0)
            state = state + value
        high = state.astype(jnp.bfloat16)
        low = (state - high.astype(jnp.float32)).astype(jnp.bfloat16)
        states.append(jnp.concatenate([high, low], axis=0))
    for position, block in enumerate(order):
        start = pl.multiple_of((place_ref[0] ^ block) * size, size)
        rows = pl.ds(start, size)
        hidden_ref = kept_ref if position * size < half else sent_ref
        placed = pl.ds(position * size % half, size)
        squares = jnp.zeros((size, DH), jnp.float32)
        for head in range(heads):
            columns = pl.ds(head * DH, DH)
            q_rows = q_ref[rows, columns]
            carried = jnp.dot(
                jnp.concatenate([q_rows, q_rows], axis=1),
                states[head],
                preferred_element_type=jnp.float32,
            )
            per_call = inners[0].shape[1] // DH
            inner = inners[head // per_call][rows, pl.ds(head % per_call * DH, DH)]
            attn = (carried + inner).astype(jnp.bfloat16).astype(jnp.float32)
            gate = 1.0 + jnp.tanh(gate_ref[rows, columns].astype(jnp.float32) * 0.5)
            gain = gain_ref[place_ref[0] * heads + head] * 0.5
            hidden_ref[placed, columns] = (attn * (gain * gate)).astype(jnp.bfloat16)
            squares = squares + attn * attn
        squares_ref[pl.ds(position, 1), :] = jnp.sum(jnp.transpose(squares), axis=0, keepdims=True)


def gated_hidden(queries, inners, kv_state, terms, gate_input, norm_gain, h, i, order):
    rows, width = queries.shape
    half = jax.ShapeDtypeStruct((rows // 2, width), jnp.bfloat16)
    return local_call(
        functools.partial(hidden_kernel, order, len(terms), len(inners)),
        scalars(h, i),
        [queries, gate_input, norm_gain.reshape(-1, 1, DH), kv_state, *terms, *inners],
        [
            half,
            half,
            jax.ShapeDtypeStruct((len(order), rows // len(order)), jnp.float32),
        ],
        4 * rows * width * DH,
    )


def project_kernel(jobs, n_rows, choices, flag_ref, *refs):
    rows_refs = refs[: 2 * n_rows]
    weight_refs = refs[2 * n_rows : -2]
    sent_ref, kept_ref = refs[-2:]

    def products(index, weight_ref):
        for rows, weight, first in jobs:
            if weight == index:
                columns = pl.ds(first, weight_ref.shape[1])
                kept_rows, sent_rows = rows_refs[2 * rows : 2 * rows + 2]
                sent_ref[:, columns] = jnp.dot(
                    sent_rows[...], weight_ref[...], preferred_element_type=jnp.float32
                ).astype(jnp.bfloat16)
                kept_ref[:, columns] = jnp.dot(
                    kept_rows[...], weight_ref[...], preferred_element_type=jnp.float32
                )

    first = 0
    for index, number in enumerate(choices):
        for k in range(number):
            one = functools.partial(products, index, weight_refs[first + k])
            if number == 1:
                one()
            else:
                pl.when(flag_ref[0] == k)(one)
        first += number


def project(jobs, rows_list, weights, flag):
    flat = [choice for weight in weights for choice in weight]
    choices = tuple(len(weight) for weight in weights)
    placed_jobs, total = [], 0
    for rows, weight in jobs:
        placed_jobs.append((rows, weight, total))
        total += weights[weight][0].shape[1]
    height, depth = rows_list[0][0].shape
    shape = (height, total)
    return local_call(
        functools.partial(project_kernel, tuple(placed_jobs), len(rows_list), choices),
        flag,
        [*[half for pair in rows_list for half in pair], *flat],
        [jax.ShapeDtypeStruct(shape, jnp.bfloat16), jax.ShapeDtypeStruct(shape, jnp.float32)],
        4 * height * depth * total,
    )


def fold_kernel(more, flag_ref, kept_ref, got_ref, *outs):
    if more:
        sent_ref, left_ref = outs
        half = left_ref.shape[0]
        left_ref[...] = kept_ref[:half] + got_ref[:half].astype(jnp.float32)
        sent_ref[...] = (kept_ref[half:] + got_ref[half:].astype(jnp.float32)).astype(jnp.bfloat16)
        return
    first = 0
    for out in outs:
        columns = pl.ds(first, out.shape[1])
        out[...] = (kept_ref[:, columns] + got_ref[:, columns].astype(jnp.float32)).astype(out.dtype)
        first += out.shape[1]


def fold(kept, got, widths=None):
    rows, width = kept.shape
    if widths is None:
        shape = (rows // 2, width)
        outs = [jax.ShapeDtypeStruct(shape, jnp.bfloat16), jax.ShapeDtypeStruct(shape, jnp.float32)]
    else:
        outs = [jax.ShapeDtypeStruct((rows, some), jnp.bfloat16) for some in widths]
    return local_call(functools.partial(fold_kernel, widths is None), scalars(0), [kept, got], outs)


def column(row):
    return jnp.transpose(jnp.broadcast_to(row, (row.shape[1], row.shape[1])))


def scaled_parts(counts, width, starts_ref, squares_ref, pieces, total_width):
    scale = lax.rsqrt(column(squares_ref[...]) / total_width + epsilon)
    where = 0
    for piece, count in zip(pieces, counts):
        for index in range(count):
            for at in range(0, width, DH):
                part = piece[:, pl.ds(index * width + at, DH)].astype(jnp.float32) * scale
                yield part, pl.multiple_of(starts_ref[where] + at, DH)
            where += 1


def placed_kernel(counts, width, total_width, starts_ref, squares_ref, *refs):
    out_ref = refs[-1]
    for part, start in scaled_parts(counts, width, starts_ref, squares_ref, refs[:-1], total_width):
        out_ref[:, pl.ds(start, DH)] = part.astype(out_ref.dtype)


def added_kernel(counts, width, total_width, starts_ref, squares_ref, *refs):
    out_ref, buf, sem = refs[-3:]
    copies = []
    parts = scaled_parts(counts, width, starts_ref, squares_ref, refs[: len(counts)], total_width)
    for at, (part, start) in enumerate(parts):
        buf[at] = part.astype(out_ref.dtype)
        copies.append(pltpu.make_async_copy(buf.at[at], out_ref.at[:, pl.ds(start, DH)], sem.at[at]))
        copies[-1].start()
    for copy in copies:
        copy.wait()


def placed(filled, pieces, squares, width, shape, total_width):
    counts = tuple(len(starts) for _, starts in pieces)
    starts = scalars(*[start for _, own in pieces for start in own])
    operands = [squares] + [piece for piece, _ in pieces]
    out_shape = jax.ShapeDtypeStruct(shape, jnp.bfloat16)
    columns = width * sum(counts)
    if filled is None:
        kernel = functools.partial(placed_kernel, counts, width, total_width)
        return local_call(kernel, starts, operands, [out_shape])[0]
    return pl.pallas_call(
        functools.partial(added_kernel, counts, width, total_width),
        in_specs=[pl.BlockSpec(memory_space=pltpu.SMEM)]
        + [pl.BlockSpec(memory_space=pltpu.VMEM)] * len(operands)
        + [pl.BlockSpec(memory_space=pl.ANY)],
        out_specs=pl.BlockSpec(memory_space=pl.ANY),
        out_shape=out_shape,
        scratch_shapes=[
            pltpu.VMEM((columns // DH, shape[0], DH), jnp.bfloat16),
            pltpu.SemaphoreType.DMA((columns // DH,)),
        ],
        input_output_aliases={len(operands) + 1: 0},
        compiler_params=pltpu.CompilerParams(vmem_limit_bytes=VMEM_BYTES),
        cost_estimate=pl.CostEstimate(
            flops=0, bytes_accessed=4 * shape[0] * columns, transcendentals=0
        ),
    )(starts, *operands, filled)


def shards(queries, key_input, value_input, gate_input, kv_state, norm_gain, out_weight):
    n_seq, n_head = lax.axis_size("seq"), lax.axis_size("head")
    inner = n_seq // LINE
    place, h = lax.axis_index("seq"), lax.axis_index("head")
    z, i = place // inner, place % inner
    tok_rows, local_width = queries.shape
    assert tok_rows == BLOCK
    heads = local_width // DH
    total_width = local_width * n_head
    width = out_weight.shape[1]

    def along(value, hops):
        return lax.ppermute(value, "seq", line_pairs(n_seq, hops))

    terms, stepped = state_prefix(key_input, value_input, n_seq, place)
    some = heads // 2
    inners = [
        causal_part(queries, key_input, value_input, 0, some),
        causal_part(queries, key_input, value_input, some, heads - some),
    ]

    own_columns = hold(out_weight, *stepped)
    w_halves = along(own_columns, SWAP_HALVES)
    w_next = along(own_columns, SWAP_NEXT)
    w_middle = along(own_columns, SWAP_MIDDLE)

    bits = n_head.bit_length() - 1
    order = [int(format(j, "b").zfill(bits)[::-1], 2) for j in range(n_head)] if bits else [0]
    kept_rows, sent_rows, squares = gated_hidden(
        queries, inners, kv_state, terms, gate_input, norm_gain, h, i, order
    )
    rows_list = [(kept_rows, sent_rows)]
    for turn in range(1, inner):
        pairs = turn_pairs(n_seq, turn)
        rows_list.append((lax.ppermute(kept_rows, "seq", pairs), lax.ppermute(sent_rows, "seq", pairs)))

    out_rows = tok_rows // n_head
    half, bit = n_head // 2, 1
    while bit < n_head:
        squares = squares[:half] + lax.ppermute(squares[half:], "head", flip_pairs(n_head, bit))
        half //= 2
        bit *= 2

    is_end = (z == 0) | (z == LINE - 1)
    flag = scalars(is_end)


    owners = [z ^ block for block in range(LINE)]
    blocks = [(out_weight,), (w_next,), (w_halves,)]

    def summed(parts, pins, pin_end=None):
        weights = sorted({block for _, own in parts for block in own})
        jobs = [(p, weights.index(block)) for p, (_, own) in enumerate(parts) for block in own]
        sent, kept = project(
            jobs,
            [rows_list[turn] for turn, _ in parts],
            [blocks[block] for block in weights],
            hold(flag, *pins),
        )
        first_sent, bit = sent, 1
        while bit < n_head:
            got = lax.ppermute(sent, "head", flip_pairs(n_head, bit))
            bit *= 2
            if bit < n_head:
                sent, kept = fold(kept, got)
            else:
                got = got if pin_end is None else hold(got, pin_end)
                kept = fold(kept, got, [width * len(own) for _, own in parts])
        pieces = []
        for piece, (turn, own) in zip(kept, parts):
            if turn:
                piece = lax.ppermute(piece, "seq", turn_pairs(n_seq, -turn))
            starts = [(owners[block] * inner + (i + turn) % inner) * width for block in own]
            pieces.append((piece, starts))
        return pieces, first_sent, got

    turns = list(range(inner))
    shape = (out_rows, width * n_seq)
    in_kernel = width % DH == 0 and out_rows == DH

    pieces, pins, ends = [], [], []

    def group(members, some):
        more, sent, end = summed([(turn, some) for turn in members], pins)
        pieces.extend(more)
        ends.append(end)
        pins[:] = [sent, squares]
        return [piece for piece, _ in more]

    group(turns[:1], [0])
    returned = group(turns[1:], [0]) if inner > 1 else []
    w_ends = along(hold(w_halves, *ends), TO_ENDS)
    blocks.append((w_middle, w_ends))
    group(turns[:1], [1, 2])
    if inner > 1:
        group(turns[1:], [1, 2])
    filled = placed(None, pieces, squares, width, shape, total_width) if in_kernel else None
    last, _, _ = summed(
        [(turn, [3]) for turn in turns], [*pins, *ends, *returned], filled
    )
    if in_kernel:
        return placed(filled, last, squares, width, shape, total_width)
    scale = lax.rsqrt(squares.reshape(out_rows, 1) / total_width + epsilon)
    output = jnp.zeros(shape, jnp.bfloat16)
    for piece, starts in pieces + last:
        piece = (piece.astype(jnp.float32) * scale).astype(jnp.bfloat16)
        for index, start in enumerate(starts):
            part = piece[:, index * width : (index + 1) * width]
            output = lax.dynamic_update_slice_in_dim(output, part, start, 1)
    return output


def solution(mesh):
    in_specs = (
        P("seq", "head"),
        P("seq", "head"),
        P("seq", "head"),
        P("seq", "head"),
        P("head", None, None),
        P(),
        P("head", "seq"),
    )
    out_specs = P(("seq", "head"), None)
    return jax.shard_map(shards, mesh=mesh, in_specs=in_specs, out_specs=out_specs, check_vma=False)
```

```python
import functools

import jax
import jax.numpy as jnp
from jax import lax
from jax.experimental import pallas as pl
from jax.experimental.pallas import tpu as pltpu
from jax.sharding import PartitionSpec as P

DH = 128
BLOCK = 512
LINE = 4
VMEM_BYTES = 16 * 1024 * 1024


epsilon = 1e-05


def line_pairs(n_seq, hops):
    inner = n_seq // LINE
    return [(a * inner + i, b * inner + i) for a, b in hops for i in range(inner)]


def turn_pairs(n_seq, turn):
    inner = n_seq // LINE
    return [(a * inner + i, a * inner + (i + turn) % inner) for a in range(LINE) for i in range(inner)]


def flip_pairs(n_head, bit):
    return [(h, h ^ bit) for h in range(n_head)]


SWAP_NEXT = [(z, z ^ 1) for z in range(LINE)]
SWAP_HALVES = [(z, z ^ 2) for z in range(LINE)]
SWAP_MIDDLE = [(1, 2), (2, 1)]
TO_ENDS = [(1, 0), (2, 3)]


def hold(value, *others):
    return lax.optimization_barrier((value, *others))[0]


def scalars(*values):
    return jnp.stack([jnp.asarray(value, jnp.int32) for value in values])


def local_call(kernel, places, operands, out_shapes, flops=0):
    held = sum(value.size * value.dtype.itemsize for value in [*operands, *out_shapes])
    return pl.pallas_call(
        kernel,
        in_specs=[pl.BlockSpec(memory_space=pltpu.SMEM)]
        + [pl.BlockSpec(memory_space=pltpu.VMEM)] * len(operands),
        out_specs=[pl.BlockSpec(memory_space=pltpu.VMEM)] * len(out_shapes),
        out_shape=out_shapes,
        compiler_params=pltpu.CompilerParams(vmem_limit_bytes=max(VMEM_BYTES, held + held // 2)),
        cost_estimate=pl.CostEstimate(flops=flops, bytes_accessed=held, transcendentals=0),
    )(places, *operands)


def combine_kernel(count, always, masks_ref, *refs):
    values, outs = refs[:count], refs[count:]
    for index in range(values[0].shape[0]):
        total = values[0][index].astype(jnp.float32)
        for value in values[1:always]:
            total = total + value[index].astype(jnp.float32)
        for position, out in enumerate(outs):
            own = total
            for k in range(always, count):
                mask = masks_ref[position * (count - always) + k - always]
                own = own + jnp.where(mask != 0, values[k][index].astype(jnp.float32), 0.0)
            out[index] = own.astype(out.dtype)


def combine(values, dtypes, sometimes=(), masks=None):
    operands = list(values) + list(sometimes)
    masks = scalars(0) if masks is None else scalars(*masks)
    return local_call(
        functools.partial(combine_kernel, len(operands), len(values)),
        masks,
        operands,
        [jax.ShapeDtypeStruct(values[0].shape, dtype) for dtype in dtypes],
    )


def states_kernel(part_ref, k_ref, v_ref, out_ref):
    heads = out_ref.shape[0]
    for index in range(heads):
        columns = pl.ds(pl.multiple_of((part_ref[0] * heads + index) * DH, DH), DH)
        out_ref[index] = lax.dot_general(
            k_ref[:, columns],
            v_ref[:, columns],
            (((0,), (0,)), ((), ())),
            preferred_element_type=jnp.float32,
        ).astype(out_ref.dtype)


def block_states(key_input, value_input, part, heads, dtype):
    return local_call(
        states_kernel,
        scalars(part),
        [key_input, value_input],
        [jax.ShapeDtypeStruct((heads, DH, DH), dtype)],
        2 * key_input.shape[0] * heads * DH * DH,
    )[0]


def state_prefix(key_input, value_input, n_seq, place):
    inner = n_seq // LINE
    i = place % inner
    heads = key_input.shape[1] // DH
    split = heads % inner == 0
    share = heads // inner if split else heads
    if split:
        sends = [
            block_states(key_input, value_input, (i + turn) % inner, share, jnp.bfloat16)
            for turn in range(1, inner)
        ]
        own = block_states(key_input, value_input, i, share, jnp.float32)
    else:
        own = block_states(key_input, value_input, 0, share, jnp.float32)
        sends = [own.astype(jnp.bfloat16)] * (inner - 1)
    values, members = [own], [i]
    for turn in range(1, inner):
        values.append(lax.ppermute(sends[turn - 1], "seq", turn_pairs(n_seq, turn)))
        members.append((i - turn) % inner)
    (first,) = combine(values, [jnp.bfloat16])
    from_left = lax.ppermute(first, "seq", line_pairs(n_seq, [(0, 1), (2, 3)]))
    (second,) = combine(values + [from_left], [jnp.bfloat16])
    near = lax.ppermute(second, "seq", line_pairs(n_seq, [(1, 2)]))
    far = lax.ppermute(second, "seq", line_pairs(n_seq, [(1, 3)]))
    targets = [i] + [(i + turn) % inner for turn in range(1, inner)] if split else [i]
    masks = [owner < target for target in targets for owner in members]
    dtypes = [jnp.float32] + [jnp.bfloat16] * (len(targets) - 1)
    befores = combine([from_left, near, far], dtypes, values, masks)
    terms = [befores[0]]
    for turn in range(1, len(targets)):
        terms.append(lax.ppermute(befores[turn], "seq", turn_pairs(n_seq, turn)))
    return terms, [near, far]


def causal_kernel(first_head, place_ref, q_ref, k_ref, v_ref, out_ref):
    rows = q_ref.shape[0]
    half = rows // 2
    top, bottom = pl.ds(0, half), pl.ds(half, half)
    keep = lax.broadcasted_iota(jnp.int32, (half, half), 0) >= lax.broadcasted_iota(
        jnp.int32, (half, half), 1
    )

    def scores(q_rows, k_rows, columns):
        return lax.dot_general(
            q_ref[q_rows, columns],
            k_ref[k_rows, columns],
            (((1,), (1,)), ((), ())),
            preferred_element_type=jnp.float32,
        )

    for index in range(out_ref.shape[1] // DH):
        columns = pl.ds((first_head + index) * DH, DH)
        placed = pl.ds(index * DH, DH)
        first = jnp.where(keep, scores(top, top, columns), 0.0).astype(jnp.bfloat16)
        below = scores(bottom, top, columns).astype(jnp.bfloat16)
        last = jnp.where(keep, scores(bottom, bottom, columns), 0.0).astype(jnp.bfloat16)
        out_ref[top, placed] = jnp.dot(first, v_ref[top, columns], preferred_element_type=jnp.float32)
        out_ref[bottom, placed] = jnp.dot(
            jnp.concatenate([below, last], axis=1),
            v_ref[:, columns],
            preferred_element_type=jnp.float32,
        )


def causal_part(queries, key_input, value_input, first_head, heads):
    return local_call(
        functools.partial(causal_kernel, first_head),
        scalars(0),
        [queries, key_input, value_input],
        [jax.ShapeDtypeStruct((queries.shape[0], heads * DH), jnp.float32)],
        3 * queries.shape[0] ** 2 * heads * DH,
    )[0]


def hidden_kernel(order, group, calls, place_ref, q_ref, gate_ref, gain_ref, kv_ref, *refs):
    terms, inners = refs[:group], refs[group : group + calls]
    kept_ref, sent_ref, squares_ref = refs[group + calls :]
    half = kept_ref.shape[0]
    heads = kv_ref.shape[0]
    share = heads // group
    size = q_ref.shape[0] // len(order)
    states = []
    for head in range(heads):
        state = kv_ref[head]
        for turn, term in enumerate(terms):
            value = term[head % share].astype(jnp.float32)
            if group > 1:
                covers = lax.rem(place_ref[1] - turn + group, group)
                value = jnp.where(covers == head // share, value, 0.0)
            state = state + value
        high = state.astype(jnp.bfloat16)
        low = (state - high.astype(jnp.float32)).astype(jnp.bfloat16)
        states.append(jnp.concatenate([high, low], axis=0))
    for position, block in enumerate(order):
        start = pl.multiple_of((place_ref[0] ^ block) * size, size)
        rows = pl.ds(start, size)
        hidden_ref = kept_ref if position * size < half else sent_ref
        placed = pl.ds(position * size % half, size)
        squares = jnp.zeros((size, DH), jnp.float32)
        for head in range(heads):
            columns = pl.ds(head * DH, DH)
            q_rows = q_ref[rows, columns]
            carried = jnp.dot(
                jnp.concatenate([q_rows, q_rows], axis=1),
                states[head],
                preferred_element_type=jnp.float32,
            )
            per_call = inners[0].shape[1] // DH
            inner = inners[head // per_call][rows, pl.ds(head % per_call * DH, DH)]
            attn = (carried + inner).astype(jnp.bfloat16).astype(jnp.float32)
            gate = 1.0 + jnp.tanh(gate_ref[rows, columns].astype(jnp.float32) * 0.5)
            gain = gain_ref[place_ref[0] * heads + head] * 0.5
            hidden_ref[placed, columns] = (attn * (gain * gate)).astype(jnp.bfloat16)
            squares = squares + attn * attn
        squares_ref[pl.ds(position, 1), :] = jnp.sum(jnp.transpose(squares), axis=0, keepdims=True)


def gated_hidden(queries, inners, kv_state, terms, gate_input, norm_gain, h, i, order):
    rows, width = queries.shape
    half = jax.ShapeDtypeStruct((rows // 2, width), jnp.bfloat16)
    return local_call(
        functools.partial(hidden_kernel, order, len(terms), len(inners)),
        scalars(h, i),
        [queries, gate_input, norm_gain.reshape(-1, 1, DH), kv_state, *terms, *inners],
        [
            half,
            half,
            jax.ShapeDtypeStruct((len(order), rows // len(order)), jnp.float32),
        ],
        4 * rows * width * DH,
    )


def project_kernel(jobs, n_rows, choices, flag_ref, *refs):
    rows_refs = refs[: 2 * n_rows]
    weight_refs = refs[2 * n_rows : -2]
    sent_ref, kept_ref = refs[-2:]

    def products(index, weight_ref):
        for rows, weight, first in jobs:
            if weight == index:
                columns = pl.ds(first, weight_ref.shape[1])
                kept_rows, sent_rows = rows_refs[2 * rows : 2 * rows + 2]
                sent_ref[:, columns] = jnp.dot(
                    sent_rows[...], weight_ref[...], preferred_element_type=jnp.float32
                ).astype(jnp.bfloat16)
                kept_ref[:, columns] = jnp.dot(
                    kept_rows[...], weight_ref[...], preferred_element_type=jnp.float32
                )

    first = 0
    for index, number in enumerate(choices):
        for k in range(number):
            one = functools.partial(products, index, weight_refs[first + k])
            if number == 1:
                one()
            else:
                pl.when(flag_ref[0] == k)(one)
        first += number


def project(jobs, rows_list, weights, flag):
    flat = [choice for weight in weights for choice in weight]
    choices = tuple(len(weight) for weight in weights)
    placed_jobs, total = [], 0
    for rows, weight in jobs:
        placed_jobs.append((rows, weight, total))
        total += weights[weight][0].shape[1]
    height, depth = rows_list[0][0].shape
    shape = (height, total)
    return local_call(
        functools.partial(project_kernel, tuple(placed_jobs), len(rows_list), choices),
        flag,
        [*[half for pair in rows_list for half in pair], *flat],
        [jax.ShapeDtypeStruct(shape, jnp.bfloat16), jax.ShapeDtypeStruct(shape, jnp.float32)],
        4 * height * depth * total,
    )


def fold_kernel(more, flag_ref, kept_ref, got_ref, *outs):
    if more:
        sent_ref, left_ref = outs
        half = left_ref.shape[0]
        left_ref[...] = kept_ref[:half] + got_ref[:half].astype(jnp.float32)
        sent_ref[...] = (kept_ref[half:] + got_ref[half:].astype(jnp.float32)).astype(jnp.bfloat16)
        return
    first = 0
    for out in outs:
        columns = pl.ds(first, out.shape[1])
        out[...] = (kept_ref[:, columns] + got_ref[:, columns].astype(jnp.float32)).astype(out.dtype)
        first += out.shape[1]


def fold(kept, got, widths=None):
    rows, width = kept.shape
    if widths is None:
        shape = (rows // 2, width)
        outs = [jax.ShapeDtypeStruct(shape, jnp.bfloat16), jax.ShapeDtypeStruct(shape, jnp.float32)]
    else:
        outs = [jax.ShapeDtypeStruct((rows, some), jnp.bfloat16) for some in widths]
    return local_call(functools.partial(fold_kernel, widths is None), scalars(0), [kept, got], outs)


def column(row):
    return jnp.transpose(jnp.broadcast_to(row, (row.shape[1], row.shape[1])))


def scaled_parts(counts, width, starts_ref, squares_ref, pieces, total_width):
    scale = lax.rsqrt(column(squares_ref[...]) / total_width + epsilon)
    where = 0
    for piece, count in zip(pieces, counts):
        for index in range(count):
            for at in range(0, width, DH):
                part = piece[:, pl.ds(index * width + at, DH)].astype(jnp.float32) * scale
                yield part, pl.multiple_of(starts_ref[where] + at, DH)
            where += 1


def placed_kernel(counts, width, total_width, starts_ref, squares_ref, *refs):
    out_ref = refs[-1]
    for part, start in scaled_parts(counts, width, starts_ref, squares_ref, refs[:-1], total_width):
        out_ref[:, pl.ds(start, DH)] = part.astype(out_ref.dtype)


def added_kernel(counts, width, total_width, starts_ref, squares_ref, *refs):
    out_ref, buf, sem = refs[-3:]
    copies = []
    parts = scaled_parts(counts, width, starts_ref, squares_ref, refs[: len(counts)], total_width)
    for at, (part, start) in enumerate(parts):
        buf[at] = part.astype(out_ref.dtype)
        copies.append(pltpu.make_async_copy(buf.at[at], out_ref.at[:, pl.ds(start, DH)], sem.at[at]))
        copies[-1].start()
    for copy in copies:
        copy.wait()


def placed(filled, pieces, squares, width, shape, total_width):
    counts = tuple(len(starts) for _, starts in pieces)
    starts = scalars(*[start for _, own in pieces for start in own])
    operands = [squares] + [piece for piece, _ in pieces]
    out_shape = jax.ShapeDtypeStruct(shape, jnp.bfloat16)
    columns = width * sum(counts)
    if filled is None:
        kernel = functools.partial(placed_kernel, counts, width, total_width)
        return local_call(kernel, starts, operands, [out_shape])[0]
    return pl.pallas_call(
        functools.partial(added_kernel, counts, width, total_width),
        in_specs=[pl.BlockSpec(memory_space=pltpu.SMEM)]
        + [pl.BlockSpec(memory_space=pltpu.VMEM)] * len(operands)
        + [pl.BlockSpec(memory_space=pl.ANY)],
        out_specs=pl.BlockSpec(memory_space=pl.ANY),
        out_shape=out_shape,
        scratch_shapes=[
            pltpu.VMEM((columns // DH, shape[0], DH), jnp.bfloat16),
            pltpu.SemaphoreType.DMA((columns // DH,)),
        ],
        input_output_aliases={len(operands) + 1: 0},
        compiler_params=pltpu.CompilerParams(vmem_limit_bytes=VMEM_BYTES),
        cost_estimate=pl.CostEstimate(
            flops=0, bytes_accessed=4 * shape[0] * columns, transcendentals=0
        ),
    )(starts, *operands, filled)


def shards(queries, key_input, value_input, gate_input, kv_state, norm_gain, out_weight):
    n_seq, n_head = lax.axis_size("seq"), lax.axis_size("head")
    inner = n_seq // LINE
    place, h = lax.axis_index("seq"), lax.axis_index("head")
    z, i = place // inner, place % inner
    tok_rows, local_width = queries.shape
    assert tok_rows == BLOCK
    heads = local_width // DH
    total_width = local_width * n_head
    width = out_weight.shape[1]

    def along(value, hops):
        return lax.ppermute(value, "seq", line_pairs(n_seq, hops))

    terms, stepped = state_prefix(key_input, value_input, n_seq, place)
    some = heads // 2
    inners = [
        causal_part(queries, key_input, value_input, 0, some),
        causal_part(queries, key_input, value_input, some, heads - some),
    ]

    own_columns = hold(out_weight, *stepped)
    w_halves = along(own_columns, SWAP_HALVES)
    w_next = along(hold(own_columns, terms[0]), SWAP_NEXT)
    w_middle = along(own_columns, SWAP_MIDDLE)

    bits = n_head.bit_length() - 1
    order = [int(format(j, "b").zfill(bits)[::-1], 2) for j in range(n_head)] if bits else [0]
    kept_rows, sent_rows, squares = gated_hidden(
        queries, inners, kv_state, terms, gate_input, norm_gain, h, i, order
    )
    rows_list = [(kept_rows, sent_rows)]
    for turn in range(1, inner):
        pairs = turn_pairs(n_seq, turn)
        rows_list.append((lax.ppermute(kept_rows, "seq", pairs), lax.ppermute(sent_rows, "seq", pairs)))

    out_rows = tok_rows // n_head
    half, bit = n_head // 2, 1
    while bit < n_head:
        squares = squares[:half] + lax.ppermute(squares[half:], "head", flip_pairs(n_head, bit))
        half //= 2
        bit *= 2

    is_end = (z == 0) | (z == LINE - 1)
    flag = scalars(is_end)


    owners = [z ^ block for block in range(LINE)]
    blocks = [(out_weight,), (w_next,), (w_halves,)]

    def summed(parts, pins, pin_end=None):
        weights = sorted({block for _, own in parts for block in own})
        jobs = [(p, weights.index(block)) for p, (_, own) in enumerate(parts) for block in own]
        sent, kept = project(
            jobs,
            [rows_list[turn] for turn, _ in parts],
            [blocks[block] for block in weights],
            hold(flag, *pins),
        )
        first_sent, bit = sent, 1
        while bit < n_head:
            got = lax.ppermute(sent, "head", flip_pairs(n_head, bit))
            bit *= 2
            if bit < n_head:
                sent, kept = fold(kept, got)
            else:
                got = got if pin_end is None else hold(got, pin_end)
                kept = fold(kept, got, [width * len(own) for _, own in parts])
        pieces = []
        for piece, (turn, own) in zip(kept, parts):
            if turn:
                piece = lax.ppermute(piece, "seq", turn_pairs(n_seq, -turn))
            starts = [(owners[block] * inner + (i + turn) % inner) * width for block in own]
            pieces.append((piece, starts))
        return pieces, first_sent, got

    turns = list(range(inner))
    shape = (out_rows, width * n_seq)
    in_kernel = width % DH == 0 and out_rows == DH

    pieces, pins, ends = [], [], []

    def group(members, some):
        more, sent, end = summed([(turn, some) for turn in members], pins)
        pieces.extend(more)
        ends.append(end)
        pins[:] = [sent, squares]
        return [piece for piece, _ in more]

    group(turns[:1], [0])
    returned = group(turns[1:], [0]) if inner > 1 else []
    w_ends = along(hold(w_halves, *ends), TO_ENDS)
    blocks.append((w_middle, w_ends))
    for block in (2, 1) if inner > 1 else ():
        returned += group(turns[1:], [block])
    group(turns[:1], [2, 1])
    if in_kernel:
        filled = placed(None, pieces, squares, width, shape, total_width)
        pins.append(filled)
    last, _, _ = summed([(turn, [3]) for turn in turns], [*pins, *ends, *returned])
    if in_kernel:
        return placed(filled, last, squares, width, shape, total_width)
    scale = lax.rsqrt(squares.reshape(out_rows, 1) / total_width + epsilon)
    output = jnp.zeros(shape, jnp.bfloat16)
    for piece, starts in pieces + last:
        piece = (piece.astype(jnp.float32) * scale).astype(jnp.bfloat16)
        for index, start in enumerate(starts):
            part = piece[:, index * width : (index + 1) * width]
            output = lax.dynamic_update_slice_in_dim(output, part, start, 1)
    return output


def solution(mesh):
    in_specs = (
        P("seq", "head"),
        P("seq", "head"),
        P("seq", "head"),
        P("seq", "head"),
        P("head", None, None),
        P(),
        P("head", "seq"),
    )
    out_specs = P(("seq", "head"), None)
    return jax.shard_map(shards, mesh=mesh, in_specs=in_specs, out_specs=out_specs, check_vma=False)
```

```python
import functools

import jax
import jax.numpy as jnp
from jax import lax
from jax.experimental import pallas as pl
from jax.experimental.pallas import tpu as pltpu
from jax.sharding import PartitionSpec as P

DH = 128
BLOCK = 512
LINE = 4
VMEM_BYTES = 16 * 1024 * 1024


epsilon = 1e-05


def line_pairs(n_seq, hops):
    inner = n_seq // LINE
    return [(a * inner + i, b * inner + i) for a, b in hops for i in range(inner)]


def turn_pairs(n_seq, turn):
    inner = n_seq // LINE
    return [(a * inner + i, a * inner + (i + turn) % inner) for a in range(LINE) for i in range(inner)]


def flip_pairs(n_head, bit):
    return [(h, h ^ bit) for h in range(n_head)]


SWAP_NEXT = [(z, z ^ 1) for z in range(LINE)]
SWAP_HALVES = [(z, z ^ 2) for z in range(LINE)]
SWAP_MIDDLE = [(1, 2), (2, 1)]
TO_ENDS = [(1, 0), (2, 3)]


def hold(value, *others):
    return lax.optimization_barrier((value, *others))[0]


def scalars(*values):
    return jnp.stack([jnp.asarray(value, jnp.int32) for value in values])


def local_call(kernel, places, operands, out_shapes, flops=0):
    held = sum(value.size * value.dtype.itemsize for value in [*operands, *out_shapes])
    return pl.pallas_call(
        kernel,
        in_specs=[pl.BlockSpec(memory_space=pltpu.SMEM)]
        + [pl.BlockSpec(memory_space=pltpu.VMEM)] * len(operands),
        out_specs=[pl.BlockSpec(memory_space=pltpu.VMEM)] * len(out_shapes),
        out_shape=out_shapes,
        compiler_params=pltpu.CompilerParams(vmem_limit_bytes=max(VMEM_BYTES, held + held // 2)),
        cost_estimate=pl.CostEstimate(flops=flops, bytes_accessed=held, transcendentals=0),
    )(places, *operands)


def combine_kernel(count, always, masks_ref, *refs):
    values, outs = refs[:count], refs[count:]
    for index in range(values[0].shape[0]):
        total = values[0][index].astype(jnp.float32)
        for value in values[1:always]:
            total = total + value[index].astype(jnp.float32)
        for position, out in enumerate(outs):
            own = total
            for k in range(always, count):
                mask = masks_ref[position * (count - always) + k - always]
                own = own + jnp.where(mask != 0, values[k][index].astype(jnp.float32), 0.0)
            out[index] = own.astype(out.dtype)


def combine(values, dtypes, sometimes=(), masks=None):
    operands = list(values) + list(sometimes)
    masks = scalars(0) if masks is None else scalars(*masks)
    return local_call(
        functools.partial(combine_kernel, len(operands), len(values)),
        masks,
        operands,
        [jax.ShapeDtypeStruct(values[0].shape, dtype) for dtype in dtypes],
    )


def states_kernel(part_ref, k_ref, v_ref, out_ref):
    heads = out_ref.shape[0]
    for index in range(heads):
        columns = pl.ds(pl.multiple_of((part_ref[0] * heads + index) * DH, DH), DH)
        out_ref[index] = lax.dot_general(
            k_ref[:, columns],
            v_ref[:, columns],
            (((0,), (0,)), ((), ())),
            preferred_element_type=jnp.float32,
        ).astype(out_ref.dtype)


def block_states(key_input, value_input, part, heads, dtype):
    return local_call(
        states_kernel,
        scalars(part),
        [key_input, value_input],
        [jax.ShapeDtypeStruct((heads, DH, DH), dtype)],
        2 * key_input.shape[0] * heads * DH * DH,
    )[0]


def state_prefix(key_input, value_input, n_seq, place):
    inner = n_seq // LINE
    i = place % inner
    heads = key_input.shape[1] // DH
    split = heads % inner == 0
    share = heads // inner if split else heads
    if split:
        sends = [
            block_states(key_input, value_input, (i + turn) % inner, share, jnp.bfloat16)
            for turn in range(1, inner)
        ]
        own = block_states(key_input, value_input, i, share, jnp.float32)
    else:
        own = block_states(key_input, value_input, 0, share, jnp.float32)
        sends = [own.astype(jnp.bfloat16)] * (inner - 1)
    values, members = [own], [i]
    for turn in range(1, inner):
        values.append(lax.ppermute(sends[turn - 1], "seq", turn_pairs(n_seq, turn)))
        members.append((i - turn) % inner)
    (first,) = combine(values, [jnp.bfloat16])
    from_pair = lax.ppermute(first, "seq", line_pairs(n_seq, SWAP_NEXT))
    (second,) = combine(values + [from_pair], [jnp.bfloat16])
    from_half = lax.ppermute(second, "seq", line_pairs(n_seq, [(0, 2), (1, 3)]))
    targets = [i] + [(i + turn) % inner for turn in range(1, inner)] if split else [i]
    later = (place // inner) % 2 == 1
    masks = [mask for target in targets for mask in [later] + [owner < target for owner in members]]
    dtypes = [jnp.float32] + [jnp.bfloat16] * (len(targets) - 1)
    befores = combine([from_half], dtypes, [from_pair] + values, masks)
    terms = [befores[0]]
    for turn in range(1, len(targets)):
        terms.append(lax.ppermute(befores[turn], "seq", turn_pairs(n_seq, turn)))
    return terms, from_half


def causal_kernel(first_head, place_ref, q_ref, k_ref, v_ref, out_ref):
    rows = q_ref.shape[0]
    half = rows // 2
    top, bottom = pl.ds(0, half), pl.ds(half, half)
    keep = lax.broadcasted_iota(jnp.int32, (half, half), 0) >= lax.broadcasted_iota(
        jnp.int32, (half, half), 1
    )

    def scores(q_rows, k_rows, columns):
        return lax.dot_general(
            q_ref[q_rows, columns],
            k_ref[k_rows, columns],
            (((1,), (1,)), ((), ())),
            preferred_element_type=jnp.float32,
        )

    for index in range(out_ref.shape[1] // DH):
        columns = pl.ds((first_head + index) * DH, DH)
        placed = pl.ds(index * DH, DH)
        first = jnp.where(keep, scores(top, top, columns), 0.0).astype(jnp.bfloat16)
        below = scores(bottom, top, columns).astype(jnp.bfloat16)
        last = jnp.where(keep, scores(bottom, bottom, columns), 0.0).astype(jnp.bfloat16)
        out_ref[top, placed] = jnp.dot(first, v_ref[top, columns], preferred_element_type=jnp.float32)
        out_ref[bottom, placed] = jnp.dot(
            jnp.concatenate([below, last], axis=1),
            v_ref[:, columns],
            preferred_element_type=jnp.float32,
        )


def causal_part(queries, key_input, value_input, first_head, heads):
    return local_call(
        functools.partial(causal_kernel, first_head),
        scalars(0),
        [queries, key_input, value_input],
        [jax.ShapeDtypeStruct((queries.shape[0], heads * DH), jnp.float32)],
        3 * queries.shape[0] ** 2 * heads * DH,
    )[0]


def hidden_kernel(order, group, calls, place_ref, q_ref, gate_ref, gain_ref, kv_ref, *refs):
    terms, inners = refs[:group], refs[group : group + calls]
    kept_ref, sent_ref, squares_ref = refs[group + calls :]
    half = kept_ref.shape[0]
    heads = kv_ref.shape[0]
    share = heads // group
    size = q_ref.shape[0] // len(order)
    states = []
    for head in range(heads):
        state = kv_ref[head]
        for turn, term in enumerate(terms):
            value = term[head % share].astype(jnp.float32)
            if group > 1:
                covers = lax.rem(place_ref[1] - turn + group, group)
                value = jnp.where(covers == head // share, value, 0.0)
            state = state + value
        high = state.astype(jnp.bfloat16)
        low = (state - high.astype(jnp.float32)).astype(jnp.bfloat16)
        states.append(jnp.concatenate([high, low], axis=0))
    for position, block in enumerate(order):
        start = pl.multiple_of((place_ref[0] ^ block) * size, size)
        rows = pl.ds(start, size)
        hidden_ref = kept_ref if position * size < half else sent_ref
        placed = pl.ds(position * size % half, size)
        squares = jnp.zeros((size, DH), jnp.float32)
        for head in range(heads):
            columns = pl.ds(head * DH, DH)
            q_rows = q_ref[rows, columns]
            carried = jnp.dot(
                jnp.concatenate([q_rows, q_rows], axis=1),
                states[head],
                preferred_element_type=jnp.float32,
            )
            per_call = inners[0].shape[1] // DH
            inner = inners[head // per_call][rows, pl.ds(head % per_call * DH, DH)]
            attn = (carried + inner).astype(jnp.bfloat16).astype(jnp.float32)
            gate = 1.0 + jnp.tanh(gate_ref[rows, columns].astype(jnp.float32) * 0.5)
            gain = gain_ref[place_ref[0] * heads + head] * 0.5
            hidden_ref[placed, columns] = (attn * (gain * gate)).astype(jnp.bfloat16)
            squares = squares + attn * attn
        squares_ref[pl.ds(position, 1), :] = jnp.sum(jnp.transpose(squares), axis=0, keepdims=True)


def gated_hidden(queries, inners, kv_state, terms, gate_input, norm_gain, h, i, order):
    rows, width = queries.shape
    half = jax.ShapeDtypeStruct((rows // 2, width), jnp.bfloat16)
    return local_call(
        functools.partial(hidden_kernel, order, len(terms), len(inners)),
        scalars(h, i),
        [queries, gate_input, norm_gain.reshape(-1, 1, DH), kv_state, *terms, *inners],
        [
            half,
            half,
            jax.ShapeDtypeStruct((len(order), rows // len(order)), jnp.float32),
        ],
        4 * rows * width * DH,
    )


def project_kernel(jobs, n_rows, choices, flag_ref, *refs):
    rows_refs = refs[: 2 * n_rows]
    weight_refs = refs[2 * n_rows : -2]
    sent_ref, kept_ref = refs[-2:]

    def products(index, weight_ref):
        for rows, weight, first in jobs:
            if weight == index:
                columns = pl.ds(first, weight_ref.shape[1])
                kept_rows, sent_rows = rows_refs[2 * rows : 2 * rows + 2]
                sent_ref[:, columns] = jnp.dot(
                    sent_rows[...], weight_ref[...], preferred_element_type=jnp.float32
                ).astype(jnp.bfloat16)
                kept_ref[:, columns] = jnp.dot(
                    kept_rows[...], weight_ref[...], preferred_element_type=jnp.float32
                )

    first = 0
    for index, number in enumerate(choices):
        for k in range(number):
            one = functools.partial(products, index, weight_refs[first + k])
            if number == 1:
                one()
            else:
                pl.when(flag_ref[0] == k)(one)
        first += number


def project(jobs, rows_list, weights, flag):
    flat = [choice for weight in weights for choice in weight]
    choices = tuple(len(weight) for weight in weights)
    placed_jobs, total = [], 0
    for rows, weight in jobs:
        placed_jobs.append((rows, weight, total))
        total += weights[weight][0].shape[1]
    height, depth = rows_list[0][0].shape
    shape = (height, total)
    return local_call(
        functools.partial(project_kernel, tuple(placed_jobs), len(rows_list), choices),
        flag,
        [*[half for pair in rows_list for half in pair], *flat],
        [jax.ShapeDtypeStruct(shape, jnp.bfloat16), jax.ShapeDtypeStruct(shape, jnp.float32)],
        4 * height * depth * total,
    )


def fold_kernel(more, flag_ref, kept_ref, got_ref, *outs):
    if more:
        sent_ref, left_ref = outs
        half = left_ref.shape[0]
        left_ref[...] = kept_ref[:half] + got_ref[:half].astype(jnp.float32)
        sent_ref[...] = (kept_ref[half:] + got_ref[half:].astype(jnp.float32)).astype(jnp.bfloat16)
        return
    first = 0
    for out in outs:
        columns = pl.ds(first, out.shape[1])
        out[...] = (kept_ref[:, columns] + got_ref[:, columns].astype(jnp.float32)).astype(out.dtype)
        first += out.shape[1]


def fold(kept, got, widths=None):
    rows, width = kept.shape
    if widths is None:
        shape = (rows // 2, width)
        outs = [jax.ShapeDtypeStruct(shape, jnp.bfloat16), jax.ShapeDtypeStruct(shape, jnp.float32)]
    else:
        outs = [jax.ShapeDtypeStruct((rows, some), jnp.bfloat16) for some in widths]
    return local_call(functools.partial(fold_kernel, widths is None), scalars(0), [kept, got], outs)


def column(row):
    return jnp.transpose(jnp.broadcast_to(row, (row.shape[1], row.shape[1])))


def scaled_parts(counts, width, starts_ref, squares_ref, pieces, total_width):
    scale = lax.rsqrt(column(squares_ref[...]) / total_width + epsilon)
    where = 0
    for piece, count in zip(pieces, counts):
        for index in range(count):
            for at in range(0, width, DH):
                part = piece[:, pl.ds(index * width + at, DH)].astype(jnp.float32) * scale
                yield part, pl.multiple_of(starts_ref[where] + at, DH)
            where += 1


def placed_kernel(counts, width, total_width, starts_ref, squares_ref, *refs):
    out_ref = refs[-1]
    for part, start in scaled_parts(counts, width, starts_ref, squares_ref, refs[:-1], total_width):
        out_ref[:, pl.ds(start, DH)] = part.astype(out_ref.dtype)


def added_kernel(counts, width, total_width, starts_ref, squares_ref, *refs):
    out_ref, buf, sem = refs[-3:]
    copies = []
    parts = scaled_parts(counts, width, starts_ref, squares_ref, refs[: len(counts)], total_width)
    for at, (part, start) in enumerate(parts):
        buf[at] = part.astype(out_ref.dtype)
        copies.append(pltpu.make_async_copy(buf.at[at], out_ref.at[:, pl.ds(start, DH)], sem.at[at]))
        copies[-1].start()
    for copy in copies:
        copy.wait()


def placed(filled, pieces, squares, width, shape, total_width):
    counts = tuple(len(starts) for _, starts in pieces)
    starts = scalars(*[start for _, own in pieces for start in own])
    operands = [squares] + [piece for piece, _ in pieces]
    out_shape = jax.ShapeDtypeStruct(shape, jnp.bfloat16)
    columns = width * sum(counts)
    if filled is None:
        kernel = functools.partial(placed_kernel, counts, width, total_width)
        return local_call(kernel, starts, operands, [out_shape])[0]
    return pl.pallas_call(
        functools.partial(added_kernel, counts, width, total_width),
        in_specs=[pl.BlockSpec(memory_space=pltpu.SMEM)]
        + [pl.BlockSpec(memory_space=pltpu.VMEM)] * len(operands)
        + [pl.BlockSpec(memory_space=pl.ANY)],
        out_specs=pl.BlockSpec(memory_space=pl.ANY),
        out_shape=out_shape,
        scratch_shapes=[
            pltpu.VMEM((columns // DH, shape[0], DH), jnp.bfloat16),
            pltpu.SemaphoreType.DMA((columns // DH,)),
        ],
        input_output_aliases={len(operands) + 1: 0},
        compiler_params=pltpu.CompilerParams(vmem_limit_bytes=VMEM_BYTES),
        cost_estimate=pl.CostEstimate(
            flops=0, bytes_accessed=4 * shape[0] * columns, transcendentals=0
        ),
    )(starts, *operands, filled)


def shards(queries, key_input, value_input, gate_input, kv_state, norm_gain, out_weight):
    n_seq, n_head = lax.axis_size("seq"), lax.axis_size("head")
    inner = n_seq // LINE
    place, h = lax.axis_index("seq"), lax.axis_index("head")
    z, i = place // inner, place % inner
    tok_rows, local_width = queries.shape
    assert tok_rows == BLOCK
    heads = local_width // DH
    total_width = local_width * n_head
    width = out_weight.shape[1]

    def along(value, hops):
        return lax.ppermute(value, "seq", line_pairs(n_seq, hops))

    terms, stepped = state_prefix(key_input, value_input, n_seq, place)
    some = heads // 2
    inners = [
        causal_part(queries, key_input, value_input, 0, some),
        causal_part(queries, key_input, value_input, some, heads - some),
    ]

    own_columns = hold(out_weight, stepped)
    w_halves = along(own_columns, SWAP_HALVES)
    w_next = along(own_columns, SWAP_NEXT)
    w_middle = along(own_columns, SWAP_MIDDLE)

    bits = n_head.bit_length() - 1
    order = [int(format(j, "b").zfill(bits)[::-1], 2) for j in range(n_head)] if bits else [0]
    kept_rows, sent_rows, squares = gated_hidden(
        queries, inners, kv_state, terms, gate_input, norm_gain, h, i, order
    )
    rows_list = [(kept_rows, sent_rows)]
    for turn in range(1, inner):
        pairs = turn_pairs(n_seq, turn)
        rows_list.append((lax.ppermute(kept_rows, "seq", pairs), lax.ppermute(sent_rows, "seq", pairs)))

    out_rows = tok_rows // n_head
    half, bit = n_head // 2, 1
    while bit < n_head:
        squares = squares[:half] + lax.ppermute(squares[half:], "head", flip_pairs(n_head, bit))
        half //= 2
        bit *= 2

    is_end = (z == 0) | (z == LINE - 1)
    flag = scalars(is_end)


    owners = [z ^ block for block in range(LINE)]
    blocks = [(out_weight,), (w_next,), (w_halves,)]

    def summed(parts, pins):
        weights = sorted({block for _, own in parts for block in own})
        jobs = [(p, weights.index(block)) for p, (_, own) in enumerate(parts) for block in own]
        sent, kept = project(
            jobs,
            [rows_list[turn] for turn, _ in parts],
            [blocks[block] for block in weights],
            hold(flag, *pins),
        )
        first_sent, bit = sent, 1
        while bit < n_head:
            got = lax.ppermute(sent, "head", flip_pairs(n_head, bit))
            bit *= 2
            if bit < n_head:
                sent, kept = fold(kept, got)
            else:
                kept = fold(kept, got, [width * len(own) for _, own in parts])
        pieces = []
        for piece, (turn, own) in zip(kept, parts):
            if turn:
                piece = lax.ppermute(piece, "seq", turn_pairs(n_seq, -turn))
            starts = [(owners[block] * inner + (i + turn) % inner) * width for block in own]
            pieces.append((piece, starts))
        return pieces, first_sent, got

    turns = list(range(inner))
    shape = (out_rows, width * n_seq)
    in_kernel = width % DH == 0 and out_rows == DH

    pieces, pins, ends = [], [], []

    def group(members, some):
        more, sent, end = summed([(turn, some) for turn in members], pins)
        pieces.extend(more)
        ends.append(end)
        pins[:] = [sent, squares]
        return [piece for piece, _ in more]

    group(turns[:1], [0])
    returned = group(turns[1:], [0]) if inner > 1 else []
    w_ends = along(hold(w_halves, *ends), TO_ENDS)
    blocks.append((w_middle, w_ends))
    group(turns[:1], [1, 2])
    if inner > 1:
        group(turns[1:], [1, 2])
    filled = placed(None, pieces, squares, width, shape, total_width) if in_kernel else None
    last, _, _ = summed(
        [(turn, [3]) for turn in turns], [*pins, *ends, *returned]
    )
    if in_kernel:
        return placed(filled, last, squares, width, shape, total_width)
    scale = lax.rsqrt(squares.reshape(out_rows, 1) / total_width + epsilon)
    output = jnp.zeros(shape, jnp.bfloat16)
    for piece, starts in pieces + last:
        piece = (piece.astype(jnp.float32) * scale).astype(jnp.bfloat16)
        for index, start in enumerate(starts):
            part = piece[:, index * width : (index + 1) * width]
            output = lax.dynamic_update_slice_in_dim(output, part, start, 1)
    return output


def solution(mesh):
    in_specs = (
        P("seq", "head"),
        P("seq", "head"),
        P("seq", "head"),
        P("seq", "head"),
        P("head", None, None),
        P(),
        P("head", "seq"),
    )
    out_specs = P(("seq", "head"), None)
    return jax.shard_map(shards, mesh=mesh, in_specs=in_specs, out_specs=out_specs, check_vma=False)
```

```python
import functools

import jax
import jax.numpy as jnp
from jax import lax
from jax.experimental import pallas as pl
from jax.experimental.pallas import tpu as pltpu
from jax.sharding import PartitionSpec as P

DH = 128
BLOCK = 512
LINE = 4
VMEM_BYTES = 16 * 1024 * 1024


epsilon = 1e-05


def line_pairs(n_seq, hops):
    inner = n_seq // LINE
    return [(a * inner + i, b * inner + i) for a, b in hops for i in range(inner)]


def turn_pairs(n_seq, turn):
    inner = n_seq // LINE
    return [(a * inner + i, a * inner + (i + turn) % inner) for a in range(LINE) for i in range(inner)]


def flip_pairs(n_head, bit):
    return [(h, h ^ bit) for h in range(n_head)]


SWAP_NEXT = [(z, z ^ 1) for z in range(LINE)]
SWAP_HALVES = [(z, z ^ 2) for z in range(LINE)]
SWAP_MIDDLE = [(1, 2), (2, 1)]
TO_ENDS = [(1, 0), (2, 3)]


def hold(value, *others):
    return lax.optimization_barrier((value, *others))[0]


def scalars(*values):
    return jnp.stack([jnp.asarray(value, jnp.int32) for value in values])


def local_call(kernel, places, operands, out_shapes, flops=0):
    held = sum(value.size * value.dtype.itemsize for value in [*operands, *out_shapes])
    return pl.pallas_call(
        kernel,
        in_specs=[pl.BlockSpec(memory_space=pltpu.SMEM)]
        + [pl.BlockSpec(memory_space=pltpu.VMEM)] * len(operands),
        out_specs=[pl.BlockSpec(memory_space=pltpu.VMEM)] * len(out_shapes),
        out_shape=out_shapes,
        compiler_params=pltpu.CompilerParams(vmem_limit_bytes=max(VMEM_BYTES, held + held // 2)),
        cost_estimate=pl.CostEstimate(flops=flops, bytes_accessed=held, transcendentals=0),
    )(places, *operands)


def combine_kernel(count, always, masks_ref, *refs):
    values, outs = refs[:count], refs[count:]
    for index in range(values[0].shape[0]):
        total = values[0][index].astype(jnp.float32)
        for value in values[1:always]:
            total = total + value[index].astype(jnp.float32)
        for position, out in enumerate(outs):
            own = total
            for k in range(always, count):
                mask = masks_ref[position * (count - always) + k - always]
                own = own + jnp.where(mask != 0, values[k][index].astype(jnp.float32), 0.0)
            out[index] = own.astype(out.dtype)


def combine(values, dtypes, sometimes=(), masks=None):
    operands = list(values) + list(sometimes)
    masks = scalars(0) if masks is None else scalars(*masks)
    return local_call(
        functools.partial(combine_kernel, len(operands), len(values)),
        masks,
        operands,
        [jax.ShapeDtypeStruct(values[0].shape, dtype) for dtype in dtypes],
    )


def states_kernel(part_ref, k_ref, v_ref, out_ref):
    heads = out_ref.shape[0]
    for index in range(heads):
        columns = pl.ds(pl.multiple_of((part_ref[0] * heads + index) * DH, DH), DH)
        out_ref[index] = lax.dot_general(
            k_ref[:, columns],
            v_ref[:, columns],
            (((0,), (0,)), ((), ())),
            preferred_element_type=jnp.float32,
        ).astype(out_ref.dtype)


def block_states(key_input, value_input, part, heads, dtype):
    return local_call(
        states_kernel,
        scalars(part),
        [key_input, value_input],
        [jax.ShapeDtypeStruct((heads, DH, DH), dtype)],
        2 * key_input.shape[0] * heads * DH * DH,
    )[0]


def state_prefix(key_input, value_input, n_seq, place, beside):
    inner = n_seq // LINE
    i = place % inner
    heads = key_input.shape[1] // DH
    split = heads % inner == 0
    share = heads // inner if split else heads
    if split:
        sends = [
            block_states(key_input, value_input, (i + turn) % inner, share, jnp.bfloat16)
            for turn in range(1, inner)
        ]
        own = block_states(key_input, value_input, i, share, jnp.float32)
    else:
        own = block_states(key_input, value_input, 0, share, jnp.float32)
        sends = [own.astype(jnp.bfloat16)] * (inner - 1)
    values, members = [own], [i]
    for turn in range(1, inner):
        values.append(lax.ppermute(sends[turn - 1], "seq", turn_pairs(n_seq, turn)))
        members.append((i - turn) % inner)
    (first,) = combine(values, [jnp.bfloat16])
    from_pair = lax.ppermute(first, "seq", line_pairs(n_seq, SWAP_NEXT))
    (second,) = combine(values + [from_pair], [jnp.bfloat16])
    from_half = lax.ppermute(second, "seq", line_pairs(n_seq, [(0, 2), (1, 3)]))
    targets = [i] + [(i + turn) % inner for turn in range(1, inner)] if split else [i]
    later = (place // inner) % 2 == 1
    masks = [mask for target in targets for mask in [later] + [owner < target for owner in members]]
    dtypes = [jnp.float32] + [jnp.bfloat16] * (len(targets) - 1)
    befores = combine([hold(from_half, *beside)], dtypes, [from_pair] + values, masks)
    terms = [befores[0]]
    for turn in range(1, len(targets)):
        terms.append(lax.ppermute(befores[turn], "seq", turn_pairs(n_seq, turn)))
    return terms, from_half


def causal_kernel(first_head, place_ref, q_ref, k_ref, v_ref, out_ref):
    rows = q_ref.shape[0]
    half = rows // 2
    top, bottom = pl.ds(0, half), pl.ds(half, half)
    keep = lax.broadcasted_iota(jnp.int32, (half, half), 0) >= lax.broadcasted_iota(
        jnp.int32, (half, half), 1
    )

    def scores(q_rows, k_rows, columns):
        return lax.dot_general(
            q_ref[q_rows, columns],
            k_ref[k_rows, columns],
            (((1,), (1,)), ((), ())),
            preferred_element_type=jnp.float32,
        )

    for index in range(out_ref.shape[1] // DH):
        columns = pl.ds((first_head + index) * DH, DH)
        placed = pl.ds(index * DH, DH)
        first = jnp.where(keep, scores(top, top, columns), 0.0).astype(jnp.bfloat16)
        below = scores(bottom, top, columns).astype(jnp.bfloat16)
        last = jnp.where(keep, scores(bottom, bottom, columns), 0.0).astype(jnp.bfloat16)
        out_ref[top, placed] = jnp.dot(first, v_ref[top, columns], preferred_element_type=jnp.float32)
        out_ref[bottom, placed] = jnp.dot(
            jnp.concatenate([below, last], axis=1),
            v_ref[:, columns],
            preferred_element_type=jnp.float32,
        )


def causal_part(queries, key_input, value_input, first_head, heads):
    return local_call(
        functools.partial(causal_kernel, first_head),
        scalars(0),
        [queries, key_input, value_input],
        [jax.ShapeDtypeStruct((queries.shape[0], heads * DH), jnp.float32)],
        3 * queries.shape[0] ** 2 * heads * DH,
    )[0]


def hidden_kernel(order, group, calls, place_ref, q_ref, gate_ref, gain_ref, kv_ref, *refs):
    terms, inners = refs[:group], refs[group : group + calls]
    kept_ref, sent_ref, squares_ref = refs[group + calls :]
    half = kept_ref.shape[0]
    heads = kv_ref.shape[0]
    share = heads // group
    size = q_ref.shape[0] // len(order)
    states = []
    for head in range(heads):
        state = kv_ref[head]
        for turn, term in enumerate(terms):
            value = term[head % share].astype(jnp.float32)
            if group > 1:
                covers = lax.rem(place_ref[1] - turn + group, group)
                value = jnp.where(covers == head // share, value, 0.0)
            state = state + value
        high = state.astype(jnp.bfloat16)
        low = (state - high.astype(jnp.float32)).astype(jnp.bfloat16)
        states.append(jnp.concatenate([high, low], axis=0))
    for position, block in enumerate(order):
        start = pl.multiple_of((place_ref[0] ^ block) * size, size)
        rows = pl.ds(start, size)
        hidden_ref = kept_ref if position * size < half else sent_ref
        placed = pl.ds(position * size % half, size)
        squares = jnp.zeros((size, DH), jnp.float32)
        for head in range(heads):
            columns = pl.ds(head * DH, DH)
            q_rows = q_ref[rows, columns]
            carried = jnp.dot(
                jnp.concatenate([q_rows, q_rows], axis=1),
                states[head],
                preferred_element_type=jnp.float32,
            )
            per_call = inners[0].shape[1] // DH
            inner = inners[head // per_call][rows, pl.ds(head % per_call * DH, DH)]
            attn = (carried + inner).astype(jnp.bfloat16).astype(jnp.float32)
            gate = 1.0 + jnp.tanh(gate_ref[rows, columns].astype(jnp.float32) * 0.5)
            gain = gain_ref[place_ref[0] * heads + head] * 0.5
            hidden_ref[placed, columns] = (attn * (gain * gate)).astype(jnp.bfloat16)
            squares = squares + attn * attn
        squares_ref[pl.ds(position, 1), :] = jnp.sum(jnp.transpose(squares), axis=0, keepdims=True)


def gated_hidden(queries, inners, kv_state, terms, gate_input, norm_gain, h, i, order):
    rows, width = queries.shape
    half = jax.ShapeDtypeStruct((rows // 2, width), jnp.bfloat16)
    return local_call(
        functools.partial(hidden_kernel, order, len(terms), len(inners)),
        scalars(h, i),
        [queries, gate_input, norm_gain.reshape(-1, 1, DH), kv_state, *terms, *inners],
        [
            half,
            half,
            jax.ShapeDtypeStruct((len(order), rows // len(order)), jnp.float32),
        ],
        4 * rows * width * DH,
    )


def project_kernel(jobs, n_rows, choices, flag_ref, *refs):
    rows_refs = refs[: 2 * n_rows]
    weight_refs = refs[2 * n_rows : -2]
    sent_ref, kept_ref = refs[-2:]

    def products(index, weight_ref):
        for rows, weight, first in jobs:
            if weight == index:
                columns = pl.ds(first, weight_ref.shape[1])
                kept_rows, sent_rows = rows_refs[2 * rows : 2 * rows + 2]
                sent_ref[:, columns] = jnp.dot(
                    sent_rows[...], weight_ref[...], preferred_element_type=jnp.float32
                ).astype(jnp.bfloat16)
                kept_ref[:, columns] = jnp.dot(
                    kept_rows[...], weight_ref[...], preferred_element_type=jnp.float32
                )

    first = 0
    for index, number in enumerate(choices):
        for k in range(number):
            one = functools.partial(products, index, weight_refs[first + k])
            if number == 1:
                one()
            else:
                pl.when(flag_ref[0] == k)(one)
        first += number


def project(jobs, rows_list, weights, flag):
    flat = [choice for weight in weights for choice in weight]
    choices = tuple(len(weight) for weight in weights)
    placed_jobs, total = [], 0
    for rows, weight in jobs:
        placed_jobs.append((rows, weight, total))
        total += weights[weight][0].shape[1]
    height, depth = rows_list[0][0].shape
    shape = (height, total)
    return local_call(
        functools.partial(project_kernel, tuple(placed_jobs), len(rows_list), choices),
        flag,
        [*[half for pair in rows_list for half in pair], *flat],
        [jax.ShapeDtypeStruct(shape, jnp.bfloat16), jax.ShapeDtypeStruct(shape, jnp.float32)],
        4 * height * depth * total,
    )


def fold_kernel(more, flag_ref, kept_ref, got_ref, *outs):
    if more:
        sent_ref, left_ref = outs
        half = left_ref.shape[0]
        left_ref[...] = kept_ref[:half] + got_ref[:half].astype(jnp.float32)
        sent_ref[...] = (kept_ref[half:] + got_ref[half:].astype(jnp.float32)).astype(jnp.bfloat16)
        return
    first = 0
    for out in outs:
        columns = pl.ds(first, out.shape[1])
        out[...] = (kept_ref[:, columns] + got_ref[:, columns].astype(jnp.float32)).astype(out.dtype)
        first += out.shape[1]


def fold(kept, got, widths=None):
    rows, width = kept.shape
    if widths is None:
        shape = (rows // 2, width)
        outs = [jax.ShapeDtypeStruct(shape, jnp.bfloat16), jax.ShapeDtypeStruct(shape, jnp.float32)]
    else:
        outs = [jax.ShapeDtypeStruct((rows, some), jnp.bfloat16) for some in widths]
    return local_call(functools.partial(fold_kernel, widths is None), scalars(0), [kept, got], outs)


def column(row):
    return jnp.transpose(jnp.broadcast_to(row, (row.shape[1], row.shape[1])))


def scaled_parts(counts, width, starts_ref, squares_ref, pieces, total_width):
    scale = lax.rsqrt(column(squares_ref[...]) / total_width + epsilon)
    where = 0
    for piece, count in zip(pieces, counts):
        for index in range(count):
            for at in range(0, width, DH):
                part = piece[:, pl.ds(index * width + at, DH)].astype(jnp.float32) * scale
                yield part, pl.multiple_of(starts_ref[where] + at, DH)
            where += 1


def placed_kernel(counts, width, total_width, starts_ref, squares_ref, *refs):
    out_ref = refs[-1]
    for part, start in scaled_parts(counts, width, starts_ref, squares_ref, refs[:-1], total_width):
        out_ref[:, pl.ds(start, DH)] = part.astype(out_ref.dtype)


def added_kernel(counts, width, total_width, starts_ref, squares_ref, *refs):
    out_ref, buf, sem = refs[-3:]
    copies = []
    parts = scaled_parts(counts, width, starts_ref, squares_ref, refs[: len(counts)], total_width)
    for at, (part, start) in enumerate(parts):
        buf[at] = part.astype(out_ref.dtype)
        copies.append(pltpu.make_async_copy(buf.at[at], out_ref.at[:, pl.ds(start, DH)], sem.at[at]))
        copies[-1].start()
    for copy in copies:
        copy.wait()


def placed(filled, pieces, squares, width, shape, total_width):
    counts = tuple(len(starts) for _, starts in pieces)
    starts = scalars(*[start for _, own in pieces for start in own])
    operands = [squares] + [piece for piece, _ in pieces]
    out_shape = jax.ShapeDtypeStruct(shape, jnp.bfloat16)
    columns = width * sum(counts)
    if filled is None:
        kernel = functools.partial(placed_kernel, counts, width, total_width)
        return local_call(kernel, starts, operands, [out_shape])[0]
    return pl.pallas_call(
        functools.partial(added_kernel, counts, width, total_width),
        in_specs=[pl.BlockSpec(memory_space=pltpu.SMEM)]
        + [pl.BlockSpec(memory_space=pltpu.VMEM)] * len(operands)
        + [pl.BlockSpec(memory_space=pl.ANY)],
        out_specs=pl.BlockSpec(memory_space=pl.ANY),
        out_shape=out_shape,
        scratch_shapes=[
            pltpu.VMEM((columns // DH, shape[0], DH), jnp.bfloat16),
            pltpu.SemaphoreType.DMA((columns // DH,)),
        ],
        input_output_aliases={len(operands) + 1: 0},
        compiler_params=pltpu.CompilerParams(vmem_limit_bytes=VMEM_BYTES),
        cost_estimate=pl.CostEstimate(
            flops=0, bytes_accessed=4 * shape[0] * columns, transcendentals=0
        ),
    )(starts, *operands, filled)


def shards(queries, key_input, value_input, gate_input, kv_state, norm_gain, out_weight):
    n_seq, n_head = lax.axis_size("seq"), lax.axis_size("head")
    inner = n_seq // LINE
    place, h = lax.axis_index("seq"), lax.axis_index("head")
    z, i = place // inner, place % inner
    tok_rows, local_width = queries.shape
    assert tok_rows == BLOCK
    heads = local_width // DH
    total_width = local_width * n_head
    width = out_weight.shape[1]

    def along(value, hops):
        return lax.ppermute(value, "seq", line_pairs(n_seq, hops))

    some = heads // 2
    inners = [
        causal_part(queries, key_input, value_input, 0, some),
        causal_part(queries, key_input, value_input, some, heads - some),
    ]
    terms, stepped = state_prefix(key_input, value_input, n_seq, place, inners)

    own_columns = hold(out_weight, stepped)
    w_halves = along(own_columns, SWAP_HALVES)
    w_next = along(own_columns, SWAP_NEXT)
    w_middle = along(own_columns, SWAP_MIDDLE)

    bits = n_head.bit_length() - 1
    order = [int(format(j, "b").zfill(bits)[::-1], 2) for j in range(n_head)] if bits else [0]
    kept_rows, sent_rows, squares = gated_hidden(
        queries, inners, kv_state, terms, gate_input, norm_gain, h, i, order
    )
    rows_list = [(kept_rows, sent_rows)]
    for turn in range(1, inner):
        pairs = turn_pairs(n_seq, turn)
        rows_list.append((lax.ppermute(kept_rows, "seq", pairs), lax.ppermute(sent_rows, "seq", pairs)))

    out_rows = tok_rows // n_head
    half, bit = n_head // 2, 1
    while bit < n_head:
        squares = squares[:half] + lax.ppermute(squares[half:], "head", flip_pairs(n_head, bit))
        half //= 2
        bit *= 2

    is_end = (z == 0) | (z == LINE - 1)
    flag = scalars(is_end)


    owners = [z ^ block for block in range(LINE)]
    blocks = [(out_weight,), (w_next,), (w_halves,)]

    def summed(parts, pins):
        weights = sorted({block for _, own in parts for block in own})
        jobs = [(p, weights.index(block)) for p, (_, own) in enumerate(parts) for block in own]
        sent, kept = project(
            jobs,
            [rows_list[turn] for turn, _ in parts],
            [blocks[block] for block in weights],
            hold(flag, *pins),
        )
        first_sent, steps, bit = sent, [], 1
        while bit < n_head:
            got = lax.ppermute(sent, "head", flip_pairs(n_head, bit))
            steps.append(got)
            bit *= 2
            if bit < n_head:
                sent, kept = fold(kept, got)
            else:
                kept = fold(kept, got, [width * len(own) for _, own in parts])
        pieces = []
        for piece, (turn, own) in zip(kept, parts):
            if turn:
                piece = lax.ppermute(piece, "seq", turn_pairs(n_seq, -turn))
            starts = [(owners[block] * inner + (i + turn) % inner) * width for block in own]
            pieces.append((piece, starts))
        return pieces, first_sent, steps

    turns = list(range(inner))
    shape = (out_rows, width * n_seq)
    in_kernel = width % DH == 0 and out_rows == DH

    pieces, pins, firsts, ends = [], [], [], []

    def group(members, some):
        more, sent, steps = summed([(turn, some) for turn in members], pins)
        pieces.extend(more)
        firsts.append(steps[0])
        ends.append(steps[-1])
        pins[:] = [sent, squares]
        return [piece for piece, _ in more]

    group(turns[:1], [0])
    returned = group(turns[1:], [0]) if inner > 1 else []
    w_ends = along(hold(w_halves, ends[0], *firsts), TO_ENDS)
    blocks.append((w_middle, w_ends))
    group(turns[:1], [1, 2])
    if inner > 1:
        group(turns[1:], [1, 2])
    filled = placed(None, pieces, squares, width, shape, total_width) if in_kernel else None
    last, _, _ = summed(
        [(turn, [3]) for turn in turns], [*pins, *ends, *returned]
    )
    if in_kernel:
        return placed(filled, last, squares, width, shape, total_width)
    scale = lax.rsqrt(squares.reshape(out_rows, 1) / total_width + epsilon)
    output = jnp.zeros(shape, jnp.bfloat16)
    for piece, starts in pieces + last:
        piece = (piece.astype(jnp.float32) * scale).astype(jnp.bfloat16)
        for index, start in enumerate(starts):
            part = piece[:, index * width : (index + 1) * width]
            output = lax.dynamic_update_slice_in_dim(output, part, start, 1)
    return output


def solution(mesh):
    in_specs = (
        P("seq", "head"),
        P("seq", "head"),
        P("seq", "head"),
        P("seq", "head"),
        P("head", None, None),
        P(),
        P("head", "seq"),
    )
    out_specs = P(("seq", "head"), None)
    return jax.shard_map(shards, mesh=mesh, in_specs=in_specs, out_specs=out_specs, check_vma=False)
```

```python
import functools

import jax
import jax.numpy as jnp
from jax import lax
from jax.experimental import pallas as pl
from jax.experimental.pallas import tpu as pltpu
from jax.sharding import PartitionSpec as P

DH = 128
BLOCK = 512
LINE = 4
VMEM_BYTES = 16 * 1024 * 1024


epsilon = 1e-05


def line_pairs(n_seq, hops):
    inner = n_seq // LINE
    return [(a * inner + i, b * inner + i) for a, b in hops for i in range(inner)]


def turn_pairs(n_seq, turn):
    inner = n_seq // LINE
    return [(a * inner + i, a * inner + (i + turn) % inner) for a in range(LINE) for i in range(inner)]


def flip_pairs(n_head, bit):
    return [(h, h ^ bit) for h in range(n_head)]


SWAP_NEXT = [(z, z ^ 1) for z in range(LINE)]
SWAP_HALVES = [(z, z ^ 2) for z in range(LINE)]
SWAP_MIDDLE = [(1, 2), (2, 1)]
TO_ENDS = [(1, 0), (2, 3)]


def hold(value, *others):
    return lax.optimization_barrier((value, *others))[0]


def scalars(*values):
    return jnp.stack([jnp.asarray(value, jnp.int32) for value in values])


def local_call(kernel, places, operands, out_shapes, flops=0):
    held = sum(value.size * value.dtype.itemsize for value in [*operands, *out_shapes])
    return pl.pallas_call(
        kernel,
        in_specs=[pl.BlockSpec(memory_space=pltpu.SMEM)]
        + [pl.BlockSpec(memory_space=pltpu.VMEM)] * len(operands),
        out_specs=[pl.BlockSpec(memory_space=pltpu.VMEM)] * len(out_shapes),
        out_shape=out_shapes,
        compiler_params=pltpu.CompilerParams(vmem_limit_bytes=max(VMEM_BYTES, held + held // 2)),
        cost_estimate=pl.CostEstimate(flops=flops, bytes_accessed=held, transcendentals=0),
    )(places, *operands)


def combine_kernel(count, always, masks_ref, *refs):
    values, outs = refs[:count], refs[count:]
    for index in range(values[0].shape[0]):
        total = values[0][index].astype(jnp.float32)
        for value in values[1:always]:
            total = total + value[index].astype(jnp.float32)
        for position, out in enumerate(outs):
            own = total
            for k in range(always, count):
                mask = masks_ref[position * (count - always) + k - always]
                own = own + jnp.where(mask != 0, values[k][index].astype(jnp.float32), 0.0)
            out[index] = own.astype(out.dtype)


def combine(values, dtypes, sometimes=(), masks=None):
    operands = list(values) + list(sometimes)
    masks = scalars(0) if masks is None else scalars(*masks)
    return local_call(
        functools.partial(combine_kernel, len(operands), len(values)),
        masks,
        operands,
        [jax.ShapeDtypeStruct(values[0].shape, dtype) for dtype in dtypes],
    )


def states_kernel(part_ref, k_ref, v_ref, out_ref):
    heads = out_ref.shape[0]
    for index in range(heads):
        columns = pl.ds(pl.multiple_of((part_ref[0] * heads + index) * DH, DH), DH)
        out_ref[index] = lax.dot_general(
            k_ref[:, columns],
            v_ref[:, columns],
            (((0,), (0,)), ((), ())),
            preferred_element_type=jnp.float32,
        ).astype(out_ref.dtype)


def block_states(key_input, value_input, part, heads, dtype):
    return local_call(
        states_kernel,
        scalars(part),
        [key_input, value_input],
        [jax.ShapeDtypeStruct((heads, DH, DH), dtype)],
        2 * key_input.shape[0] * heads * DH * DH,
    )[0]


def state_prefix(key_input, value_input, n_seq, place, beside):
    inner = n_seq // LINE
    i = place % inner
    heads = key_input.shape[1] // DH
    split = heads % inner == 0
    share = heads // inner if split else heads
    if split:
        sends = [
            block_states(key_input, value_input, (i + turn) % inner, share, jnp.bfloat16)
            for turn in range(1, inner)
        ]
        own = block_states(key_input, value_input, i, share, jnp.float32)
    else:
        own = block_states(key_input, value_input, 0, share, jnp.float32)
        sends = [own.astype(jnp.bfloat16)] * (inner - 1)
    values, members = [own], [i]
    for turn in range(1, inner):
        values.append(lax.ppermute(sends[turn - 1], "seq", turn_pairs(n_seq, turn)))
        members.append((i - turn) % inner)
    (first,) = combine(values, [jnp.bfloat16])
    from_pair = lax.ppermute(first, "seq", line_pairs(n_seq, SWAP_NEXT))
    (second,) = combine(values + [from_pair], [jnp.bfloat16])
    from_half = lax.ppermute(second, "seq", line_pairs(n_seq, [(0, 2), (1, 3)]))
    targets = [i] + [(i + turn) % inner for turn in range(1, inner)] if split else [i]
    later = (place // inner) % 2 == 1
    masks = [mask for target in targets for mask in [later] + [owner < target for owner in members]]
    dtypes = [jnp.float32] + [jnp.bfloat16] * (len(targets) - 1)
    befores = combine([hold(from_half, *beside)], dtypes, [from_pair] + values, masks)
    terms = [befores[0]]
    for turn in range(1, len(targets)):
        terms.append(lax.ppermute(befores[turn], "seq", turn_pairs(n_seq, turn)))
    return terms, from_half


def causal_kernel(first_head, place_ref, q_ref, k_ref, v_ref, out_ref):
    rows = q_ref.shape[0]
    half = rows // 2
    top, bottom = pl.ds(0, half), pl.ds(half, half)
    keep = lax.broadcasted_iota(jnp.int32, (half, half), 0) >= lax.broadcasted_iota(
        jnp.int32, (half, half), 1
    )

    def scores(q_rows, k_rows, columns):
        return lax.dot_general(
            q_ref[q_rows, columns],
            k_ref[k_rows, columns],
            (((1,), (1,)), ((), ())),
            preferred_element_type=jnp.float32,
        )

    for index in range(out_ref.shape[1] // DH):
        columns = pl.ds((first_head + index) * DH, DH)
        placed = pl.ds(index * DH, DH)
        first = jnp.where(keep, scores(top, top, columns), 0.0).astype(jnp.bfloat16)
        below = scores(bottom, top, columns).astype(jnp.bfloat16)
        last = jnp.where(keep, scores(bottom, bottom, columns), 0.0).astype(jnp.bfloat16)
        out_ref[top, placed] = jnp.dot(first, v_ref[top, columns], preferred_element_type=jnp.float32)
        out_ref[bottom, placed] = jnp.dot(
            jnp.concatenate([below, last], axis=1),
            v_ref[:, columns],
            preferred_element_type=jnp.float32,
        )


def causal_part(queries, key_input, value_input, first_head, heads):
    return local_call(
        functools.partial(causal_kernel, first_head),
        scalars(0),
        [queries, key_input, value_input],
        [jax.ShapeDtypeStruct((queries.shape[0], heads * DH), jnp.float32)],
        3 * queries.shape[0] ** 2 * heads * DH,
    )[0]


def hidden_kernel(order, group, calls, place_ref, q_ref, gate_ref, gain_ref, kv_ref, *refs):
    terms, inners = refs[:group], refs[group : group + calls]
    kept_ref, sent_ref, squares_ref = refs[group + calls :]
    half = kept_ref.shape[0]
    heads = kv_ref.shape[0]
    share = heads // group
    size = q_ref.shape[0] // len(order)
    states = []
    for head in range(heads):
        state = kv_ref[head]
        for turn, term in enumerate(terms):
            value = term[head % share].astype(jnp.float32)
            if group > 1:
                covers = lax.rem(place_ref[1] - turn + group, group)
                value = jnp.where(covers == head // share, value, 0.0)
            state = state + value
        high = state.astype(jnp.bfloat16)
        low = (state - high.astype(jnp.float32)).astype(jnp.bfloat16)
        states.append(jnp.concatenate([high, low], axis=0))
    for position, block in enumerate(order):
        start = pl.multiple_of((place_ref[0] ^ block) * size, size)
        rows = pl.ds(start, size)
        hidden_ref = kept_ref if position * size < half else sent_ref
        placed = pl.ds(position * size % half, size)
        squares = jnp.zeros((size, DH), jnp.float32)
        for head in range(heads):
            columns = pl.ds(head * DH, DH)
            q_rows = q_ref[rows, columns]
            carried = jnp.dot(
                jnp.concatenate([q_rows, q_rows], axis=1),
                states[head],
                preferred_element_type=jnp.float32,
            )
            per_call = inners[0].shape[1] // DH
            inner = inners[head // per_call][rows, pl.ds(head % per_call * DH, DH)]
            attn = (carried + inner).astype(jnp.bfloat16).astype(jnp.float32)
            gate = 1.0 + jnp.tanh(gate_ref[rows, columns].astype(jnp.float32) * 0.5)
            gain = gain_ref[place_ref[0] * heads + head] * 0.5
            hidden_ref[placed, columns] = (attn * (gain * gate)).astype(jnp.bfloat16)
            squares = squares + attn * attn
        squares_ref[pl.ds(position, 1), :] = jnp.sum(jnp.transpose(squares), axis=0, keepdims=True)


def gated_hidden(queries, inners, kv_state, terms, gate_input, norm_gain, h, i, order):
    rows, width = queries.shape
    half = jax.ShapeDtypeStruct((rows // 2, width), jnp.bfloat16)
    return local_call(
        functools.partial(hidden_kernel, order, len(terms), len(inners)),
        scalars(h, i),
        [queries, gate_input, norm_gain.reshape(-1, 1, DH), kv_state, *terms, *inners],
        [
            half,
            half,
            jax.ShapeDtypeStruct((len(order), rows // len(order)), jnp.float32),
        ],
        4 * rows * width * DH,
    )


def project_kernel(jobs, n_rows, choices, flag_ref, *refs):
    rows_refs = refs[: 2 * n_rows]
    weight_refs = refs[2 * n_rows : -2]
    sent_ref, kept_ref = refs[-2:]

    def products(index, weight_ref):
        for rows, weight, first in jobs:
            if weight == index:
                columns = pl.ds(first, weight_ref.shape[1])
                kept_rows, sent_rows = rows_refs[2 * rows : 2 * rows + 2]
                sent_ref[:, columns] = jnp.dot(
                    sent_rows[...], weight_ref[...], preferred_element_type=jnp.float32
                ).astype(jnp.bfloat16)
                kept_ref[:, columns] = jnp.dot(
                    kept_rows[...], weight_ref[...], preferred_element_type=jnp.float32
                )

    first = 0
    for index, number in enumerate(choices):
        for k in range(number):
            one = functools.partial(products, index, weight_refs[first + k])
            if number == 1:
                one()
            else:
                pl.when(flag_ref[0] == k)(one)
        first += number


def project(jobs, rows_list, weights, flag):
    flat = [choice for weight in weights for choice in weight]
    choices = tuple(len(weight) for weight in weights)
    placed_jobs, total = [], 0
    for rows, weight in jobs:
        placed_jobs.append((rows, weight, total))
        total += weights[weight][0].shape[1]
    height, depth = rows_list[0][0].shape
    shape = (height, total)
    return local_call(
        functools.partial(project_kernel, tuple(placed_jobs), len(rows_list), choices),
        flag,
        [*[half for pair in rows_list for half in pair], *flat],
        [jax.ShapeDtypeStruct(shape, jnp.bfloat16), jax.ShapeDtypeStruct(shape, jnp.float32)],
        4 * height * depth * total,
    )


def fold_kernel(more, flag_ref, kept_ref, got_ref, *outs):
    if more:
        sent_ref, left_ref = outs
        half = left_ref.shape[0]
        left_ref[...] = kept_ref[:half] + got_ref[:half].astype(jnp.float32)
        sent_ref[...] = (kept_ref[half:] + got_ref[half:].astype(jnp.float32)).astype(jnp.bfloat16)
        return
    first = 0
    for out in outs:
        columns = pl.ds(first, out.shape[1])
        out[...] = (kept_ref[:, columns] + got_ref[:, columns].astype(jnp.float32)).astype(out.dtype)
        first += out.shape[1]


def fold(kept, got, widths=None):
    rows, width = kept.shape
    if widths is None:
        shape = (rows // 2, width)
        outs = [jax.ShapeDtypeStruct(shape, jnp.bfloat16), jax.ShapeDtypeStruct(shape, jnp.float32)]
    else:
        outs = [jax.ShapeDtypeStruct((rows, some), jnp.bfloat16) for some in widths]
    return local_call(functools.partial(fold_kernel, widths is None), scalars(0), [kept, got], outs)


def column(row):
    return jnp.transpose(jnp.broadcast_to(row, (row.shape[1], row.shape[1])))


def scaled_parts(counts, width, starts_ref, squares_ref, pieces, total_width):
    scale = lax.rsqrt(column(squares_ref[...]) / total_width + epsilon)
    where = 0
    for piece, count in zip(pieces, counts):
        for index in range(count):
            for at in range(0, width, DH):
                part = piece[:, pl.ds(index * width + at, DH)].astype(jnp.float32) * scale
                yield part, pl.multiple_of(starts_ref[where] + at, DH)
            where += 1


def placed_kernel(counts, width, total_width, starts_ref, squares_ref, *refs):
    out_ref = refs[-1]
    for part, start in scaled_parts(counts, width, starts_ref, squares_ref, refs[:-1], total_width):
        out_ref[:, pl.ds(start, DH)] = part.astype(out_ref.dtype)


def added_kernel(counts, width, total_width, starts_ref, squares_ref, *refs):
    out_ref, buf, sem = refs[-3:]
    copies = []
    parts = scaled_parts(counts, width, starts_ref, squares_ref, refs[: len(counts)], total_width)
    for at, (part, start) in enumerate(parts):
        buf[at] = part.astype(out_ref.dtype)
        copies.append(pltpu.make_async_copy(buf.at[at], out_ref.at[:, pl.ds(start, DH)], sem.at[at]))
        copies[-1].start()
    for copy in copies:
        copy.wait()


def placed(filled, pieces, squares, width, shape, total_width):
    counts = tuple(len(starts) for _, starts in pieces)
    starts = scalars(*[start for _, own in pieces for start in own])
    operands = [squares] + [piece for piece, _ in pieces]
    out_shape = jax.ShapeDtypeStruct(shape, jnp.bfloat16)
    columns = width * sum(counts)
    if filled is None:
        kernel = functools.partial(placed_kernel, counts, width, total_width)
        return local_call(kernel, starts, operands, [out_shape])[0]
    return pl.pallas_call(
        functools.partial(added_kernel, counts, width, total_width),
        in_specs=[pl.BlockSpec(memory_space=pltpu.SMEM)]
        + [pl.BlockSpec(memory_space=pltpu.VMEM)] * len(operands)
        + [pl.BlockSpec(memory_space=pl.ANY)],
        out_specs=pl.BlockSpec(memory_space=pl.ANY),
        out_shape=out_shape,
        scratch_shapes=[
            pltpu.VMEM((columns // DH, shape[0], DH), jnp.bfloat16),
            pltpu.SemaphoreType.DMA((columns // DH,)),
        ],
        input_output_aliases={len(operands) + 1: 0},
        compiler_params=pltpu.CompilerParams(vmem_limit_bytes=VMEM_BYTES),
        cost_estimate=pl.CostEstimate(
            flops=0, bytes_accessed=4 * shape[0] * columns, transcendentals=0
        ),
    )(starts, *operands, filled)


def shards(queries, key_input, value_input, gate_input, kv_state, norm_gain, out_weight):
    n_seq, n_head = lax.axis_size("seq"), lax.axis_size("head")
    inner = n_seq // LINE
    place, h = lax.axis_index("seq"), lax.axis_index("head")
    z, i = place // inner, place % inner
    tok_rows, local_width = queries.shape
    assert tok_rows == BLOCK
    heads = local_width // DH
    total_width = local_width * n_head
    width = out_weight.shape[1]

    def along(value, hops):
        return lax.ppermute(value, "seq", line_pairs(n_seq, hops))

    some = heads // 2
    inners = [
        causal_part(queries, key_input, value_input, 0, some),
        causal_part(queries, key_input, value_input, some, heads - some),
    ]
    terms, stepped = state_prefix(key_input, value_input, n_seq, place, inners)

    own_columns = hold(out_weight, stepped)
    w_halves = along(own_columns, SWAP_HALVES)
    w_next = along(own_columns, SWAP_NEXT)
    w_middle = along(own_columns, SWAP_MIDDLE)

    bits = n_head.bit_length() - 1
    order = [int(format(j, "b").zfill(bits)[::-1], 2) for j in range(n_head)] if bits else [0]
    kept_rows, sent_rows, squares = gated_hidden(
        queries, inners, kv_state, terms, gate_input, norm_gain, h, i, order
    )
    rows_list = [(kept_rows, sent_rows)]
    for turn in range(1, inner):
        pairs = turn_pairs(n_seq, turn)
        rows_list.append((lax.ppermute(kept_rows, "seq", pairs), lax.ppermute(sent_rows, "seq", pairs)))

    out_rows = tok_rows // n_head
    half, bit = n_head // 2, 1
    while bit < n_head:
        squares = squares[:half] + lax.ppermute(squares[half:], "head", flip_pairs(n_head, bit))
        half //= 2
        bit *= 2

    is_end = (z == 0) | (z == LINE - 1)
    flag = scalars(is_end)


    owners = [z ^ block for block in range(LINE)]
    blocks = [(out_weight,), (w_next,), (w_halves,)]

    def summed(parts, pins):
        weights = sorted({block for _, own in parts for block in own})
        jobs = [(p, weights.index(block)) for p, (_, own) in enumerate(parts) for block in own]
        sent, kept = project(
            jobs,
            [rows_list[turn] for turn, _ in parts],
            [blocks[block] for block in weights],
            hold(flag, *pins),
        )
        first_sent, bit = sent, 1
        while bit < n_head:
            got = lax.ppermute(sent, "head", flip_pairs(n_head, bit))
            bit *= 2
            if bit < n_head:
                sent, kept = fold(kept, got)
            else:
                kept = fold(kept, got, [width * len(own) for _, own in parts])
        pieces = []
        for piece, (turn, own) in zip(kept, parts):
            if turn:
                piece = lax.ppermute(piece, "seq", turn_pairs(n_seq, -turn))
            starts = [(owners[block] * inner + (i + turn) % inner) * width for block in own]
            pieces.append((piece, starts))
        return pieces, first_sent, got

    turns = list(range(inner))
    shape = (out_rows, width * n_seq)
    in_kernel = width % DH == 0 and out_rows == DH

    pieces, pins, ends = [], [], []

    def group(members, some):
        more, sent, end = summed([(turn, some) for turn in members], pins)
        pieces.extend(more)
        ends.append(end)
        pins[:] = [sent, squares]
        return [piece for piece, _ in more]

    group(turns[:1], [0])
    returned = group(turns[1:], [0]) if inner > 1 else []
    w_ends = along(hold(w_halves, *ends), TO_ENDS)
    blocks.append((w_middle, w_ends))
    group(turns[:1], [1, 2])
    if inner > 1:
        group(turns[1:], [1, 2])
    filled = placed(None, pieces, squares, width, shape, total_width) if in_kernel else None
    last, _, _ = summed(
        [(turn, [3]) for turn in turns], [*pins, *ends, *returned]
    )
    if in_kernel:
        return placed(filled, last, squares, width, shape, total_width)
    scale = lax.rsqrt(squares.reshape(out_rows, 1) / total_width + epsilon)
    output = jnp.zeros(shape, jnp.bfloat16)
    for piece, starts in pieces + last:
        piece = (piece.astype(jnp.float32) * scale).astype(jnp.bfloat16)
        for index, start in enumerate(starts):
            part = piece[:, index * width : (index + 1) * width]
            output = lax.dynamic_update_slice_in_dim(output, part, start, 1)
    return output


def solution(mesh):
    in_specs = (
        P("seq", "head"),
        P("seq", "head"),
        P("seq", "head"),
        P("seq", "head"),
        P("head", None, None),
        P(),
        P("head", "seq"),
    )
    out_specs = P(("seq", "head"), None)
    return jax.shard_map(shards, mesh=mesh, in_specs=in_specs, out_specs=out_specs, check_vma=False)
```

```python
import functools

import jax
import jax.numpy as jnp
from jax import lax
from jax.experimental import pallas as pl
from jax.experimental.pallas import tpu as pltpu
from jax.sharding import PartitionSpec as P

DH = 128
BLOCK = 512
LINE = 4
VMEM_BYTES = 16 * 1024 * 1024


epsilon = 1e-05


def line_pairs(n_seq, hops):
    inner = n_seq // LINE
    return [(a * inner + i, b * inner + i) for a, b in hops for i in range(inner)]


def turn_pairs(n_seq, turn):
    inner = n_seq // LINE
    return [(a * inner + i, a * inner + (i + turn) % inner) for a in range(LINE) for i in range(inner)]


def flip_pairs(n_head, bit):
    return [(h, h ^ bit) for h in range(n_head)]


SWAP_NEXT = [(z, z ^ 1) for z in range(LINE)]
SWAP_HALVES = [(z, z ^ 2) for z in range(LINE)]
SWAP_MIDDLE = [(1, 2), (2, 1)]
TO_ENDS = [(1, 0), (2, 3)]


def hold(value, *others):
    return lax.optimization_barrier((value, *others))[0]


def scalars(*values):
    return jnp.stack([jnp.asarray(value, jnp.int32) for value in values])


def local_call(kernel, places, operands, out_shapes, flops=0):
    held = sum(value.size * value.dtype.itemsize for value in [*operands, *out_shapes])
    return pl.pallas_call(
        kernel,
        in_specs=[pl.BlockSpec(memory_space=pltpu.SMEM)]
        + [pl.BlockSpec(memory_space=pltpu.VMEM)] * len(operands),
        out_specs=[pl.BlockSpec(memory_space=pltpu.VMEM)] * len(out_shapes),
        out_shape=out_shapes,
        compiler_params=pltpu.CompilerParams(vmem_limit_bytes=max(VMEM_BYTES, held + held // 2)),
        cost_estimate=pl.CostEstimate(flops=flops, bytes_accessed=held, transcendentals=0),
    )(places, *operands)


def combine_kernel(count, always, masks_ref, *refs):
    values, outs = refs[:count], refs[count:]
    for index in range(values[0].shape[0]):
        total = values[0][index].astype(jnp.float32)
        for value in values[1:always]:
            total = total + value[index].astype(jnp.float32)
        for position, out in enumerate(outs):
            own = total
            for k in range(always, count):
                mask = masks_ref[position * (count - always) + k - always]
                own = own + jnp.where(mask != 0, values[k][index].astype(jnp.float32), 0.0)
            out[index] = own.astype(out.dtype)


def combine(values, dtypes, sometimes=(), masks=None):
    operands = list(values) + list(sometimes)
    masks = scalars(0) if masks is None else scalars(*masks)
    return local_call(
        functools.partial(combine_kernel, len(operands), len(values)),
        masks,
        operands,
        [jax.ShapeDtypeStruct(values[0].shape, dtype) for dtype in dtypes],
    )


def states_kernel(part_ref, k_ref, v_ref, out_ref):
    heads = out_ref.shape[0]
    for index in range(heads):
        columns = pl.ds(pl.multiple_of((part_ref[0] * heads + index) * DH, DH), DH)
        out_ref[index] = lax.dot_general(
            k_ref[:, columns],
            v_ref[:, columns],
            (((0,), (0,)), ((), ())),
            preferred_element_type=jnp.float32,
        ).astype(out_ref.dtype)


def block_states(key_input, value_input, part, heads, dtype):
    return local_call(
        states_kernel,
        scalars(part),
        [key_input, value_input],
        [jax.ShapeDtypeStruct((heads, DH, DH), dtype)],
        2 * key_input.shape[0] * heads * DH * DH,
    )[0]


def state_prefix(key_input, value_input, n_seq, place, ahead):
    inner = n_seq // LINE
    i = place % inner
    heads = key_input.shape[1] // DH
    split = heads % inner == 0
    share = heads // inner if split else heads
    if split:
        sends = [
            block_states(key_input, value_input, (i + turn) % inner, share, jnp.bfloat16)
            for turn in range(1, inner)
        ]
        own = block_states(key_input, value_input, i, share, jnp.float32)
    else:
        own = block_states(key_input, value_input, 0, share, jnp.float32)
        sends = [own.astype(jnp.bfloat16)] * (inner - 1)
    values, members = [own], [i]
    for turn in range(1, inner):
        values.append(lax.ppermute(sends[turn - 1], "seq", turn_pairs(n_seq, turn)))
        members.append((i - turn) % inner)
    (first,) = combine(values, [jnp.bfloat16])
    from_pair = lax.ppermute(first, "seq", line_pairs(n_seq, SWAP_NEXT))
    from_pair = hold(from_pair, ahead[0])
    (second,) = combine(values + [from_pair], [jnp.bfloat16])
    from_half = lax.ppermute(second, "seq", line_pairs(n_seq, [(0, 2), (1, 3)]))
    from_half = hold(from_half, ahead[1])
    targets = [i] + [(i + turn) % inner for turn in range(1, inner)] if split else [i]
    later = (place // inner) % 2 == 1
    masks = [mask for target in targets for mask in [later] + [owner < target for owner in members]]
    dtypes = [jnp.float32] + [jnp.bfloat16] * (len(targets) - 1)
    befores = combine([from_half], dtypes, [from_pair] + values, masks)
    terms = [befores[0]]
    for turn in range(1, len(targets)):
        terms.append(lax.ppermute(befores[turn], "seq", turn_pairs(n_seq, turn)))
    return terms


def causal_kernel(first_head, place_ref, q_ref, k_ref, v_ref, out_ref):
    rows = q_ref.shape[0]
    half = rows // 2
    top, bottom = pl.ds(0, half), pl.ds(half, half)
    keep = lax.broadcasted_iota(jnp.int32, (half, half), 0) >= lax.broadcasted_iota(
        jnp.int32, (half, half), 1
    )

    def scores(q_rows, k_rows, columns):
        return lax.dot_general(
            q_ref[q_rows, columns],
            k_ref[k_rows, columns],
            (((1,), (1,)), ((), ())),
            preferred_element_type=jnp.float32,
        )

    for index in range(out_ref.shape[1] // DH):
        columns = pl.ds((first_head + index) * DH, DH)
        placed = pl.ds(index * DH, DH)
        first = jnp.where(keep, scores(top, top, columns), 0.0).astype(jnp.bfloat16)
        below = scores(bottom, top, columns).astype(jnp.bfloat16)
        last = jnp.where(keep, scores(bottom, bottom, columns), 0.0).astype(jnp.bfloat16)
        out_ref[top, placed] = jnp.dot(first, v_ref[top, columns], preferred_element_type=jnp.float32)
        out_ref[bottom, placed] = jnp.dot(
            jnp.concatenate([below, last], axis=1),
            v_ref[:, columns],
            preferred_element_type=jnp.float32,
        )


def causal_part(queries, key_input, value_input, first_head, heads):
    return local_call(
        functools.partial(causal_kernel, first_head),
        scalars(0),
        [queries, key_input, value_input],
        [jax.ShapeDtypeStruct((queries.shape[0], heads * DH), jnp.float32)],
        3 * queries.shape[0] ** 2 * heads * DH,
    )[0]


def hidden_kernel(order, group, calls, place_ref, q_ref, gate_ref, gain_ref, kv_ref, *refs):
    terms, inners = refs[:group], refs[group : group + calls]
    kept_ref, sent_ref, squares_ref = refs[group + calls :]
    half = kept_ref.shape[0]
    heads = kv_ref.shape[0]
    share = heads // group
    size = q_ref.shape[0] // len(order)
    states = []
    for head in range(heads):
        state = kv_ref[head]
        for turn, term in enumerate(terms):
            value = term[head % share].astype(jnp.float32)
            if group > 1:
                covers = lax.rem(place_ref[1] - turn + group, group)
                value = jnp.where(covers == head // share, value, 0.0)
            state = state + value
        high = state.astype(jnp.bfloat16)
        low = (state - high.astype(jnp.float32)).astype(jnp.bfloat16)
        states.append(jnp.concatenate([high, low], axis=0))
    for position, block in enumerate(order):
        start = pl.multiple_of((place_ref[0] ^ block) * size, size)
        rows = pl.ds(start, size)
        hidden_ref = kept_ref if position * size < half else sent_ref
        placed = pl.ds(position * size % half, size)
        squares = jnp.zeros((size, DH), jnp.float32)
        for head in range(heads):
            columns = pl.ds(head * DH, DH)
            q_rows = q_ref[rows, columns]
            carried = jnp.dot(
                jnp.concatenate([q_rows, q_rows], axis=1),
                states[head],
                preferred_element_type=jnp.float32,
            )
            per_call = inners[0].shape[1] // DH
            inner = inners[head // per_call][rows, pl.ds(head % per_call * DH, DH)]
            attn = (carried + inner).astype(jnp.bfloat16).astype(jnp.float32)
            gate = 1.0 + jnp.tanh(gate_ref[rows, columns].astype(jnp.float32) * 0.5)
            gain = gain_ref[place_ref[0] * heads + head] * 0.5
            hidden_ref[placed, columns] = (attn * (gain * gate)).astype(jnp.bfloat16)
            squares = squares + attn * attn
        squares_ref[pl.ds(position, 1), :] = jnp.sum(jnp.transpose(squares), axis=0, keepdims=True)


def gated_hidden(queries, inners, kv_state, terms, gate_input, norm_gain, h, i, order):
    rows, width = queries.shape
    half = jax.ShapeDtypeStruct((rows // 2, width), jnp.bfloat16)
    return local_call(
        functools.partial(hidden_kernel, order, len(terms), len(inners)),
        scalars(h, i),
        [queries, gate_input, norm_gain.reshape(-1, 1, DH), kv_state, *terms, *inners],
        [
            half,
            half,
            jax.ShapeDtypeStruct((len(order), rows // len(order)), jnp.float32),
        ],
        4 * rows * width * DH,
    )


def project_kernel(jobs, n_rows, choices, flag_ref, *refs):
    rows_refs = refs[: 2 * n_rows]
    weight_refs = refs[2 * n_rows : -2]
    sent_ref, kept_ref = refs[-2:]

    def products(index, weight_ref):
        for rows, weight, first in jobs:
            if weight == index:
                columns = pl.ds(first, weight_ref.shape[1])
                kept_rows, sent_rows = rows_refs[2 * rows : 2 * rows + 2]
                sent_ref[:, columns] = jnp.dot(
                    sent_rows[...], weight_ref[...], preferred_element_type=jnp.float32
                ).astype(jnp.bfloat16)
                kept_ref[:, columns] = jnp.dot(
                    kept_rows[...], weight_ref[...], preferred_element_type=jnp.float32
                )

    first = 0
    for index, number in enumerate(choices):
        for k in range(number):
            one = functools.partial(products, index, weight_refs[first + k])
            if number == 1:
                one()
            else:
                pl.when(flag_ref[0] == k)(one)
        first += number


def project(jobs, rows_list, weights, flag):
    flat = [choice for weight in weights for choice in weight]
    choices = tuple(len(weight) for weight in weights)
    placed_jobs, total = [], 0
    for rows, weight in jobs:
        placed_jobs.append((rows, weight, total))
        total += weights[weight][0].shape[1]
    height, depth = rows_list[0][0].shape
    shape = (height, total)
    return local_call(
        functools.partial(project_kernel, tuple(placed_jobs), len(rows_list), choices),
        flag,
        [*[half for pair in rows_list for half in pair], *flat],
        [jax.ShapeDtypeStruct(shape, jnp.bfloat16), jax.ShapeDtypeStruct(shape, jnp.float32)],
        4 * height * depth * total,
    )


def fold_kernel(more, flag_ref, kept_ref, got_ref, *outs):
    if more:
        sent_ref, left_ref = outs
        half = left_ref.shape[0]
        left_ref[...] = kept_ref[:half] + got_ref[:half].astype(jnp.float32)
        sent_ref[...] = (kept_ref[half:] + got_ref[half:].astype(jnp.float32)).astype(jnp.bfloat16)
        return
    first = 0
    for out in outs:
        columns = pl.ds(first, out.shape[1])
        out[...] = (kept_ref[:, columns] + got_ref[:, columns].astype(jnp.float32)).astype(out.dtype)
        first += out.shape[1]


def fold(kept, got, widths=None):
    rows, width = kept.shape
    if widths is None:
        shape = (rows // 2, width)
        outs = [jax.ShapeDtypeStruct(shape, jnp.bfloat16), jax.ShapeDtypeStruct(shape, jnp.float32)]
    else:
        outs = [jax.ShapeDtypeStruct((rows, some), jnp.bfloat16) for some in widths]
    return local_call(functools.partial(fold_kernel, widths is None), scalars(0), [kept, got], outs)


def column(row):
    return jnp.transpose(jnp.broadcast_to(row, (row.shape[1], row.shape[1])))


def scaled_parts(counts, width, starts_ref, squares_ref, pieces, total_width):
    scale = lax.rsqrt(column(squares_ref[...]) / total_width + epsilon)
    where = 0
    for piece, count in zip(pieces, counts):
        for index in range(count):
            for at in range(0, width, DH):
                part = piece[:, pl.ds(index * width + at, DH)].astype(jnp.float32) * scale
                yield part, pl.multiple_of(starts_ref[where] + at, DH)
            where += 1


def placed_kernel(counts, width, total_width, starts_ref, squares_ref, *refs):
    out_ref = refs[-1]
    for part, start in scaled_parts(counts, width, starts_ref, squares_ref, refs[:-1], total_width):
        out_ref[:, pl.ds(start, DH)] = part.astype(out_ref.dtype)


def added_kernel(counts, width, total_width, starts_ref, squares_ref, *refs):
    out_ref, buf, sem = refs[-3:]
    copies = []
    parts = scaled_parts(counts, width, starts_ref, squares_ref, refs[: len(counts)], total_width)
    for at, (part, start) in enumerate(parts):
        buf[at] = part.astype(out_ref.dtype)
        copies.append(pltpu.make_async_copy(buf.at[at], out_ref.at[:, pl.ds(start, DH)], sem.at[at]))
        copies[-1].start()
    for copy in copies:
        copy.wait()


def placed(filled, pieces, squares, width, shape, total_width):
    counts = tuple(len(starts) for _, starts in pieces)
    starts = scalars(*[start for _, own in pieces for start in own])
    operands = [squares] + [piece for piece, _ in pieces]
    out_shape = jax.ShapeDtypeStruct(shape, jnp.bfloat16)
    columns = width * sum(counts)
    if filled is None:
        kernel = functools.partial(placed_kernel, counts, width, total_width)
        return local_call(kernel, starts, operands, [out_shape])[0]
    return pl.pallas_call(
        functools.partial(added_kernel, counts, width, total_width),
        in_specs=[pl.BlockSpec(memory_space=pltpu.SMEM)]
        + [pl.BlockSpec(memory_space=pltpu.VMEM)] * len(operands)
        + [pl.BlockSpec(memory_space=pl.ANY)],
        out_specs=pl.BlockSpec(memory_space=pl.ANY),
        out_shape=out_shape,
        scratch_shapes=[
            pltpu.VMEM((columns // DH, shape[0], DH), jnp.bfloat16),
            pltpu.SemaphoreType.DMA((columns // DH,)),
        ],
        input_output_aliases={len(operands) + 1: 0},
        compiler_params=pltpu.CompilerParams(vmem_limit_bytes=VMEM_BYTES),
        cost_estimate=pl.CostEstimate(
            flops=0, bytes_accessed=4 * shape[0] * columns, transcendentals=0
        ),
    )(starts, *operands, filled)


def shards(queries, key_input, value_input, gate_input, kv_state, norm_gain, out_weight):
    n_seq, n_head = lax.axis_size("seq"), lax.axis_size("head")
    inner = n_seq // LINE
    place, h = lax.axis_index("seq"), lax.axis_index("head")
    z, i = place // inner, place % inner
    tok_rows, local_width = queries.shape
    assert tok_rows == BLOCK
    heads = local_width // DH
    total_width = local_width * n_head
    width = out_weight.shape[1]

    def along(value, hops):
        return lax.ppermute(value, "seq", line_pairs(n_seq, hops))

    w_halves = along(out_weight, SWAP_HALVES)
    w_next = along(out_weight, SWAP_NEXT)
    terms = state_prefix(key_input, value_input, n_seq, place, (w_halves, w_next))
    w_middle = along(hold(out_weight, *terms), SWAP_MIDDLE)
    w_ends = along(hold(w_halves, *terms), TO_ENDS)
    some = heads // 2
    inners = [
        causal_part(queries, key_input, value_input, 0, some),
        causal_part(queries, key_input, value_input, some, heads - some),
    ]

    bits = n_head.bit_length() - 1
    order = [int(format(j, "b").zfill(bits)[::-1], 2) for j in range(n_head)] if bits else [0]
    kept_rows, sent_rows, squares = gated_hidden(
        queries, inners, kv_state, terms, gate_input, norm_gain, h, i, order
    )
    rows_list = [(kept_rows, sent_rows)]
    for turn in range(1, inner):
        pairs = turn_pairs(n_seq, turn)
        rows_list.append((lax.ppermute(kept_rows, "seq", pairs), lax.ppermute(sent_rows, "seq", pairs)))

    out_rows = tok_rows // n_head
    half, bit = n_head // 2, 1
    while bit < n_head:
        squares = squares[:half] + lax.ppermute(squares[half:], "head", flip_pairs(n_head, bit))
        half //= 2
        bit *= 2

    is_end = (z == 0) | (z == LINE - 1)
    flag = scalars(is_end)


    owners = [z ^ block for block in range(LINE)]
    blocks = [(out_weight,), (w_next,), (w_halves,), (w_middle, w_ends)]

    def summed(parts, pins):
        weights = sorted({block for _, own in parts for block in own})
        jobs = [(p, weights.index(block)) for p, (_, own) in enumerate(parts) for block in own]
        sent, kept = project(
            jobs,
            [rows_list[turn] for turn, _ in parts],
            [blocks[block] for block in weights],
            hold(flag, *pins),
        )
        first_sent, bit = sent, 1
        while bit < n_head:
            got = lax.ppermute(sent, "head", flip_pairs(n_head, bit))
            bit *= 2
            if bit < n_head:
                sent, kept = fold(kept, got)
            else:
                kept = fold(kept, got, [width * len(own) for _, own in parts])
        pieces = []
        for piece, (turn, own) in zip(kept, parts):
            if turn:
                piece = lax.ppermute(piece, "seq", turn_pairs(n_seq, -turn))
            starts = [(owners[block] * inner + (i + turn) % inner) * width for block in own]
            pieces.append((piece, starts))
        return pieces, first_sent, got

    turns = list(range(inner))
    shape = (out_rows, width * n_seq)
    in_kernel = width % DH == 0 and out_rows == DH

    groups = [(turns[:1], [0, 1, 2]), (turns[:1], [3])]
    groups += [(turns[1:], [block]) for block in range(LINE)] if inner > 1 else []
    pieces, pins = [], []
    for members, some in groups:
        last, sent, _ = summed([(turn, some) for turn in members], pins)
        pieces += last
        pins = [sent, squares]
    pieces = pieces[: len(pieces) - len(last)]
    filled = placed(None, pieces, squares, width, shape, total_width) if in_kernel else None
    if in_kernel:
        return placed(filled, last, squares, width, shape, total_width)
    scale = lax.rsqrt(squares.reshape(out_rows, 1) / total_width + epsilon)
    output = jnp.zeros(shape, jnp.bfloat16)
    for piece, starts in pieces + last:
        piece = (piece.astype(jnp.float32) * scale).astype(jnp.bfloat16)
        for index, start in enumerate(starts):
            part = piece[:, index * width : (index + 1) * width]
            output = lax.dynamic_update_slice_in_dim(output, part, start, 1)
    return output


def solution(mesh):
    in_specs = (
        P("seq", "head"),
        P("seq", "head"),
        P("seq", "head"),
        P("seq", "head"),
        P("head", None, None),
        P(),
        P("head", "seq"),
    )
    out_specs = P(("seq", "head"), None)
    return jax.shard_map(shards, mesh=mesh, in_specs=in_specs, out_specs=out_specs, check_vma=False)
```

```python
import functools

import jax
import jax.numpy as jnp
from jax import lax
from jax.experimental import pallas as pl
from jax.experimental.pallas import tpu as pltpu
from jax.sharding import PartitionSpec as P

DH = 128
BLOCK = 512
LINE = 4
VMEM_BYTES = 16 * 1024 * 1024


epsilon = 1e-05


def line_pairs(n_seq, hops):
    inner = n_seq // LINE
    return [(a * inner + i, b * inner + i) for a, b in hops for i in range(inner)]


def turn_pairs(n_seq, turn):
    inner = n_seq // LINE
    return [(a * inner + i, a * inner + (i + turn) % inner) for a in range(LINE) for i in range(inner)]


def flip_pairs(n_head, bit):
    return [(h, h ^ bit) for h in range(n_head)]


SWAP_NEXT = [(z, z ^ 1) for z in range(LINE)]
SWAP_HALVES = [(z, z ^ 2) for z in range(LINE)]
SWAP_MIDDLE = [(1, 2), (2, 1)]
TO_ENDS = [(1, 0), (2, 3)]


def hold(value, *others):
    return lax.optimization_barrier((value, *others))[0]


def scalars(*values):
    return jnp.stack([jnp.asarray(value, jnp.int32) for value in values])


def local_call(kernel, places, operands, out_shapes, flops=0):
    held = sum(value.size * value.dtype.itemsize for value in [*operands, *out_shapes])
    return pl.pallas_call(
        kernel,
        in_specs=[pl.BlockSpec(memory_space=pltpu.SMEM)]
        + [pl.BlockSpec(memory_space=pltpu.VMEM)] * len(operands),
        out_specs=[pl.BlockSpec(memory_space=pltpu.VMEM)] * len(out_shapes),
        out_shape=out_shapes,
        compiler_params=pltpu.CompilerParams(vmem_limit_bytes=max(VMEM_BYTES, held + held // 2)),
        cost_estimate=pl.CostEstimate(flops=flops, bytes_accessed=held, transcendentals=0),
    )(places, *operands)


def combine_kernel(count, always, masks_ref, *refs):
    values, outs = refs[:count], refs[count:]
    for index in range(values[0].shape[0]):
        total = values[0][index].astype(jnp.float32)
        for value in values[1:always]:
            total = total + value[index].astype(jnp.float32)
        for position, out in enumerate(outs):
            own = total
            for k in range(always, count):
                mask = masks_ref[position * (count - always) + k - always]
                own = own + jnp.where(mask != 0, values[k][index].astype(jnp.float32), 0.0)
            out[index] = own.astype(out.dtype)


def combine(values, dtypes, sometimes=(), masks=None):
    operands = list(values) + list(sometimes)
    masks = scalars(0) if masks is None else scalars(*masks)
    return local_call(
        functools.partial(combine_kernel, len(operands), len(values)),
        masks,
        operands,
        [jax.ShapeDtypeStruct(values[0].shape, dtype) for dtype in dtypes],
    )


def states_kernel(part_ref, k_ref, v_ref, out_ref):
    heads = out_ref.shape[0]
    for index in range(heads):
        columns = pl.ds(pl.multiple_of((part_ref[0] * heads + index) * DH, DH), DH)
        out_ref[index] = lax.dot_general(
            k_ref[:, columns],
            v_ref[:, columns],
            (((0,), (0,)), ((), ())),
            preferred_element_type=jnp.float32,
        ).astype(out_ref.dtype)


def block_states(key_input, value_input, part, heads, dtype):
    return local_call(
        states_kernel,
        scalars(part),
        [key_input, value_input],
        [jax.ShapeDtypeStruct((heads, DH, DH), dtype)],
        2 * key_input.shape[0] * heads * DH * DH,
    )[0]


def state_prefix(key_input, value_input, n_seq, place):
    inner = n_seq // LINE
    i = place % inner
    heads = key_input.shape[1] // DH
    split = heads % inner == 0
    share = heads // inner if split else heads
    if split:
        sends = [
            block_states(key_input, value_input, (i + turn) % inner, share, jnp.bfloat16)
            for turn in range(1, inner)
        ]
        own = block_states(key_input, value_input, i, share, jnp.float32)
    else:
        own = block_states(key_input, value_input, 0, share, jnp.float32)
        sends = [own.astype(jnp.bfloat16)] * (inner - 1)
    values, members = [own], [i]
    for turn in range(1, inner):
        values.append(lax.ppermute(sends[turn - 1], "seq", turn_pairs(n_seq, turn)))
        members.append((i - turn) % inner)
    (first,) = combine(values, [jnp.bfloat16])
    from_pair = lax.ppermute(first, "seq", line_pairs(n_seq, SWAP_NEXT))
    (second,) = combine(values + [from_pair], [jnp.bfloat16])
    from_half = lax.ppermute(second, "seq", line_pairs(n_seq, [(0, 2), (1, 3)]))
    targets = [i] + [(i + turn) % inner for turn in range(1, inner)] if split else [i]
    later = (place // inner) % 2 == 1
    masks = [mask for target in targets for mask in [later] + [owner < target for owner in members]]
    dtypes = [jnp.float32] + [jnp.bfloat16] * (len(targets) - 1)
    befores = combine([from_half], dtypes, [from_pair] + values, masks)
    terms = [befores[0]]
    for turn in range(1, len(targets)):
        terms.append(lax.ppermute(befores[turn], "seq", turn_pairs(n_seq, turn)))
    return terms, from_half


def causal_kernel(first_head, place_ref, q_ref, k_ref, v_ref, out_ref):
    rows = q_ref.shape[0]
    half = rows // 2
    top, bottom = pl.ds(0, half), pl.ds(half, half)
    keep = lax.broadcasted_iota(jnp.int32, (half, half), 0) >= lax.broadcasted_iota(
        jnp.int32, (half, half), 1
    )

    def scores(q_rows, k_rows, columns):
        return lax.dot_general(
            q_ref[q_rows, columns],
            k_ref[k_rows, columns],
            (((1,), (1,)), ((), ())),
            preferred_element_type=jnp.float32,
        )

    for index in range(out_ref.shape[1] // DH):
        columns = pl.ds((first_head + index) * DH, DH)
        placed = pl.ds(index * DH, DH)
        first = jnp.where(keep, scores(top, top, columns), 0.0).astype(jnp.bfloat16)
        below = scores(bottom, top, columns).astype(jnp.bfloat16)
        last = jnp.where(keep, scores(bottom, bottom, columns), 0.0).astype(jnp.bfloat16)
        out_ref[top, placed] = jnp.dot(first, v_ref[top, columns], preferred_element_type=jnp.float32)
        out_ref[bottom, placed] = jnp.dot(
            jnp.concatenate([below, last], axis=1),
            v_ref[:, columns],
            preferred_element_type=jnp.float32,
        )


def causal_part(queries, key_input, value_input, first_head, heads):
    return local_call(
        functools.partial(causal_kernel, first_head),
        scalars(0),
        [queries, key_input, value_input],
        [jax.ShapeDtypeStruct((queries.shape[0], heads * DH), jnp.float32)],
        3 * queries.shape[0] ** 2 * heads * DH,
    )[0]


def hidden_kernel(order, group, calls, place_ref, q_ref, gate_ref, gain_ref, kv_ref, *refs):
    terms, inners = refs[:group], refs[group : group + calls]
    kept_ref, sent_ref, squares_ref = refs[group + calls :]
    half = kept_ref.shape[0]
    heads = kv_ref.shape[0]
    share = heads // group
    size = q_ref.shape[0] // len(order)
    states = []
    for head in range(heads):
        state = kv_ref[head]
        for turn, term in enumerate(terms):
            value = term[head % share].astype(jnp.float32)
            if group > 1:
                covers = lax.rem(place_ref[1] - turn + group, group)
                value = jnp.where(covers == head // share, value, 0.0)
            state = state + value
        high = state.astype(jnp.bfloat16)
        low = (state - high.astype(jnp.float32)).astype(jnp.bfloat16)
        states.append(jnp.concatenate([high, low], axis=0))
    for position, block in enumerate(order):
        start = pl.multiple_of((place_ref[0] ^ block) * size, size)
        rows = pl.ds(start, size)
        hidden_ref = kept_ref if position * size < half else sent_ref
        placed = pl.ds(position * size % half, size)
        squares = jnp.zeros((size, DH), jnp.float32)
        for head in range(heads):
            columns = pl.ds(head * DH, DH)
            q_rows = q_ref[rows, columns]
            carried = jnp.dot(
                jnp.concatenate([q_rows, q_rows], axis=1),
                states[head],
                preferred_element_type=jnp.float32,
            )
            per_call = inners[0].shape[1] // DH
            inner = inners[head // per_call][rows, pl.ds(head % per_call * DH, DH)]
            attn = (carried + inner).astype(jnp.bfloat16).astype(jnp.float32)
            gate = 1.0 + jnp.tanh(gate_ref[rows, columns].astype(jnp.float32) * 0.5)
            gain = gain_ref[place_ref[0] * heads + head] * 0.5
            hidden_ref[placed, columns] = (attn * (gain * gate)).astype(jnp.bfloat16)
            squares = squares + attn * attn
        squares_ref[pl.ds(position, 1), :] = jnp.sum(jnp.transpose(squares), axis=0, keepdims=True)


def gated_hidden(queries, inners, kv_state, terms, gate_input, norm_gain, h, i, order):
    rows, width = queries.shape
    half = jax.ShapeDtypeStruct((rows // 2, width), jnp.bfloat16)
    return local_call(
        functools.partial(hidden_kernel, order, len(terms), len(inners)),
        scalars(h, i),
        [queries, gate_input, norm_gain.reshape(-1, 1, DH), kv_state, *terms, *inners],
        [
            half,
            half,
            jax.ShapeDtypeStruct((len(order), rows // len(order)), jnp.float32),
        ],
        4 * rows * width * DH,
    )


def project_kernel(jobs, n_rows, choices, flag_ref, *refs):
    rows_refs = refs[: 2 * n_rows]
    weight_refs = refs[2 * n_rows : -2]
    sent_ref, kept_ref = refs[-2:]

    def products(index, weight_ref):
        for rows, weight, first in jobs:
            if weight == index:
                columns = pl.ds(first, weight_ref.shape[1])
                kept_rows, sent_rows = rows_refs[2 * rows : 2 * rows + 2]
                sent_ref[:, columns] = jnp.dot(
                    sent_rows[...], weight_ref[...], preferred_element_type=jnp.float32
                ).astype(jnp.bfloat16)
                kept_ref[:, columns] = jnp.dot(
                    kept_rows[...], weight_ref[...], preferred_element_type=jnp.float32
                )

    first = 0
    for index, number in enumerate(choices):
        for k in range(number):
            one = functools.partial(products, index, weight_refs[first + k])
            if number == 1:
                one()
            else:
                pl.when(flag_ref[0] == k)(one)
        first += number


def project(jobs, rows_list, weights, flag):
    flat = [choice for weight in weights for choice in weight]
    choices = tuple(len(weight) for weight in weights)
    placed_jobs, total = [], 0
    for rows, weight in jobs:
        placed_jobs.append((rows, weight, total))
        total += weights[weight][0].shape[1]
    height, depth = rows_list[0][0].shape
    shape = (height, total)
    return local_call(
        functools.partial(project_kernel, tuple(placed_jobs), len(rows_list), choices),
        flag,
        [*[half for pair in rows_list for half in pair], *flat],
        [jax.ShapeDtypeStruct(shape, jnp.bfloat16), jax.ShapeDtypeStruct(shape, jnp.float32)],
        4 * height * depth * total,
    )


def fold_kernel(more, flag_ref, kept_ref, got_ref, *outs):
    if more:
        sent_ref, left_ref = outs
        half = left_ref.shape[0]
        left_ref[...] = kept_ref[:half] + got_ref[:half].astype(jnp.float32)
        sent_ref[...] = (kept_ref[half:] + got_ref[half:].astype(jnp.float32)).astype(jnp.bfloat16)
        return
    first = 0
    for out in outs:
        columns = pl.ds(first, out.shape[1])
        out[...] = (kept_ref[:, columns] + got_ref[:, columns].astype(jnp.float32)).astype(out.dtype)
        first += out.shape[1]


def fold(kept, got, widths=None):
    rows, width = kept.shape
    if widths is None:
        shape = (rows // 2, width)
        outs = [jax.ShapeDtypeStruct(shape, jnp.bfloat16), jax.ShapeDtypeStruct(shape, jnp.float32)]
    else:
        outs = [jax.ShapeDtypeStruct((rows, some), jnp.bfloat16) for some in widths]
    return local_call(functools.partial(fold_kernel, widths is None), scalars(0), [kept, got], outs)


def column(row):
    return jnp.transpose(jnp.broadcast_to(row, (row.shape[1], row.shape[1])))


def scaled_parts(counts, width, starts_ref, squares_ref, pieces, total_width):
    scale = lax.rsqrt(column(squares_ref[...]) / total_width + epsilon)
    where = 0
    for piece, count in zip(pieces, counts):
        for index in range(count):
            for at in range(0, width, DH):
                part = piece[:, pl.ds(index * width + at, DH)].astype(jnp.float32) * scale
                yield part, pl.multiple_of(starts_ref[where] + at, DH)
            where += 1


def placed_kernel(counts, width, total_width, starts_ref, squares_ref, *refs):
    out_ref = refs[-1]
    for part, start in scaled_parts(counts, width, starts_ref, squares_ref, refs[:-1], total_width):
        out_ref[:, pl.ds(start, DH)] = part.astype(out_ref.dtype)


def added_kernel(counts, width, total_width, starts_ref, squares_ref, *refs):
    out_ref, buf, sem = refs[-3:]
    copies = []
    parts = scaled_parts(counts, width, starts_ref, squares_ref, refs[: len(counts)], total_width)
    for at, (part, start) in enumerate(parts):
        buf[at] = part.astype(out_ref.dtype)
        copies.append(pltpu.make_async_copy(buf.at[at], out_ref.at[:, pl.ds(start, DH)], sem.at[at]))
        copies[-1].start()
    for copy in copies:
        copy.wait()


def placed(filled, pieces, squares, width, shape, total_width):
    counts = tuple(len(starts) for _, starts in pieces)
    starts = scalars(*[start for _, own in pieces for start in own])
    operands = [squares] + [piece for piece, _ in pieces]
    out_shape = jax.ShapeDtypeStruct(shape, jnp.bfloat16)
    columns = width * sum(counts)
    if filled is None:
        kernel = functools.partial(placed_kernel, counts, width, total_width)
        return local_call(kernel, starts, operands, [out_shape])[0]
    return pl.pallas_call(
        functools.partial(added_kernel, counts, width, total_width),
        in_specs=[pl.BlockSpec(memory_space=pltpu.SMEM)]
        + [pl.BlockSpec(memory_space=pltpu.VMEM)] * len(operands)
        + [pl.BlockSpec(memory_space=pl.ANY)],
        out_specs=pl.BlockSpec(memory_space=pl.ANY),
        out_shape=out_shape,
        scratch_shapes=[
            pltpu.VMEM((columns // DH, shape[0], DH), jnp.bfloat16),
            pltpu.SemaphoreType.DMA((columns // DH,)),
        ],
        input_output_aliases={len(operands) + 1: 0},
        compiler_params=pltpu.CompilerParams(vmem_limit_bytes=VMEM_BYTES),
        cost_estimate=pl.CostEstimate(
            flops=0, bytes_accessed=4 * shape[0] * columns, transcendentals=0
        ),
    )(starts, *operands, filled)


def shards(queries, key_input, value_input, gate_input, kv_state, norm_gain, out_weight):
    n_seq, n_head = lax.axis_size("seq"), lax.axis_size("head")
    inner = n_seq // LINE
    place, h = lax.axis_index("seq"), lax.axis_index("head")
    z, i = place // inner, place % inner
    tok_rows, local_width = queries.shape
    assert tok_rows == BLOCK
    heads = local_width // DH
    total_width = local_width * n_head
    width = out_weight.shape[1]

    def along(value, hops):
        return lax.ppermute(value, "seq", line_pairs(n_seq, hops))

    terms, stepped = state_prefix(key_input, value_input, n_seq, place)
    some = heads // 2
    inners = [
        causal_part(queries, key_input, value_input, 0, some),
        causal_part(queries, key_input, value_input, some, heads - some),
    ]

    own_columns = hold(out_weight, stepped)
    w_halves = along(own_columns, SWAP_HALVES)
    w_next = along(own_columns, SWAP_NEXT)
    w_middle = along(own_columns, SWAP_MIDDLE)

    bits = n_head.bit_length() - 1
    order = [int(format(j, "b").zfill(bits)[::-1], 2) for j in range(n_head)] if bits else [0]
    kept_rows, sent_rows, squares = gated_hidden(
        queries, inners, kv_state, terms, gate_input, norm_gain, h, i, order
    )
    rows_list = [(kept_rows, sent_rows)]
    for turn in range(1, inner):
        pairs = turn_pairs(n_seq, turn)
        rows_list.append((lax.ppermute(kept_rows, "seq", pairs), lax.ppermute(sent_rows, "seq", pairs)))

    out_rows = tok_rows // n_head
    half, bit = n_head // 2, 1
    while bit < n_head:
        squares = squares[:half] + lax.ppermute(squares[half:], "head", flip_pairs(n_head, bit))
        half //= 2
        bit *= 2

    is_end = (z == 0) | (z == LINE - 1)
    flag = scalars(is_end)


    owners = [z ^ block for block in range(LINE)]
    blocks = [(out_weight,), (w_next,), (w_halves,)]

    def summed(parts, pins):
        weights = sorted({block for _, own in parts for block in own})
        jobs = [(p, weights.index(block)) for p, (_, own) in enumerate(parts) for block in own]
        sent, kept = project(
            jobs,
            [rows_list[turn] for turn, _ in parts],
            [blocks[block] for block in weights],
            hold(flag, *pins),
        )
        first_sent, bit = sent, 1
        while bit < n_head:
            got = lax.ppermute(sent, "head", flip_pairs(n_head, bit))
            bit *= 2
            if bit < n_head:
                sent, kept = fold(kept, got)
            else:
                kept = fold(kept, got, [width * len(own) for _, own in parts])
        pieces = []
        for piece, (turn, own) in zip(kept, parts):
            if turn:
                piece = lax.ppermute(piece, "seq", turn_pairs(n_seq, -turn))
            starts = [(owners[block] * inner + (i + turn) % inner) * width for block in own]
            pieces.append((piece, starts))
        return pieces, first_sent, got

    turns = list(range(inner))
    shape = (out_rows, width * n_seq)
    in_kernel = width % DH == 0 and out_rows == DH

    pieces, pins, ends = [], [], []

    def group(members, some):
        more, sent, end = summed([(turn, some) for turn in members], pins)
        pieces.extend(more)
        ends.append(end)
        pins[:] = [sent, squares]
        return [piece for piece, _ in more]

    group(turns[:1], [0])
    returned = group(turns[1:], [0]) if inner > 1 else []
    w_ends = along(hold(w_halves, *ends), TO_ENDS)
    blocks.append((w_middle, w_ends))
    group(turns[:1], [1, 2])
    if inner > 1:
        group(turns[1:], [1, 2])
    filled = placed(None, pieces, squares, width, shape, total_width) if in_kernel else None
    pins += [*ends, *returned]
    last = []
    for members in (turns[1:], turns[:1]):
        if members:
            more, sent, _ = summed([(turn, [3]) for turn in members], pins)
            last += more
            pins = [sent]
    if in_kernel:
        return placed(filled, last, squares, width, shape, total_width)
    scale = lax.rsqrt(squares.reshape(out_rows, 1) / total_width + epsilon)
    output = jnp.zeros(shape, jnp.bfloat16)
    for piece, starts in pieces + last:
        piece = (piece.astype(jnp.float32) * scale).astype(jnp.bfloat16)
        for index, start in enumerate(starts):
            part = piece[:, index * width : (index + 1) * width]
            output = lax.dynamic_update_slice_in_dim(output, part, start, 1)
    return output


def solution(mesh):
    in_specs = (
        P("seq", "head"),
        P("seq", "head"),
        P("seq", "head"),
        P("seq", "head"),
        P("head", None, None),
        P(),
        P("head", "seq"),
    )
    out_specs = P(("seq", "head"), None)
    return jax.shard_map(shards, mesh=mesh, in_specs=in_specs, out_specs=out_specs, check_vma=False)
```

```python
import functools

import jax
import jax.numpy as jnp
from jax import lax
from jax.experimental import pallas as pl
from jax.experimental.pallas import tpu as pltpu
from jax.sharding import PartitionSpec as P

DH = 128
BLOCK = 512
LINE = 4
VMEM_BYTES = 16 * 1024 * 1024


epsilon = 1e-05


def line_pairs(n_seq, hops):
    inner = n_seq // LINE
    return [(a * inner + i, b * inner + i) for a, b in hops for i in range(inner)]


def turn_pairs(n_seq, turn):
    inner = n_seq // LINE
    return [(a * inner + i, a * inner + (i + turn) % inner) for a in range(LINE) for i in range(inner)]


def flip_pairs(n_head, bit):
    return [(h, h ^ bit) for h in range(n_head)]


SWAP_NEXT = [(z, z ^ 1) for z in range(LINE)]
SWAP_HALVES = [(z, z ^ 2) for z in range(LINE)]
SWAP_MIDDLE = [(1, 2), (2, 1)]
TO_ENDS = [(1, 0), (2, 3)]


def hold(value, *others):
    return lax.optimization_barrier((value, *others))[0]


def scalars(*values):
    return jnp.stack([jnp.asarray(value, jnp.int32) for value in values])


def local_call(kernel, places, operands, out_shapes, flops=0):
    held = sum(value.size * value.dtype.itemsize for value in [*operands, *out_shapes])
    return pl.pallas_call(
        kernel,
        in_specs=[pl.BlockSpec(memory_space=pltpu.SMEM)]
        + [pl.BlockSpec(memory_space=pltpu.VMEM)] * len(operands),
        out_specs=[pl.BlockSpec(memory_space=pltpu.VMEM)] * len(out_shapes),
        out_shape=out_shapes,
        compiler_params=pltpu.CompilerParams(vmem_limit_bytes=max(VMEM_BYTES, held + held // 2)),
        cost_estimate=pl.CostEstimate(flops=flops, bytes_accessed=held, transcendentals=0),
    )(places, *operands)


def combine_kernel(count, always, masks_ref, *refs):
    values, outs = refs[:count], refs[count:]
    for index in range(values[0].shape[0]):
        total = values[0][index].astype(jnp.float32)
        for value in values[1:always]:
            total = total + value[index].astype(jnp.float32)
        for position, out in enumerate(outs):
            own = total
            for k in range(always, count):
                mask = masks_ref[position * (count - always) + k - always]
                own = own + jnp.where(mask != 0, values[k][index].astype(jnp.float32), 0.0)
            out[index] = own.astype(out.dtype)


def combine(values, dtypes, sometimes=(), masks=None):
    operands = list(values) + list(sometimes)
    masks = scalars(0) if masks is None else scalars(*masks)
    return local_call(
        functools.partial(combine_kernel, len(operands), len(values)),
        masks,
        operands,
        [jax.ShapeDtypeStruct(values[0].shape, dtype) for dtype in dtypes],
    )


def states_kernel(part_ref, k_ref, v_ref, out_ref):
    heads = out_ref.shape[0]
    for index in range(heads):
        columns = pl.ds(pl.multiple_of((part_ref[0] * heads + index) * DH, DH), DH)
        out_ref[index] = lax.dot_general(
            k_ref[:, columns],
            v_ref[:, columns],
            (((0,), (0,)), ((), ())),
            preferred_element_type=jnp.float32,
        ).astype(out_ref.dtype)


def block_states(key_input, value_input, part, heads, dtype):
    return local_call(
        states_kernel,
        scalars(part),
        [key_input, value_input],
        [jax.ShapeDtypeStruct((heads, DH, DH), dtype)],
        2 * key_input.shape[0] * heads * DH * DH,
    )[0]


def state_prefix(key_input, value_input, n_seq, place):
    inner = n_seq // LINE
    i = place % inner
    heads = key_input.shape[1] // DH
    split = heads % inner == 0
    share = heads // inner if split else heads
    if split:
        sends = [
            block_states(key_input, value_input, (i + turn) % inner, share, jnp.bfloat16)
            for turn in range(1, inner)
        ]
        own = block_states(key_input, value_input, i, share, jnp.float32)
    else:
        own = block_states(key_input, value_input, 0, share, jnp.float32)
        sends = [own.astype(jnp.bfloat16)] * (inner - 1)
    values, members = [own], [i]
    for turn in range(1, inner):
        values.append(lax.ppermute(sends[turn - 1], "seq", turn_pairs(n_seq, turn)))
        members.append((i - turn) % inner)
    (first,) = combine(values, [jnp.bfloat16])
    from_pair = lax.ppermute(first, "seq", line_pairs(n_seq, SWAP_NEXT))
    (second,) = combine(values + [from_pair], [jnp.bfloat16])
    from_half = lax.ppermute(second, "seq", line_pairs(n_seq, [(0, 2), (1, 3)]))
    targets = [i] + [(i + turn) % inner for turn in range(1, inner)] if split else [i]
    later = (place // inner) % 2 == 1
    masks = [mask for target in targets for mask in [later] + [owner < target for owner in members]]
    dtypes = [jnp.float32] + [jnp.bfloat16] * (len(targets) - 1)
    befores = combine([from_half], dtypes, [from_pair] + values, masks)
    terms = [befores[0]]
    for turn in range(1, len(targets)):
        terms.append(lax.ppermute(befores[turn], "seq", turn_pairs(n_seq, turn)))
    return terms, from_half


def causal_kernel(first_head, place_ref, q_ref, k_ref, v_ref, out_ref):
    rows = q_ref.shape[0]
    half = rows // 2
    top, bottom = pl.ds(0, half), pl.ds(half, half)
    keep = lax.broadcasted_iota(jnp.int32, (half, half), 0) >= lax.broadcasted_iota(
        jnp.int32, (half, half), 1
    )

    def scores(q_rows, k_rows, columns):
        return lax.dot_general(
            q_ref[q_rows, columns],
            k_ref[k_rows, columns],
            (((1,), (1,)), ((), ())),
            preferred_element_type=jnp.float32,
        )

    for index in range(out_ref.shape[1] // DH):
        columns = pl.ds((first_head + index) * DH, DH)
        placed = pl.ds(index * DH, DH)
        first = jnp.where(keep, scores(top, top, columns), 0.0).astype(jnp.bfloat16)
        below = scores(bottom, top, columns).astype(jnp.bfloat16)
        last = jnp.where(keep, scores(bottom, bottom, columns), 0.0).astype(jnp.bfloat16)
        out_ref[top, placed] = jnp.dot(first, v_ref[top, columns], preferred_element_type=jnp.float32)
        out_ref[bottom, placed] = jnp.dot(
            jnp.concatenate([below, last], axis=1),
            v_ref[:, columns],
            preferred_element_type=jnp.float32,
        )


def causal_part(queries, key_input, value_input, first_head, heads):
    return local_call(
        functools.partial(causal_kernel, first_head),
        scalars(0),
        [queries, key_input, value_input],
        [jax.ShapeDtypeStruct((queries.shape[0], heads * DH), jnp.float32)],
        3 * queries.shape[0] ** 2 * heads * DH,
    )[0]


def hidden_kernel(order, group, calls, place_ref, q_ref, gate_ref, gain_ref, kv_ref, *refs):
    terms, inners = refs[:group], refs[group : group + calls]
    kept_ref, sent_ref, squares_ref = refs[group + calls :]
    half = kept_ref.shape[0]
    heads = kv_ref.shape[0]
    share = heads // group
    size = q_ref.shape[0] // len(order)
    states = []
    for head in range(heads):
        state = kv_ref[head]
        for turn, term in enumerate(terms):
            value = term[head % share].astype(jnp.float32)
            if group > 1:
                covers = lax.rem(place_ref[1] - turn + group, group)
                value = jnp.where(covers == head // share, value, 0.0)
            state = state + value
        high = state.astype(jnp.bfloat16)
        low = (state - high.astype(jnp.float32)).astype(jnp.bfloat16)
        states.append(jnp.concatenate([high, low], axis=0))
    for position, block in enumerate(order):
        start = pl.multiple_of((place_ref[0] ^ block) * size, size)
        rows = pl.ds(start, size)
        hidden_ref = kept_ref if position * size < half else sent_ref
        placed = pl.ds(position * size % half, size)
        squares = jnp.zeros((size, DH), jnp.float32)
        for head in range(heads):
            columns = pl.ds(head * DH, DH)
            q_rows = q_ref[rows, columns]
            carried = jnp.dot(
                jnp.concatenate([q_rows, q_rows], axis=1),
                states[head],
                preferred_element_type=jnp.float32,
            )
            per_call = inners[0].shape[1] // DH
            inner = inners[head // per_call][rows, pl.ds(head % per_call * DH, DH)]
            attn = (carried + inner).astype(jnp.bfloat16).astype(jnp.float32)
            gate = 1.0 + jnp.tanh(gate_ref[rows, columns].astype(jnp.float32) * 0.5)
            gain = gain_ref[place_ref[0] * heads + head] * 0.5
            hidden_ref[placed, columns] = (attn * (gain * gate)).astype(jnp.bfloat16)
            squares = squares + attn * attn
        squares_ref[pl.ds(position, 1), :] = jnp.sum(jnp.transpose(squares), axis=0, keepdims=True)


def gated_hidden(queries, inners, kv_state, terms, gate_input, norm_gain, h, i, order):
    rows, width = queries.shape
    half = jax.ShapeDtypeStruct((rows // 2, width), jnp.bfloat16)
    return local_call(
        functools.partial(hidden_kernel, order, len(terms), len(inners)),
        scalars(h, i),
        [queries, gate_input, norm_gain.reshape(-1, 1, DH), kv_state, *terms, *inners],
        [
            half,
            half,
            jax.ShapeDtypeStruct((len(order), rows // len(order)), jnp.float32),
        ],
        4 * rows * width * DH,
    )


def project_kernel(jobs, n_rows, choices, flag_ref, *refs):
    rows_refs = refs[: 2 * n_rows]
    weight_refs = refs[2 * n_rows : -2]
    sent_ref, kept_ref = refs[-2:]

    def products(index, weight_ref):
        for rows, weight, first in jobs:
            if weight == index:
                columns = pl.ds(first, weight_ref.shape[1])
                kept_rows, sent_rows = rows_refs[2 * rows : 2 * rows + 2]
                sent_ref[:, columns] = jnp.dot(
                    sent_rows[...], weight_ref[...], preferred_element_type=jnp.float32
                ).astype(jnp.bfloat16)
                kept_ref[:, columns] = jnp.dot(
                    kept_rows[...], weight_ref[...], preferred_element_type=jnp.float32
                )

    first = 0
    for index, number in enumerate(choices):
        for k in range(number):
            one = functools.partial(products, index, weight_refs[first + k])
            if number == 1:
                one()
            else:
                pl.when(flag_ref[0] == k)(one)
        first += number


def project(jobs, rows_list, weights, flag):
    flat = [choice for weight in weights for choice in weight]
    choices = tuple(len(weight) for weight in weights)
    placed_jobs, total = [], 0
    for rows, weight in jobs:
        placed_jobs.append((rows, weight, total))
        total += weights[weight][0].shape[1]
    height, depth = rows_list[0][0].shape
    shape = (height, total)
    return local_call(
        functools.partial(project_kernel, tuple(placed_jobs), len(rows_list), choices),
        flag,
        [*[half for pair in rows_list for half in pair], *flat],
        [jax.ShapeDtypeStruct(shape, jnp.bfloat16), jax.ShapeDtypeStruct(shape, jnp.float32)],
        4 * height * depth * total,
    )


def fold_kernel(more, flag_ref, kept_ref, got_ref, *outs):
    if more:
        sent_ref, left_ref = outs
        half = left_ref.shape[0]
        left_ref[...] = kept_ref[:half] + got_ref[:half].astype(jnp.float32)
        sent_ref[...] = (kept_ref[half:] + got_ref[half:].astype(jnp.float32)).astype(jnp.bfloat16)
        return
    first = 0
    for out in outs:
        columns = pl.ds(first, out.shape[1])
        out[...] = (kept_ref[:, columns] + got_ref[:, columns].astype(jnp.float32)).astype(out.dtype)
        first += out.shape[1]


def fold(kept, got, widths=None):
    rows, width = kept.shape
    if widths is None:
        shape = (rows // 2, width)
        outs = [jax.ShapeDtypeStruct(shape, jnp.bfloat16), jax.ShapeDtypeStruct(shape, jnp.float32)]
    else:
        outs = [jax.ShapeDtypeStruct((rows, some), jnp.bfloat16) for some in widths]
    return local_call(functools.partial(fold_kernel, widths is None), scalars(0), [kept, got], outs)


def column(row):
    return jnp.transpose(jnp.broadcast_to(row, (row.shape[1], row.shape[1])))


def scaled_parts(counts, width, starts_ref, squares_ref, pieces, total_width):
    scale = lax.rsqrt(column(squares_ref[...]) / total_width + epsilon)
    where = 0
    for piece, count in zip(pieces, counts):
        for index in range(count):
            for at in range(0, width, DH):
                part = piece[:, pl.ds(index * width + at, DH)].astype(jnp.float32) * scale
                yield part, pl.multiple_of(starts_ref[where] + at, DH)
            where += 1


def placed_kernel(counts, width, total_width, starts_ref, squares_ref, *refs):
    out_ref = refs[-1]
    for part, start in scaled_parts(counts, width, starts_ref, squares_ref, refs[:-1], total_width):
        out_ref[:, pl.ds(start, DH)] = part.astype(out_ref.dtype)


def added_kernel(counts, width, total_width, starts_ref, squares_ref, *refs):
    out_ref, buf, sem = refs[-3:]
    copies = []
    parts = scaled_parts(counts, width, starts_ref, squares_ref, refs[: len(counts)], total_width)
    steps = width // DH
    for at, (part, _) in enumerate(parts):
        where = at // steps
        buf[where, :, pl.ds(at % steps * DH, DH)] = part.astype(out_ref.dtype)
        if at % steps == steps - 1:
            start = pl.multiple_of(starts_ref[where], DH)
            target = out_ref.at[:, pl.ds(start, width)]
            copies.append(pltpu.make_async_copy(buf.at[where], target, sem.at[where]))
            copies[-1].start()
    for copy in copies:
        copy.wait()


def placed(filled, pieces, squares, width, shape, total_width):
    counts = tuple(len(starts) for _, starts in pieces)
    starts = scalars(*[start for _, own in pieces for start in own])
    operands = [squares] + [piece for piece, _ in pieces]
    out_shape = jax.ShapeDtypeStruct(shape, jnp.bfloat16)
    columns = width * sum(counts)
    if filled is None:
        kernel = functools.partial(placed_kernel, counts, width, total_width)
        return local_call(kernel, starts, operands, [out_shape])[0]
    return pl.pallas_call(
        functools.partial(added_kernel, counts, width, total_width),
        in_specs=[pl.BlockSpec(memory_space=pltpu.SMEM)]
        + [pl.BlockSpec(memory_space=pltpu.VMEM)] * len(operands)
        + [pl.BlockSpec(memory_space=pl.ANY)],
        out_specs=pl.BlockSpec(memory_space=pl.ANY),
        out_shape=out_shape,
        scratch_shapes=[
            pltpu.VMEM((columns // width, shape[0], width), jnp.bfloat16),
            pltpu.SemaphoreType.DMA((columns // width,)),
        ],
        input_output_aliases={len(operands) + 1: 0},
        compiler_params=pltpu.CompilerParams(vmem_limit_bytes=VMEM_BYTES),
        cost_estimate=pl.CostEstimate(
            flops=0, bytes_accessed=4 * shape[0] * columns, transcendentals=0
        ),
    )(starts, *operands, filled)


def shards(queries, key_input, value_input, gate_input, kv_state, norm_gain, out_weight):
    n_seq, n_head = lax.axis_size("seq"), lax.axis_size("head")
    inner = n_seq // LINE
    place, h = lax.axis_index("seq"), lax.axis_index("head")
    z, i = place // inner, place % inner
    tok_rows, local_width = queries.shape
    assert tok_rows == BLOCK
    heads = local_width // DH
    total_width = local_width * n_head
    width = out_weight.shape[1]

    def along(value, hops):
        return lax.ppermute(value, "seq", line_pairs(n_seq, hops))

    terms, stepped = state_prefix(key_input, value_input, n_seq, place)
    some = heads // 2
    inners = [
        causal_part(queries, key_input, value_input, 0, some),
        causal_part(queries, key_input, value_input, some, heads - some),
    ]

    own_columns = hold(out_weight, stepped)
    w_halves = along(own_columns, SWAP_HALVES)
    w_next = along(own_columns, SWAP_NEXT)
    w_middle = along(own_columns, SWAP_MIDDLE)

    bits = n_head.bit_length() - 1
    order = [int(format(j, "b").zfill(bits)[::-1], 2) for j in range(n_head)] if bits else [0]
    kept_rows, sent_rows, squares = gated_hidden(
        queries, inners, kv_state, terms, gate_input, norm_gain, h, i, order
    )
    rows_list = [(kept_rows, sent_rows)]
    for turn in range(1, inner):
        pairs = turn_pairs(n_seq, turn)
        rows_list.append((lax.ppermute(kept_rows, "seq", pairs), lax.ppermute(sent_rows, "seq", pairs)))

    out_rows = tok_rows // n_head
    half, bit = n_head // 2, 1
    while bit < n_head:
        squares = squares[:half] + lax.ppermute(squares[half:], "head", flip_pairs(n_head, bit))
        half //= 2
        bit *= 2

    is_end = (z == 0) | (z == LINE - 1)
    flag = scalars(is_end)


    owners = [z ^ block for block in range(LINE)]
    blocks = [(out_weight,), (w_next,), (w_halves,)]

    def summed(parts, pins):
        weights = sorted({block for _, own in parts for block in own})
        jobs = [(p, weights.index(block)) for p, (_, own) in enumerate(parts) for block in own]
        sent, kept = project(
            jobs,
            [rows_list[turn] for turn, _ in parts],
            [blocks[block] for block in weights],
            hold(flag, *pins),
        )
        first_sent, bit = sent, 1
        while bit < n_head:
            got = lax.ppermute(sent, "head", flip_pairs(n_head, bit))
            bit *= 2
            if bit < n_head:
                sent, kept = fold(kept, got)
            else:
                kept = fold(kept, got, [width * len(own) for _, own in parts])
        pieces = []
        for piece, (turn, own) in zip(kept, parts):
            if turn:
                piece = lax.ppermute(piece, "seq", turn_pairs(n_seq, -turn))
            starts = [(owners[block] * inner + (i + turn) % inner) * width for block in own]
            pieces.append((piece, starts))
        return pieces, first_sent, got

    turns = list(range(inner))
    shape = (out_rows, width * n_seq)
    in_kernel = width % DH == 0 and out_rows == DH

    pieces, pins, ends = [], [], []

    def group(members, some):
        more, sent, end = summed([(turn, some) for turn in members], pins)
        pieces.extend(more)
        ends.append(end)
        pins[:] = [sent, squares]
        return [piece for piece, _ in more]

    group(turns[:1], [0])
    returned = group(turns[1:], [0]) if inner > 1 else []
    w_ends = along(hold(w_halves, *ends), TO_ENDS)
    blocks.append((w_middle, w_ends))
    late = group(turns[1:], [1, 2]) if inner > 1 else []
    group(turns[:1], [1, 2])
    filled = placed(None, pieces, squares, width, shape, total_width) if in_kernel else None
    pins += [*ends, *returned]
    last = []
    for members in (turns[1:], turns[:1]):
        if members:
            more, sent, _ = summed([(turn, [3]) for turn in members], pins)
            last += more
            pins = [sent, *late]
    if in_kernel:
        return placed(filled, last, squares, width, shape, total_width)
    scale = lax.rsqrt(squares.reshape(out_rows, 1) / total_width + epsilon)
    output = jnp.zeros(shape, jnp.bfloat16)
    for piece, starts in pieces + last:
        piece = (piece.astype(jnp.float32) * scale).astype(jnp.bfloat16)
        for index, start in enumerate(starts):
            part = piece[:, index * width : (index + 1) * width]
            output = lax.dynamic_update_slice_in_dim(output, part, start, 1)
    return output


def solution(mesh):
    in_specs = (
        P("seq", "head"),
        P("seq", "head"),
        P("seq", "head"),
        P("seq", "head"),
        P("head", None, None),
        P(),
        P("head", "seq"),
    )
    out_specs = P(("seq", "head"), None)
    return jax.shard_map(shards, mesh=mesh, in_specs=in_specs, out_specs=out_specs, check_vma=False)
```
